128 devices in a mesh: row: 16 (over x_lo, z, core), col: 8 (over y, x_hi).
Axes of the slice: x: 4 (x_hi: 2, x_lo: 2; x = x_hi * 2 + x_lo), y: 4, z: 4, core: 2. Of those that a mesh axis runs over, the one named last changes fastest.
Arguments:
- tokens: bfloat16 [256, 8192], P('col', 'row'), may hold values from -6 to 6
- out_grad: bfloat16 [256, 8192], P('col', 'row'), may hold values from -0.75 to 0.75
- token_weight: float32 [256], replicated, may hold values from -0.4375 to 0.4375
- gate_weight: bfloat16 [8192, 29568], P('row', 'col'), may hold values from -0.0625 to 0.0625
- up_weight: bfloat16 [8192, 29568], P('row', 'col'), may hold values from -0.0625 to 0.0625
- down_weight: bfloat16 [29568, 8192], P('col', 'row'), may hold values from -0.03125 to 0.03125
Outputs:
- input_grad: float32 [256, 8192], P('col', 'row')
- gate_grad: bfloat16 [8192, 29568], P('row', 'col')
- up_grad: bfloat16 [8192, 29568], P('row', 'col')
- down_grad: bfloat16 [29568, 8192], P('col', 'row')
The draws below stay inside these ranges and needn't reach their ends.
All inputs are finite; a program needn't handle non-finite values.
Results may differ from the reference program's by a relative error of at most 0.0049.
Values may be sent and summed in bfloat16 or wider, within the bound.
A program may use at most 128 MiB of HBM per device.

```python
import jax
import jax.numpy as jnp
from jax import lax

D = 8192
FF = 29568
TOKENS = 256


def level_of(key, shape, cuts, smallest, high):
    level, own = 1.0, jax.random.fold_in(key, 6)
    for dim, blocks in cuts:
        draws = jnp.exp(jax.random.uniform(jax.random.fold_in(own, dim), (blocks,), jnp.float32, smallest / len(cuts), high / len(cuts)))
        level = level * jnp.repeat(draws, shape[dim] // blocks).reshape([-1 if axis == dim else 1 for axis in range(len(shape))])
    return level


def bell_draw(rng, dims, spread, limit, shards=(), held_as=jnp.bfloat16):
    factor_of = level_of(rng, dims, shards, -0.22, 0.18) if shards else 1.0
    values = jax.random.normal(rng, dims, jnp.float32) * spread * factor_of
    return jnp.minimum(jnp.maximum(values, -limit), limit).astype(held_as)


def setup_inputs(seed: int = 0) -> dict:
    arg_keys = jax.random.split(jax.random.key(seed), 7)
    return {
        "tokens": bell_draw(arg_keys[0], (TOKENS, D), 1.0, 6.0, ((0, 8), (1, 16))),
        "out_grad": bell_draw(arg_keys[1], (TOKENS, D), 0.25, 0.75, ((0, 8), (1, 16))),
        "token_weight": bell_draw(arg_keys[2], (TOKENS,), 0.07, 0.4375, (), jnp.float32),
        "gate_weight": bell_draw(arg_keys[3], (D, FF), D ** -0.5, 0.0625, ((0, 16), (1, 8))),
        "up_weight": bell_draw(arg_keys[4], (D, FF), D ** -0.5, 0.0625, ((0, 16), (1, 8))),
        "down_weight": bell_draw(arg_keys[5], (FF, D), FF ** -0.5, 0.03125, ((0, 8), (1, 16))),
    }


def reference(tokens, out_grad, token_weight, gate_weight, up_weight, down_weight):
    over_hidden = (((1,), (1,)), ((), ()))
    gate = jnp.dot(tokens, gate_weight, preferred_element_type=jnp.float32)
    up = jnp.dot(tokens, up_weight, preferred_element_type=jnp.float32)
    back = lax.dot_general(out_grad, down_weight, over_hidden, preferred_element_type=jnp.float32)
    weights = token_weight[:, None]
    sig = jax.nn.sigmoid(gate)
    silu = gate * sig
    weighted_hidden = (weights * (silu * up)).astype(jnp.bfloat16)
    scaled = weights * back
    gate_back = (scaled * up * sig * (1.0 + gate * (1.0 - sig))).astype(jnp.bfloat16)
    up_back = (scaled * silu).astype(jnp.bfloat16)
    over_tokens = (((0,), (0,)), ((), ()))
    gate_grad = lax.dot_general(tokens, gate_back, over_tokens, preferred_element_type=jnp.float32).astype(jnp.bfloat16)
    up_grad = lax.dot_general(tokens, up_back, over_tokens, preferred_element_type=jnp.float32).astype(jnp.bfloat16)
    down_grad = lax.dot_general(weighted_hidden, out_grad, over_tokens, preferred_element_type=jnp.float32).astype(jnp.bfloat16)
    input_grad = lax.dot_general(gate_back, gate_weight, over_hidden, preferred_element_type=jnp.float32)
    input_grad = input_grad + lax.dot_general(up_back, up_weight, over_hidden, preferred_element_type=jnp.float32)
    return input_grad, gate_grad, up_grad, down_grad
```

```python
import functools

import jax
import jax.numpy as jnp
from jax import lax
from jax.experimental import pallas as pl
from jax.experimental.pallas import tpu as pltpu
from jax.sharding import PartitionSpec as P

BF16, F32 = jnp.bfloat16, jnp.float32
MESH = pl.DeviceIdType.MESH
LANE = 128
TILES = (2, 4, 4, 4, 4, 4, 4, 3)
GATHER = ("zx",) * len(TILES)
LAST = 8
ORDER = sorted(
    ((s, j) for j in range(len(TILES)) for s in range(LAST + 1)),
    key=lambda e: (e[1] * 4.4 + e[0] * 2.0, -e[0]),
)
NT = (((1,), (1,)), ((), ()))


def chunks_of(width):
    assert sum(TILES) == pl.cdiv(width, LANE)
    out, at = [], 0
    for t in TILES:
        out.append((at * LANE, t * LANE, min(t * LANE, width - at * LANE)))
        at += t
    return out


(PAIR, ZA, ZB, ZUP, ZDOWN, X1, GUP, GDOWN, FUP, FDOWN, XA, XB, XC, XD, CA, CB) = range(16)
PER_CHUNK = 16
COLS = 9 + 8


def exchange_kernel(
    width,
    tok, og, tw, wg_h, wu_h, wd_h,
    r_out, ab_out, ig_out,
    wg, wu, wd, ab, pf, pr, zs1, zr1, zs2, zr2, own, xs, xr, res, rt, ig, igs, igr,
    ssem, rsem, lsem, osem,
):
    chunks = chunks_of(width)
    n = len(chunks)
    row, k = lax.axis_index("row"), lax.axis_index("col")
    x, z, c = row // 8, (row // 2) % 4, row % 2
    y, h = k // 2, k % 2
    zp, zm, zo = (z + 1) % 4, (z + 3) % 4, (z + 2) % 4
    yp, ym, yo = (y + 1) % 4, (y + 3) % 4, (y + 2) % 4

    def rdev(xx, zz, cc):
        return (xx * 8 + zz * 2 + cc, k)

    def cdev(yy, hh):
        return (row, yy * 2 + hh)

    sib, xn = rdev(x, z, 1 - c), rdev(1 - x, z, c)
    up, down = rdev(x, zp, c), rdev(x, zm, c)

    sent = []

    def send(src, dst, idx, dev):
        copy = pltpu.make_async_remote_copy(
            src_ref=src, dst_ref=dst, send_sem=ssem.at[idx], recv_sem=rsem.at[idx],
            device_id=dev, device_id_type=MESH,
        )
        copy.start()
        sent.append(copy)

    def landed(ref, idx):
        pltpu.make_async_remote_copy(
            src_ref=ref, dst_ref=ref, send_sem=ssem.at[idx], recv_sem=rsem.at[idx],
            device_id=sib, device_id_type=MESH,
        ).wait_recv()

    mine = pl.ds(pl.multiple_of(k * 32, 32), 32)
    first = [
        pltpu.make_async_copy(tok, ab.at[0, mine], lsem.at[0]),
        pltpu.make_async_copy(og, ab.at[1, mine], lsem.at[1]),
    ]
    weights = [
        pltpu.make_async_copy(wg_h, wg, lsem.at[2]),
        pltpu.make_async_copy(wu_h, wu, lsem.at[3]),
        pltpu.make_async_copy(wd_h, wd, lsem.at[4]),
    ]
    for copy in first + weights:
        copy.start()

    barrier = pltpu.get_barrier_semaphore()
    greeted = [sib, xn, up, down]
    for step in range(1, 8):
        greeted.append((row, (k + step) % 8))
    for dev in greeted:
        pl.semaphore_signal(barrier, inc=1, device_id=dev, device_id_type=MESH)
    for copy in first:
        copy.wait()
    pl.semaphore_wait(barrier, len(greeted))

    base = n * PER_CHUNK

    def block(yy, hh):
        return pl.ds(pl.multiple_of((yy * 2 + hh) * 32, 32), 32)

    def both(yy, hh):
        return ab.at[:, block(yy, hh)]

    def one(part, yy, hh):
        return ab.at[part, block(yy, hh)]

    me = both(y, h)
    send(me, me, base + 2, cdev(y, 1 - h))
    send(me, me, base + 0, cdev(yp, h))
    send(me, me, base + 1, cdev(ym, h))
    landed(both(ym, h), base + 0)
    send(one(0, ym, h), one(0, ym, h), base + 5, cdev(yp, h))
    landed(both(yp, h), base + 1)
    send(one(1, yp, h), one(1, yp, h), base + 6, cdev(ym, h))
    landed(both(y, 1 - h), base + 2)
    send(both(y, 1 - h), both(y, 1 - h), base + 3, cdev(yp, h))
    send(both(y, 1 - h), both(y, 1 - h), base + 4, cdev(ym, h))
    landed(both(ym, 1 - h), base + 3)
    send(one(0, ym, 1 - h), one(0, ym, 1 - h), base + 7, cdev(yp, h))
    landed(both(yp, 1 - h), base + 4)
    send(one(1, yp, 1 - h), one(1, yp, 1 - h), base + 8, cdev(ym, h))
    landed(one(0, yo, h), base + 5)
    landed(one(1, yo, h), base + 6)
    landed(one(0, yo, 1 - h), base + 7)
    landed(one(1, yo, 1 - h), base + 8)
    outs = [pltpu.make_async_copy(ab, ab_out, osem.at[0])]
    outs[0].start()
    for copy in weights:
        copy.wait()

    first_token = c * 128 + x * 64 + z * 16
    lanes = lax.broadcasted_iota(jnp.int32, (16, 256), 1)
    rows = lax.broadcasted_iota(jnp.int32, (16, 256), 0)
    column = jnp.sum(
        jnp.where(lanes == rows + first_token, jnp.broadcast_to(tw[...], (16, 256)), 0.0),
        axis=1, keepdims=True,
    )

    def span(j):
        o, w, _ = chunks[j]
        return slice(3 * o, 3 * o + 3 * w)

    def halves(j):
        o, w, _ = chunks[j]
        cut = 3 * o + (3 * w // LANE // 2) * LANE
        return slice(3 * o, cut), slice(cut, 3 * o + 3 * w)

    def products(j):
        o, w, valid = chunks[j]
        for part in range(3):
            for at in range(0, valid, 256):
                size = min(256, valid - at)
                lo = o + at
                value = lax.dot_general(
                    ab[part // 2], (wg, wu, wd)[part][lo : lo + size, :], NT,
                    preferred_element_type=F32,
                )
                to = 3 * o + part * w + at
                pf[:, :, :, :, to : to + size] = value.reshape(2, 2, 4, 16, size)
            if valid < w:
                pad = slice(3 * o + part * w + valid, 3 * o + part * w + w)
                pf[:, :, :, :, pad] = jnp.zeros((2, 2, 4, 16, w - valid), F32)
        cols = span(j)
        send(
            pf.at[1 - c, :, :, :, cols], pr.at[:, :, :, cols], j * PER_CHUNK + PAIR, sib
        )

    def chip(xx, zz, cols):
        return pf[c, xx, zz, :, cols] + pr[xx, zz, :, cols]

    def reduce_far(j):
        m, cols = j * PER_CHUNK, span(j)
        landed(pr.at[:, :, :, cols], m + PAIR)
        zs1[0, :, cols] = chip(0, zo, cols).astype(BF16)
        send(zs1.at[0, :, cols], zr1.at[0, :, cols], m + ZA, up)
        zs1[1, :, cols] = chip(1, zo, cols).astype(BF16)
        send(zs1.at[1, :, cols], zr1.at[1, :, cols], m + ZB, down)

    def reduce_near(j):
        m, cols = j * PER_CHUNK, span(j)
        landed(zr1.at[0, :, cols], m + ZA)
        zs2[0, 0, :, cols] = (chip(0, zp, cols) + zr1[0, :, cols].astype(F32)).astype(BF16)
        zs2[0, 1, :, cols] = chip(1, zp, cols).astype(BF16)
        send(zs2.at[0, :, :, cols], zr2.at[0, :, :, cols], m + ZUP, up)
        landed(zr1.at[1, :, cols], m + ZB)
        zs2[1, 0, :, cols] = chip(0, zm, cols).astype(BF16)
        zs2[1, 1, :, cols] = (chip(1, zm, cols) + zr1[1, :, cols].astype(F32)).astype(BF16)
        send(zs2.at[1, :, :, cols], zr2.at[1, :, :, cols], m + ZDOWN, down)

    def reduce_x(j):
        m, cols = j * PER_CHUNK, span(j)
        landed(zr2.at[0, :, :, cols], m + ZUP)
        landed(zr2.at[1, :, :, cols], m + ZDOWN)

        def ring(xx):
            return chip(xx, z, cols) + zr2[0, xx, :, cols].astype(F32) + zr2[1, xx, :, cols].astype(F32)

        xs[:, cols] = ring(1 - x).astype(BF16)
        send(xs.at[:, cols], xr.at[:, cols], m + X1, xn)
        own[:, cols] = ring(x)

    def here(xx, zz, cols):
        return res.at[c, xx, zz, :, cols]

    def push(xx, zz, cols, idx, dev):
        send(here(xx, zz, cols), here(xx, zz, cols), idx, dev)

    def activate(j):
        o, w, _ = chunks[j]
        m, cols = j * PER_CHUNK, span(j)
        landed(xr.at[:, cols], m + X1)

        def total(part):
            at = slice(3 * o + part * w, 3 * o + part * w + w)
            return own[:, at] + xr[:, at].astype(F32)

        gate, linear, back = total(0), total(1), total(2)
        sig = jax.nn.sigmoid(gate)
        silu = gate * sig
        scaled = column * back
        for part, value in enumerate((
            column * (silu * linear),
            scaled * linear * sig * (1.0 + gate * (1.0 - sig)),
            scaled * silu,
        )):
            at = slice(3 * o + part * w, 3 * o + part * w + w)
            res[c, x, z, :, at] = value.astype(BF16)
        push(x, z, cols, m + GUP, up)
        push(x, z, cols, m + GDOWN, down)
        push(x, z, cols, m + XA, xn)

    def gather_near(j):
        m, cols = j * PER_CHUNK, span(j)
        lo, hi = halves(j)
        landed(here(x, zm, cols), m + GUP)
        push(x, zm, lo, m + FUP, up)
        push(x, zm, cols, m + XB, xn)
        landed(here(x, zp, cols), m + GDOWN)
        push(x, zp, hi, m + FDOWN, down)
        push(x, zp, cols, m + XC, xn)

    def gather_far(j):
        m, cols = j * PER_CHUNK, span(j)
        lo, hi = halves(j)
        landed(here(x, zo, lo), m + FUP)
        landed(here(x, zo, hi), m + FDOWN)
        push(x, zo, cols, m + XD, xn)
        part = res.at[c, x, :, :, cols]
        send(part, part, m + CA, sib)

    def gather_x(j):
        m, cols = j * PER_CHUNK, span(j)
        landed(here(1 - x, z, cols), m + XA)
        landed(here(1 - x, zm, cols), m + XB)
        landed(here(1 - x, zp, cols), m + XC)
        landed(here(1 - x, zo, cols), m + XD)
        part = res.at[c, 1 - x, :, :, cols]
        send(part, part, m + CB, sib)

    def finish(j):
        o, w, valid = chunks[j]
        m, cols = j * PER_CHUNK, span(j)
        landed(res.at[1 - c, x, :, :, cols], m + CA)
        landed(res.at[1 - c, 1 - x, :, :, cols], m + CB)
        for part, wide in ((1, wg), (2, wu)):
            at = 3 * o + part * w
            piece = res[:, :, :, :, at : at + valid].reshape(256, valid)
            value = jnp.dot(piece, wide[o : o + valid, :], preferred_element_type=F32)
            if j == 0 and part == 1:
                ig[...] = value
            else:
                ig[...] += value
        for part in range(3):
            at = 3 * o + part * w
            rt[part, o : o + w, :] = res[:, :, :, :, at : at + w].reshape(256, w).T
        copy = pltpu.make_async_copy(
            rt.at[:, o : o + w], r_out.at[:, o : o + w], osem.at[1 + j]
        )
        copy.start()
        outs.append(copy)

    stages = (
        products, reduce_far, reduce_near, reduce_x, activate,
        gather_near, gather_far, gather_x, finish,
    )
    for stage, j in ORDER:
        stages[stage](j)

    igs[...] = ig[...].astype(BF16)
    for step in range(1, 8):
        other = (k + step) % 8
        send(
            igs.at[pl.ds(pl.multiple_of(other * 32, 32), 32)], igr.at[step], base + 9 + step,
            (row, other),
        )
    total = ig[mine, :]
    for step in range(1, 8):
        landed(igr.at[step], base + 9 + step)
        total = total + igr[step].astype(F32)
    ig_out[...] = total

    for copy in sent:
        copy.wait_send()
    for copy in outs:
        copy.wait()


def exchange(tokens, out_grad, token_weight, gate_weight, up_weight, down_weight):
    width, depth = gate_weight.shape
    wide = pl.cdiv(width, LANE) * LANE
    cols = 3 * wide
    n = len(TILES)
    messages = n * PER_CHUNK + COLS
    hbm = pl.BlockSpec(memory_space=pl.ANY)
    vmem = pl.BlockSpec(memory_space=pltpu.VMEM)
    return pl.pallas_call(
        functools.partial(exchange_kernel, width),
        out_shape=(
            jax.ShapeDtypeStruct((3, wide, 256), BF16),
            jax.ShapeDtypeStruct((2, 256, depth), BF16),
            jax.ShapeDtypeStruct((32, depth), F32),
        ),
        in_specs=[hbm, hbm, vmem, hbm, hbm, hbm],
        out_specs=(hbm, hbm, vmem),
        scratch_shapes=[
            pltpu.VMEM((width, depth), BF16),
            pltpu.VMEM((width, depth), BF16),
            pltpu.VMEM((width, depth), BF16),
            pltpu.VMEM((2, 256, depth), BF16),
            pltpu.VMEM((2, 2, 4, 16, cols), F32),
            pltpu.VMEM((2, 4, 16, cols), F32),
            pltpu.VMEM((2, 16, cols), BF16),
            pltpu.VMEM((2, 16, cols), BF16),
            pltpu.VMEM((2, 2, 16, cols), BF16),
            pltpu.VMEM((2, 2, 16, cols), BF16),
            pltpu.VMEM((16, cols), F32),
            pltpu.VMEM((16, cols), BF16),
            pltpu.VMEM((16, cols), BF16),
            pltpu.VMEM((2, 2, 4, 16, cols), BF16),
            pltpu.VMEM((3, wide, 256), BF16),
            pltpu.VMEM((256, depth), F32),
            pltpu.VMEM((256, depth), BF16),
            pltpu.VMEM((8, 32, depth), BF16),
            pltpu.SemaphoreType.DMA((messages,)),
            pltpu.SemaphoreType.DMA((messages,)),
            pltpu.SemaphoreType.DMA((5,)),
            pltpu.SemaphoreType.DMA((1 + n,)),
        ],
        compiler_params=pltpu.CompilerParams(
            collective_id=0, has_side_effects=True, vmem_limit_bytes=56 * 1024 * 1024
        ),
        cost_estimate=pl.CostEstimate(
            flops=10 * 256 * depth * width, bytes_accessed=6 * depth * width + 6 * 256 * width,
            transcendentals=0,
        ),
        name="exchange",
    )(tokens, out_grad, token_weight.reshape(1, 256), gate_weight, up_weight, down_weight)


def grads_kernel(r, ab, gate_grad, up_grad, down_grad):
    for part, out in ((1, gate_grad), (2, up_grad), (0, down_grad)):
        out[...] = jnp.dot(
            r[part], ab[0 if part else 1], preferred_element_type=F32
        ).astype(BF16)


def grads(r, ab, width):
    depth = ab.shape[2]
    step = 512
    out = pl.BlockSpec((step, depth), lambda i: (i, 0))
    return pl.pallas_call(
        grads_kernel,
        grid=(pl.cdiv(width, step),),
        in_specs=[
            pl.BlockSpec((3, step, 256), lambda i: (0, i, 0)),
            pl.BlockSpec((2, 256, depth), lambda i: (0, 0, 0)),
        ],
        out_specs=(out, out, out),
        out_shape=(jax.ShapeDtypeStruct((width, depth), BF16),) * 3,
        compiler_params=pltpu.CompilerParams(vmem_limit_bytes=56 * 1024 * 1024),
        name="grads",
    )(r, ab)


def body(tokens, out_grad, token_weight, gate_weight, up_weight, down_weight):
    width = gate_weight.shape[1]
    r, ab, input_grad = exchange(
        tokens, out_grad, token_weight, gate_weight.T, up_weight.T, down_weight
    )
    gate_grad, up_grad, down_grad = grads(r, ab, width)
    return input_grad, gate_grad.T, up_grad.T, down_grad


def solution(mesh):
    return jax.shard_map(
        body,
        mesh=mesh,
        in_specs=(
            P("col", "row"),
            P("col", "row"),
            P(),
            P("row", "col"),
            P("row", "col"),
            P("col", "row"),
        ),
        out_specs=(P("col", "row"), P("row", "col"), P("row", "col"), P("col", "row")),
        check_vma=False,
    )
```

```python
import functools

import jax
import jax.numpy as jnp
from jax import lax
from jax.experimental import pallas as pl
from jax.experimental.pallas import tpu as pltpu
from jax.sharding import PartitionSpec as P

BF16, F32 = jnp.bfloat16, jnp.float32
MESH = pl.DeviceIdType.MESH
LANE = 128
TILES = (3, 3, 4, 4, 2, 5, 4, 4)
REDUCE = ["zx", "zx", "xz", "zx", "xz", "zx", "zx", "xz"]
GATHER = ["xz", "xz", "zx", "zx", "xz", "xz", "zx", "xz"]
ORDER = (
    (0, 0), (0, 1), (0, 2), (0, 3), (0, 4), (1, 0), (0, 5), (1, 1), (0, 6), (2, 0), (1, 2), (2, 1),
    (1, 3), (1, 4), (0, 7), (3, 0), (1, 5), (3, 1), (1, 6), (2, 3), (2, 2), (1, 7), (2, 5), (4, 0),
    (2, 4), (4, 1), (3, 3), (3, 2), (2, 6), (3, 5), (3, 4), (2, 7), (5, 0), (4, 2), (5, 1), (4, 3),
    (3, 6), (4, 4), (4, 5), (3, 7), (6, 0), (5, 2), (4, 6), (5, 4), (6, 1), (5, 5), (5, 3), (4, 7),
    (7, 0), (6, 2), (5, 6), (8, 0), (6, 4), (7, 1), (5, 7), (7, 2), (8, 1), (6, 5), (6, 3), (6, 6),
    (7, 4), (8, 2), (7, 3), (6, 7), (8, 4), (7, 6), (7, 5), (8, 3), (7, 7), (8, 6), (8, 5), (8, 7),
)
NT = (((1,), (1,)), ((), ()))


def chunks_of(width):
    assert sum(TILES) == pl.cdiv(width, LANE)
    out, at = [], 0
    for t in TILES:
        out.append((at * LANE, t * LANE, min(t * LANE, width - at * LANE)))
        at += t
    return out


(
    PAIR, ZA, ZB, ZUP, ZDOWN, X1, GUP, GDOWN, FUP, FDOWN, XA, XB, XC, XD, CA, CB, CC, CD,
) = range(18)
PER_CHUNK = 18
COLS = 9 + 8


def exchange_kernel(
    width,
    tok, og, tw, wg_h, wu_h, wd_h,
    r_out, ab_out, ig_out,
    wg, wu, wd, ab, pf, pr, zs1, zr1, zs2, zr2, own, xs, xr, res, rt, ig, igs, igr,
    ssem, rsem, lsem, osem,
):
    chunks = chunks_of(width)
    n = len(chunks)
    row, k = lax.axis_index("row"), lax.axis_index("col")
    x, z, c = row // 8, (row // 2) % 4, row % 2
    y, h = k // 2, k % 2
    zp, zm, zo = (z + 1) % 4, (z + 3) % 4, (z + 2) % 4
    yp, ym, yo = (y + 1) % 4, (y + 3) % 4, (y + 2) % 4

    def rdev(xx, zz, cc):
        return (xx * 8 + zz * 2 + cc, k)

    def cdev(yy, hh):
        return (row, yy * 2 + hh)

    sib, xn = rdev(x, z, 1 - c), rdev(1 - x, z, c)
    up, down = rdev(x, zp, c), rdev(x, zm, c)

    sent = []

    def send(src, dst, idx, dev):
        copy = pltpu.make_async_remote_copy(
            src_ref=src, dst_ref=dst, send_sem=ssem.at[idx], recv_sem=rsem.at[idx],
            device_id=dev, device_id_type=MESH,
        )
        copy.start()
        sent.append(copy)

    def landed(ref, idx):
        pltpu.make_async_remote_copy(
            src_ref=ref, dst_ref=ref, send_sem=ssem.at[idx], recv_sem=rsem.at[idx],
            device_id=sib, device_id_type=MESH,
        ).wait_recv()

    mine = pl.ds(pl.multiple_of(k * 32, 32), 32)
    first = [
        pltpu.make_async_copy(tok, ab.at[0, mine], lsem.at[0]),
        pltpu.make_async_copy(og, ab.at[1, mine], lsem.at[1]),
    ]
    weights = [
        pltpu.make_async_copy(wg_h, wg, lsem.at[2]),
        pltpu.make_async_copy(wu_h, wu, lsem.at[3]),
        pltpu.make_async_copy(wd_h, wd, lsem.at[4]),
    ]
    for copy in first + weights:
        copy.start()

    barrier = pltpu.get_barrier_semaphore()
    greeted = [sib, xn, up, down]
    for step in range(1, 8):
        greeted.append((row, (k + step) % 8))
    for dev in greeted:
        pl.semaphore_signal(barrier, inc=1, device_id=dev, device_id_type=MESH)
    for copy in first:
        copy.wait()
    pl.semaphore_wait(barrier, len(greeted))

    base = n * PER_CHUNK

    def block(yy, hh):
        return pl.ds(pl.multiple_of((yy * 2 + hh) * 32, 32), 32)

    def both(yy, hh):
        return ab.at[:, block(yy, hh)]

    def one(part, yy, hh):
        return ab.at[part, block(yy, hh)]

    me = both(y, h)
    send(me, me, base + 2, cdev(y, 1 - h))
    send(me, me, base + 0, cdev(yp, h))
    send(me, me, base + 1, cdev(ym, h))
    landed(both(ym, h), base + 0)
    send(one(0, ym, h), one(0, ym, h), base + 5, cdev(yp, h))
    landed(both(yp, h), base + 1)
    send(one(1, yp, h), one(1, yp, h), base + 6, cdev(ym, h))
    landed(both(y, 1 - h), base + 2)
    send(both(y, 1 - h), both(y, 1 - h), base + 3, cdev(yp, h))
    send(both(y, 1 - h), both(y, 1 - h), base + 4, cdev(ym, h))
    landed(both(ym, 1 - h), base + 3)
    send(one(0, ym, 1 - h), one(0, ym, 1 - h), base + 7, cdev(yp, h))
    landed(both(yp, 1 - h), base + 4)
    send(one(1, yp, 1 - h), one(1, yp, 1 - h), base + 8, cdev(ym, h))
    landed(one(0, yo, h), base + 5)
    landed(one(1, yo, h), base + 6)
    landed(one(0, yo, 1 - h), base + 7)
    landed(one(1, yo, 1 - h), base + 8)
    outs = [pltpu.make_async_copy(ab, ab_out, osem.at[0])]
    outs[0].start()
    for copy in weights:
        copy.wait()

    first_token = c * 128 + x * 64 + z * 16
    lanes = lax.broadcasted_iota(jnp.int32, (16, 256), 1)
    rows = lax.broadcasted_iota(jnp.int32, (16, 256), 0)
    column = jnp.sum(
        jnp.where(lanes == rows + first_token, jnp.broadcast_to(tw[...], (16, 256)), 0.0),
        axis=1, keepdims=True,
    )

    def span(j):
        o, w, _ = chunks[j]
        return slice(3 * o, 3 * o + 3 * w)

    def halves(j):
        o, w, _ = chunks[j]
        cut = 3 * o + (3 * w // LANE // 2) * LANE
        return slice(3 * o, cut), slice(cut, 3 * o + 3 * w)

    def products(j):
        o, w, valid = chunks[j]
        for part in range(3):
            for at in range(0, valid, 256):
                size = min(256, valid - at)
                lo = o + at
                value = lax.dot_general(
                    ab[part // 2], (wg, wu, wd)[part][lo : lo + size, :], NT,
                    preferred_element_type=F32,
                )
                to = 3 * o + part * w + at
                pf[:, :, :, :, to : to + size] = value.reshape(2, 2, 4, 16, size)
            if valid < w:
                pad = slice(3 * o + part * w + valid, 3 * o + part * w + w)
                pf[:, :, :, :, pad] = jnp.zeros((2, 2, 4, 16, w - valid), F32)
        cols = span(j)
        send(
            pf.at[1 - c, :, :, :, cols], pr.at[:, :, :, cols], j * PER_CHUNK + PAIR, sib
        )

    def chip(xx, zz, cols):
        return pf[c, xx, zz, :, cols] + pr[xx, zz, :, cols]

    def chip_sum(xx, zz, cols):
        return chip(xx, zz, cols) + xr[zz, :, cols].astype(F32)

    def zx_far(j):
        m, cols = j * PER_CHUNK, span(j)
        landed(pr.at[:, :, :, cols], m + PAIR)
        zs1[0, :, cols] = chip(0, zo, cols).astype(BF16)
        send(zs1.at[0, :, cols], zr1.at[0, :, cols], m + ZA, up)
        zs1[1, :, cols] = chip(1, zo, cols).astype(BF16)
        send(zs1.at[1, :, cols], zr1.at[1, :, cols], m + ZB, down)

    def zx_near(j):
        m, cols = j * PER_CHUNK, span(j)
        landed(zr1.at[0, :, cols], m + ZA)
        zs2[0, 0, :, cols] = (chip(0, zp, cols) + zr1[0, :, cols].astype(F32)).astype(BF16)
        zs2[0, 1, :, cols] = chip(1, zp, cols).astype(BF16)
        send(zs2.at[0, :, :, cols], zr2.at[0, :, :, cols], m + ZUP, up)
        landed(zr1.at[1, :, cols], m + ZB)
        zs2[1, 0, :, cols] = chip(0, zm, cols).astype(BF16)
        zs2[1, 1, :, cols] = (chip(1, zm, cols) + zr1[1, :, cols].astype(F32)).astype(BF16)
        send(zs2.at[1, :, :, cols], zr2.at[1, :, :, cols], m + ZDOWN, down)

    def zx_cross(j):
        m, cols = j * PER_CHUNK, span(j)
        landed(zr2.at[0, :, :, cols], m + ZUP)
        landed(zr2.at[1, :, :, cols], m + ZDOWN)

        def ring(xx):
            return chip(xx, z, cols) + zr2[0, xx, :, cols].astype(F32) + zr2[1, xx, :, cols].astype(F32)

        xs[0, :, cols] = ring(1 - x).astype(BF16)
        send(xs.at[0, :, cols], xr.at[0, :, cols], m + X1, xn)
        own[:, cols] = ring(x)

    def zx_total(j):
        m, cols = j * PER_CHUNK, span(j)
        landed(xr.at[0, :, cols], m + X1)
        return lambda at: own[:, at] + xr[0, :, at].astype(F32)

    def xz_cross(j):
        m, cols = j * PER_CHUNK, span(j)
        landed(pr.at[:, :, :, cols], m + PAIR)
        xs[:, :, cols] = (pf[c, 1 - x, :, :, cols] + pr[1 - x, :, :, cols]).astype(BF16)
        send(xs.at[:, :, cols], xr.at[:, :, cols], m + X1, xn)

    def xz_far(j):
        m, cols = j * PER_CHUNK, span(j)
        lo, hi = halves(j)
        landed(xr.at[:, :, cols], m + X1)
        zs1[0, :, lo] = chip_sum(x, zo, lo).astype(BF16)
        send(zs1.at[0, :, lo], zr1.at[0, :, lo], m + ZA, up)
        zs1[1, :, hi] = chip_sum(x, zo, hi).astype(BF16)
        send(zs1.at[1, :, hi], zr1.at[1, :, hi], m + ZB, down)

    def xz_near(j):
        m, cols = j * PER_CHUNK, span(j)
        lo, hi = halves(j)
        landed(zr1.at[0, :, lo], m + ZA)
        zs2[0, 0, :, lo] = (chip_sum(x, zp, lo) + zr1[0, :, lo].astype(F32)).astype(BF16)
        zs2[0, 0, :, hi] = chip_sum(x, zp, hi).astype(BF16)
        send(zs2.at[0, 0, :, cols], zr2.at[0, 0, :, cols], m + ZUP, up)
        landed(zr1.at[1, :, hi], m + ZB)
        zs2[1, 0, :, lo] = chip_sum(x, zm, lo).astype(BF16)
        zs2[1, 0, :, hi] = (chip_sum(x, zm, hi) + zr1[1, :, hi].astype(F32)).astype(BF16)
        send(zs2.at[1, 0, :, cols], zr2.at[1, 0, :, cols], m + ZDOWN, down)

    def xz_total(j):
        m, cols = j * PER_CHUNK, span(j)
        landed(zr2.at[0, 0, :, cols], m + ZUP)
        landed(zr2.at[1, 0, :, cols], m + ZDOWN)
        return lambda at: (
            chip_sum(x, z, at) + zr2[0, 0, :, at].astype(F32) + zr2[1, 0, :, at].astype(F32)
        )

    def here(xx, zz, cols):
        return res.at[c, xx, zz, :, cols]

    def push(xx, zz, cols, idx, dev):
        send(here(xx, zz, cols), here(xx, zz, cols), idx, dev)

    def push_pair(zz, cols, idx, dev):
        part = res.at[c, :, zz, :, cols]
        send(part, part, idx, dev)

    def activate(j):
        o, w, _ = chunks[j]
        m, cols = j * PER_CHUNK, span(j)
        total = (xz_total if REDUCE[j] == "xz" else zx_total)(j)

        def place(part):
            return slice(3 * o + part * w, 3 * o + part * w + w)

        gate, linear, back = total(place(0)), total(place(1)), total(place(2))
        sig = jax.nn.sigmoid(gate)
        silu = gate * sig
        scaled = column * back
        for part, value in enumerate((
            column * (silu * linear),
            scaled * linear * sig * (1.0 + gate * (1.0 - sig)),
            scaled * silu,
        )):
            res[c, x, z, :, place(part)] = value.astype(BF16)
        push(x, z, cols, m + XA, xn)
        if GATHER[j] == "zx":
            push(x, z, cols, m + GUP, up)
            push(x, z, cols, m + GDOWN, down)

    def zx_gather_near(j):
        m, cols = j * PER_CHUNK, span(j)
        lo, hi = halves(j)
        landed(here(x, zm, cols), m + GUP)
        push(x, zm, lo, m + FUP, up)
        push(x, zm, cols, m + XB, xn)
        landed(here(x, zp, cols), m + GDOWN)
        push(x, zp, hi, m + FDOWN, down)
        push(x, zp, cols, m + XC, xn)

    def zx_gather_far(j):
        m, cols = j * PER_CHUNK, span(j)
        lo, hi = halves(j)
        landed(here(x, zo, lo), m + FUP)
        landed(here(x, zo, hi), m + FDOWN)
        push(x, zo, cols, m + XD, xn)
        part = res.at[c, x, :, :, cols]
        send(part, part, m + CA, sib)

    def zx_gather_cross(j):
        m, cols = j * PER_CHUNK, span(j)
        landed(here(1 - x, z, cols), m + XA)
        landed(here(1 - x, zm, cols), m + XB)
        landed(here(1 - x, zp, cols), m + XC)
        landed(here(1 - x, zo, cols), m + XD)
        part = res.at[c, 1 - x, :, :, cols]
        send(part, part, m + CB, sib)

    def zx_all(j):
        m, cols = j * PER_CHUNK, span(j)
        landed(res.at[1 - c, x, :, :, cols], m + CA)
        landed(res.at[1 - c, 1 - x, :, :, cols], m + CB)

    def xz_gather_cross(j):
        m, cols = j * PER_CHUNK, span(j)
        landed(here(1 - x, z, cols), m + XA)
        push_pair(z, cols, m + GUP, up)
        push_pair(z, cols, m + GDOWN, down)
        push_pair(z, cols, m + CA, sib)

    def xz_gather_near(j):
        m, cols = j * PER_CHUNK, span(j)
        landed(res.at[c, :, zm, :, cols], m + GUP)
        push(0, zm, cols, m + FUP, up)
        landed(res.at[c, :, zp, :, cols], m + GDOWN)
        push(1, zp, cols, m + FDOWN, down)
        push_pair(zm, cols, m + CB, sib)
        push_pair(zp, cols, m + CC, sib)

    def xz_gather_far(j):
        m, cols = j * PER_CHUNK, span(j)
        landed(here(0, zo, cols), m + FUP)
        landed(here(1, zo, cols), m + FDOWN)
        push_pair(zo, cols, m + CD, sib)

    def xz_all(j):
        m, cols = j * PER_CHUNK, span(j)
        for zz, idx in ((z, CA), (zm, CB), (zp, CC), (zo, CD)):
            landed(res.at[1 - c, :, zz, :, cols], m + idx)

    def finish(j):
        o, w, valid = chunks[j]
        m, cols = j * PER_CHUNK, span(j)
        (zx_all if GATHER[j] == "zx" else xz_all)(j)
        for part, wide in ((1, wg), (2, wu)):
            at = 3 * o + part * w
            piece = res[:, :, :, :, at : at + valid].reshape(256, valid)
            value = jnp.dot(piece, wide[o : o + valid, :], preferred_element_type=F32)
            if j == 0 and part == 1:
                ig[...] = value
            else:
                ig[...] += value
        for part in range(3):
            at = 3 * o + part * w
            rt[part, o : o + w, :] = res[:, :, :, :, at : at + w].reshape(256, w).T
        copy = pltpu.make_async_copy(
            rt.at[:, o : o + w], r_out.at[:, o : o + w], osem.at[1 + j]
        )
        copy.start()
        outs.append(copy)

    reduce = {"zx": (zx_far, zx_near, zx_cross), "xz": (xz_cross, xz_far, xz_near)}
    gather = {
        "zx": (zx_gather_near, zx_gather_far, zx_gather_cross),
        "xz": (xz_gather_cross, xz_gather_near, xz_gather_far),
    }
    for stage, j in ORDER:
        (products, *reduce[REDUCE[j]], activate, *gather[GATHER[j]], finish)[stage](j)

    igs[...] = ig[...].astype(BF16)
    for step in range(1, 8):
        other = (k + step) % 8
        send(
            igs.at[pl.ds(pl.multiple_of(other * 32, 32), 32)], igr.at[step], base + 9 + step,
            (row, other),
        )
    total = ig[mine, :]
    for step in range(1, 8):
        landed(igr.at[step], base + 9 + step)
        total = total + igr[step].astype(F32)
    ig_out[...] = total

    for copy in sent:
        copy.wait_send()
    for copy in outs:
        copy.wait()


def exchange(tokens, out_grad, token_weight, gate_weight, up_weight, down_weight):
    width, depth = gate_weight.shape
    wide = pl.cdiv(width, LANE) * LANE
    cols = 3 * wide
    n = len(TILES)
    messages = n * PER_CHUNK + COLS
    hbm = pl.BlockSpec(memory_space=pl.ANY)
    vmem = pl.BlockSpec(memory_space=pltpu.VMEM)
    return pl.pallas_call(
        functools.partial(exchange_kernel, width),
        out_shape=(
            jax.ShapeDtypeStruct((3, wide, 256), BF16),
            jax.ShapeDtypeStruct((2, 256, depth), BF16),
            jax.ShapeDtypeStruct((32, depth), F32),
        ),
        in_specs=[hbm, hbm, vmem, hbm, hbm, hbm],
        out_specs=(hbm, hbm, vmem),
        scratch_shapes=[
            pltpu.VMEM((width, depth), BF16),
            pltpu.VMEM((width, depth), BF16),
            pltpu.VMEM((width, depth), BF16),
            pltpu.VMEM((2, 256, depth), BF16),
            pltpu.VMEM((2, 2, 4, 16, cols), F32),
            pltpu.VMEM((2, 4, 16, cols), F32),
            pltpu.VMEM((2, 16, cols), BF16),
            pltpu.VMEM((2, 16, cols), BF16),
            pltpu.VMEM((2, 2, 16, cols), BF16),
            pltpu.VMEM((2, 2, 16, cols), BF16),
            pltpu.VMEM((16, cols), F32),
            pltpu.VMEM((4, 16, cols), BF16),
            pltpu.VMEM((4, 16, cols), BF16),
            pltpu.VMEM((2, 2, 4, 16, cols), BF16),
            pltpu.VMEM((3, wide, 256), BF16),
            pltpu.VMEM((256, depth), F32),
            pltpu.VMEM((256, depth), BF16),
            pltpu.VMEM((8, 32, depth), BF16),
            pltpu.SemaphoreType.DMA((messages,)),
            pltpu.SemaphoreType.DMA((messages,)),
            pltpu.SemaphoreType.DMA((5,)),
            pltpu.SemaphoreType.DMA((1 + n,)),
        ],
        compiler_params=pltpu.CompilerParams(
            collective_id=0, has_side_effects=True, vmem_limit_bytes=56 * 1024 * 1024
        ),
        cost_estimate=pl.CostEstimate(
            flops=10 * 256 * depth * width, bytes_accessed=6 * depth * width + 6 * 256 * width,
            transcendentals=0,
        ),
        name="exchange",
    )(tokens, out_grad, token_weight.reshape(1, 256), gate_weight, up_weight, down_weight)


def grads_kernel(r, ab, gate_grad, up_grad, down_grad):
    for part, out in ((1, gate_grad), (2, up_grad), (0, down_grad)):
        out[...] = jnp.dot(
            r[part], ab[0 if part else 1], preferred_element_type=F32
        ).astype(BF16)


def grads(r, ab, width):
    depth = ab.shape[2]
    step = 512
    out = pl.BlockSpec((step, depth), lambda i: (i, 0))
    return pl.pallas_call(
        grads_kernel,
        grid=(pl.cdiv(width, step),),
        in_specs=[
            pl.BlockSpec((3, step, 256), lambda i: (0, i, 0)),
            pl.BlockSpec((2, 256, depth), lambda i: (0, 0, 0)),
        ],
        out_specs=(out, out, out),
        out_shape=(jax.ShapeDtypeStruct((width, depth), BF16),) * 3,
        compiler_params=pltpu.CompilerParams(vmem_limit_bytes=56 * 1024 * 1024),
        name="grads",
    )(r, ab)


def body(tokens, out_grad, token_weight, gate_weight, up_weight, down_weight):
    width = gate_weight.shape[1]
    r, ab, input_grad = exchange(
        tokens, out_grad, token_weight, gate_weight.T, up_weight.T, down_weight
    )
    gate_grad, up_grad, down_grad = grads(r, ab, width)
    return input_grad, gate_grad.T, up_grad.T, down_grad


def solution(mesh):
    return jax.shard_map(
        body,
        mesh=mesh,
        in_specs=(
            P("col", "row"),
            P("col", "row"),
            P(),
            P("row", "col"),
            P("row", "col"),
            P("col", "row"),
        ),
        out_specs=(P("col", "row"), P("row", "col"), P("row", "col"), P("col", "row")),
        check_vma=False,
    )
```

```python
import functools

import jax
import jax.numpy as jnp
from jax import lax
from jax.experimental import pallas as pl
from jax.experimental.pallas import tpu as pltpu
from jax.sharding import PartitionSpec as P

BF16, F32 = jnp.bfloat16, jnp.float32
MESH = pl.DeviceIdType.MESH
LANE = 128
TILES = (3, 3, 4, 4, 2, 5, 4, 4)
REDUCE = ["zx", "zx", "xz", "zx", "xz", "zx", "zx", "xz"]
GATHER = ["xz", "xz", "zx", "zx", "xz", "xz", "zx", "xz"]
ORDER = (
    (0, 0), (0, 1), (0, 2), (0, 3), (0, 4), (1, 0), (0, 5), (1, 1), (0, 6), (2, 0), (1, 2), (2, 1),
    (1, 3), (1, 4), (0, 7), (3, 0), (1, 5), (3, 1), (1, 6), (2, 3), (2, 2), (1, 7), (2, 5), (4, 0),
    (2, 4), (4, 1), (3, 3), (3, 2), (2, 6), (3, 5), (3, 4), (2, 7), (5, 0), (4, 2), (5, 1), (4, 3),
    (3, 6), (4, 4), (4, 5), (3, 7), (6, 0), (5, 2), (4, 6), (5, 4), (6, 1), (5, 5), (5, 3), (4, 7),
    (7, 0), (6, 2), (5, 6), (8, 0), (6, 4), (7, 1), (5, 7), (7, 2), (8, 1), (6, 5), (6, 3), (6, 6),
    (7, 4), (8, 2), (7, 3), (6, 7), (8, 4), (7, 6), (7, 5), (8, 3), (7, 7), (8, 6), (8, 5), (8, 7),
)
NT = (((1,), (1,)), ((), ()))


def chunks_of(width):
    assert sum(TILES) == pl.cdiv(width, LANE)
    out, at = [], 0
    for t in TILES:
        out.append((at * LANE, t * LANE, min(t * LANE, width - at * LANE)))
        at += t
    return out


(
    PAIR, ZA, ZB, ZUP, ZDOWN, X1, GUP, GDOWN, FUP, FDOWN, XA, XB, XC, XD, CA, CB, CC, CD,
) = range(18)
PER_CHUNK = 18
COLS = 9 + 8


def exchange_kernel(
    width,
    tok, og, tw, wg_h, wu_h, wd_h,
    r_out, ab_out, ig_out,
    wg, wu, wd, ab, pf, pr, zs1, zr1, zs2, zr2, own, xs, xr, res, rt, ig, igs, igr,
    ssem, rsem, lsem, osem,
):
    chunks = chunks_of(width)
    n = len(chunks)
    row, k = lax.axis_index("row"), lax.axis_index("col")
    x, z, c = row // 8, (row // 2) % 4, row % 2
    y, h = k // 2, k % 2
    zp, zm, zo = (z + 1) % 4, (z + 3) % 4, (z + 2) % 4
    yp, ym, yo = (y + 1) % 4, (y + 3) % 4, (y + 2) % 4

    def rdev(xx, zz, cc):
        return (xx * 8 + zz * 2 + cc, k)

    def cdev(yy, hh):
        return (row, yy * 2 + hh)

    sib, xn = rdev(x, z, 1 - c), rdev(1 - x, z, c)
    up, down = rdev(x, zp, c), rdev(x, zm, c)

    sent = []

    def send(src, dst, idx, dev):
        copy = pltpu.make_async_remote_copy(
            src_ref=src, dst_ref=dst, send_sem=ssem.at[idx], recv_sem=rsem.at[idx],
            device_id=dev, device_id_type=MESH,
        )
        copy.start()
        sent.append(copy)

    def landed(ref, idx):
        pltpu.make_async_remote_copy(
            src_ref=ref, dst_ref=ref, send_sem=ssem.at[idx], recv_sem=rsem.at[idx],
            device_id=sib, device_id_type=MESH,
        ).wait_recv()

    mine = pl.ds(pl.multiple_of(k * 32, 32), 32)
    first = [
        pltpu.make_async_copy(tok, ab.at[0, mine], lsem.at[0]),
        pltpu.make_async_copy(og, ab.at[1, mine], lsem.at[1]),
    ]
    weights = [
        pltpu.make_async_copy(wg_h, wg, lsem.at[2]),
        pltpu.make_async_copy(wu_h, wu, lsem.at[3]),
        pltpu.make_async_copy(wd_h, wd, lsem.at[4]),
    ]
    for copy in first + weights:
        copy.start()

    barrier = pltpu.get_barrier_semaphore()
    greeted = [sib, xn, up, down]
    for step in range(1, 8):
        greeted.append((row, (k + step) % 8))
    for dev in greeted:
        pl.semaphore_signal(barrier, inc=1, device_id=dev, device_id_type=MESH)
    for copy in first:
        copy.wait()
    pl.semaphore_wait(barrier, len(greeted))

    base = n * PER_CHUNK

    def block(yy, hh):
        return pl.ds(pl.multiple_of((yy * 2 + hh) * 32, 32), 32)

    def both(yy, hh):
        return ab.at[:, block(yy, hh)]

    def one(part, yy, hh):
        return ab.at[part, block(yy, hh)]

    me = both(y, h)
    send(me, me, base + 2, cdev(y, 1 - h))
    send(me, me, base + 0, cdev(yp, h))
    send(me, me, base + 1, cdev(ym, h))
    landed(both(ym, h), base + 0)
    send(one(0, ym, h), one(0, ym, h), base + 5, cdev(yp, h))
    landed(both(yp, h), base + 1)
    send(one(1, yp, h), one(1, yp, h), base + 6, cdev(ym, h))
    landed(both(y, 1 - h), base + 2)
    send(both(y, 1 - h), both(y, 1 - h), base + 3, cdev(yp, h))
    send(both(y, 1 - h), both(y, 1 - h), base + 4, cdev(ym, h))
    landed(both(ym, 1 - h), base + 3)
    send(one(0, ym, 1 - h), one(0, ym, 1 - h), base + 7, cdev(yp, h))
    landed(both(yp, 1 - h), base + 4)
    send(one(1, yp, 1 - h), one(1, yp, 1 - h), base + 8, cdev(ym, h))
    landed(one(0, yo, h), base + 5)
    landed(one(1, yo, h), base + 6)
    landed(one(0, yo, 1 - h), base + 7)
    landed(one(1, yo, 1 - h), base + 8)
    outs = [pltpu.make_async_copy(ab, ab_out, osem.at[0])]
    outs[0].start()
    for copy in weights:
        copy.wait()

    first_token = c * 128 + x * 64 + z * 16
    lanes = lax.broadcasted_iota(jnp.int32, (16, 256), 1)
    rows = lax.broadcasted_iota(jnp.int32, (16, 256), 0)
    column = jnp.sum(
        jnp.where(lanes == rows + first_token, jnp.broadcast_to(tw[...], (16, 256)), 0.0),
        axis=1, keepdims=True,
    )

    def span(j):
        o, w, _ = chunks[j]
        return slice(3 * o, 3 * o + 3 * w)

    def halves(j):
        o, w, _ = chunks[j]
        cut = 3 * o + (3 * w // LANE // 2) * LANE
        return slice(3 * o, cut), slice(cut, 3 * o + 3 * w)

    def products(j):
        o, w, valid = chunks[j]
        for part in range(3):
            for at in range(0, valid, 256):
                size = min(256, valid - at)
                lo = o + at
                value = lax.dot_general(
                    ab[part // 2], (wg, wu, wd)[part][lo : lo + size, :], NT,
                    preferred_element_type=F32,
                )
                to = 3 * o + part * w + at
                pf[:, :, :, :, to : to + size] = value.reshape(2, 2, 4, 16, size)
            if valid < w:
                pad = slice(3 * o + part * w + valid, 3 * o + part * w + w)
                pf[:, :, :, :, pad] = jnp.zeros((2, 2, 4, 16, w - valid), F32)
        cols = span(j)
        send(
            pf.at[1 - c, :, :, :, cols], pr.at[:, :, :, cols], j * PER_CHUNK + PAIR, sib
        )

    def chip(xx, zz, cols):
        return pf[c, xx, zz, :, cols] + pr[xx, zz, :, cols]

    def chip_sum(xx, zz, cols):
        return chip(xx, zz, cols) + xr[zz, :, cols].astype(F32)

    def zx_far(j):
        m, cols = j * PER_CHUNK, span(j)
        landed(pr.at[:, :, :, cols], m + PAIR)
        zs1[0, :, cols] = chip(0, zo, cols).astype(BF16)
        send(zs1.at[0, :, cols], zr1.at[0, :, cols], m + ZA, up)
        zs1[1, :, cols] = chip(1, zo, cols).astype(BF16)
        send(zs1.at[1, :, cols], zr1.at[1, :, cols], m + ZB, down)

    def zx_near(j):
        m, cols = j * PER_CHUNK, span(j)
        landed(zr1.at[0, :, cols], m + ZA)
        zs2[0, 0, :, cols] = (chip(0, zp, cols) + zr1[0, :, cols].astype(F32)).astype(BF16)
        zs2[0, 1, :, cols] = chip(1, zp, cols).astype(BF16)
        send(zs2.at[0, :, :, cols], zr2.at[0, :, :, cols], m + ZUP, up)
        landed(zr1.at[1, :, cols], m + ZB)
        zs2[1, 0, :, cols] = chip(0, zm, cols).astype(BF16)
        zs2[1, 1, :, cols] = (chip(1, zm, cols) + zr1[1, :, cols].astype(F32)).astype(BF16)
        send(zs2.at[1, :, :, cols], zr2.at[1, :, :, cols], m + ZDOWN, down)

    def zx_cross(j):
        m, cols = j * PER_CHUNK, span(j)
        landed(zr2.at[0, :, :, cols], m + ZUP)
        landed(zr2.at[1, :, :, cols], m + ZDOWN)

        def ring(xx):
            return chip(xx, z, cols) + zr2[0, xx, :, cols].astype(F32) + zr2[1, xx, :, cols].astype(F32)

        xs[0, :, cols] = ring(1 - x).astype(BF16)
        send(xs.at[0, :, cols], xr.at[0, :, cols], m + X1, xn)
        own[:, cols] = ring(x)

    def zx_total(j):
        m, cols = j * PER_CHUNK, span(j)
        landed(xr.at[0, :, cols], m + X1)
        return lambda at: own[:, at] + xr[0, :, at].astype(F32)

    def xz_cross(j):
        m, cols = j * PER_CHUNK, span(j)
        landed(pr.at[:, :, :, cols], m + PAIR)
        xs[:, :, cols] = (pf[c, 1 - x, :, :, cols] + pr[1 - x, :, :, cols]).astype(BF16)
        send(xs.at[:, :, cols], xr.at[:, :, cols], m + X1, xn)

    def xz_far(j):
        m, cols = j * PER_CHUNK, span(j)
        lo, hi = halves(j)
        landed(xr.at[:, :, cols], m + X1)
        zs1[0, :, lo] = chip_sum(x, zo, lo).astype(BF16)
        send(zs1.at[0, :, lo], zr1.at[0, :, lo], m + ZA, up)
        zs1[1, :, hi] = chip_sum(x, zo, hi).astype(BF16)
        send(zs1.at[1, :, hi], zr1.at[1, :, hi], m + ZB, down)

    def xz_near(j):
        m, cols = j * PER_CHUNK, span(j)
        lo, hi = halves(j)
        landed(zr1.at[0, :, lo], m + ZA)
        zs2[0, 0, :, lo] = (chip_sum(x, zp, lo) + zr1[0, :, lo].astype(F32)).astype(BF16)
        zs2[0, 0, :, hi] = chip_sum(x, zp, hi).astype(BF16)
        send(zs2.at[0, 0, :, cols], zr2.at[0, 0, :, cols], m + ZUP, up)
        landed(zr1.at[1, :, hi], m + ZB)
        zs2[1, 0, :, lo] = chip_sum(x, zm, lo).astype(BF16)
        zs2[1, 0, :, hi] = (chip_sum(x, zm, hi) + zr1[1, :, hi].astype(F32)).astype(BF16)
        send(zs2.at[1, 0, :, cols], zr2.at[1, 0, :, cols], m + ZDOWN, down)

    def xz_total(j):
        m, cols = j * PER_CHUNK, span(j)
        landed(zr2.at[0, 0, :, cols], m + ZUP)
        landed(zr2.at[1, 0, :, cols], m + ZDOWN)
        return lambda at: (
            chip_sum(x, z, at) + zr2[0, 0, :, at].astype(F32) + zr2[1, 0, :, at].astype(F32)
        )

    def here(xx, zz, cols):
        return res.at[c, xx, zz, :, cols]

    def push(xx, zz, cols, idx, dev):
        send(here(xx, zz, cols), here(xx, zz, cols), idx, dev)

    def push_pair(zz, cols, idx, dev):
        part = res.at[c, :, zz, :, cols]
        send(part, part, idx, dev)

    def activate(j):
        o, w, _ = chunks[j]
        m, cols = j * PER_CHUNK, span(j)
        total = (xz_total if REDUCE[j] == "xz" else zx_total)(j)

        def place(part):
            return slice(3 * o + part * w, 3 * o + part * w + w)

        gate, linear, back = total(place(0)), total(place(1)), total(place(2))
        sig = jax.nn.sigmoid(gate)
        silu = gate * sig
        scaled = column * back
        for part, value in enumerate((
            column * (silu * linear),
            scaled * linear * sig * (1.0 + gate * (1.0 - sig)),
            scaled * silu,
        )):
            res[c, x, z, :, place(part)] = value.astype(BF16)
        push(x, z, cols, m + XA, xn)
        if GATHER[j] == "zx":
            push(x, z, cols, m + GUP, up)
            push(x, z, cols, m + GDOWN, down)

    def zx_gather_near(j):
        m, cols = j * PER_CHUNK, span(j)
        lo, hi = halves(j)
        landed(here(x, zm, cols), m + GUP)
        push(x, zm, lo, m + FUP, up)
        push(x, zm, cols, m + XB, xn)
        landed(here(x, zp, cols), m + GDOWN)
        push(x, zp, hi, m + FDOWN, down)
        push(x, zp, cols, m + XC, xn)

    def zx_gather_far(j):
        m, cols = j * PER_CHUNK, span(j)
        lo, hi = halves(j)
        landed(here(x, zo, lo), m + FUP)
        landed(here(x, zo, hi), m + FDOWN)
        push(x, zo, cols, m + XD, xn)
        part = res.at[c, x, :, :, cols]
        send(part, part, m + CA, sib)

    def zx_gather_cross(j):
        m, cols = j * PER_CHUNK, span(j)
        landed(here(1 - x, z, cols), m + XA)
        landed(here(1 - x, zm, cols), m + XB)
        landed(here(1 - x, zp, cols), m + XC)
        landed(here(1 - x, zo, cols), m + XD)
        part = res.at[c, 1 - x, :, :, cols]
        send(part, part, m + CB, sib)

    def zx_all(j):
        m, cols = j * PER_CHUNK, span(j)
        landed(res.at[1 - c, x, :, :, cols], m + CA)
        landed(res.at[1 - c, 1 - x, :, :, cols], m + CB)

    def xz_gather_cross(j):
        m, cols = j * PER_CHUNK, span(j)
        landed(here(1 - x, z, cols), m + XA)
        push_pair(z, cols, m + GUP, up)
        push_pair(z, cols, m + GDOWN, down)
        push_pair(z, cols, m + CA, sib)

    def xz_gather_near(j):
        m, cols = j * PER_CHUNK, span(j)
        landed(res.at[c, :, zm, :, cols], m + GUP)
        push(0, zm, cols, m + FUP, up)
        landed(res.at[c, :, zp, :, cols], m + GDOWN)
        push(1, zp, cols, m + FDOWN, down)
        push_pair(zm, cols, m + CB, sib)
        push_pair(zp, cols, m + CC, sib)

    def xz_gather_far(j):
        m, cols = j * PER_CHUNK, span(j)
        landed(here(0, zo, cols), m + FUP)
        landed(here(1, zo, cols), m + FDOWN)
        push_pair(zo, cols, m + CD, sib)

    def xz_all(j):
        m, cols = j * PER_CHUNK, span(j)
        for zz, idx in ((z, CA), (zm, CB), (zp, CC), (zo, CD)):
            landed(res.at[1 - c, :, zz, :, cols], m + idx)

    def finish(j):
        o, w, valid = chunks[j]
        m, cols = j * PER_CHUNK, span(j)
        (zx_all if GATHER[j] == "zx" else xz_all)(j)
        for part, wide in ((1, wg), (2, wu)):
            at = 3 * o + part * w
            piece = res[:, :, :, :, at : at + valid].reshape(256, valid)
            value = jnp.dot(piece, wide[o : o + valid, :], preferred_element_type=F32)
            if j == 0 and part == 1:
                ig[...] = value
            else:
                ig[...] += value
        for part in range(3):
            at = 3 * o + part * w
            rt[part, o : o + w, :] = res[:, :, :, :, at : at + w].reshape(256, w).T
        copy = pltpu.make_async_copy(
            rt.at[:, o : o + w], r_out.at[:, o : o + w], osem.at[1 + j]
        )
        copy.start()
        outs.append(copy)

    reduce = {"zx": (zx_far, zx_near, zx_cross), "xz": (xz_cross, xz_far, xz_near)}
    gather = {
        "zx": (zx_gather_near, zx_gather_far, zx_gather_cross),
        "xz": (xz_gather_cross, xz_gather_near, xz_gather_far),
    }
    for stage, j in ORDER:
        (products, *reduce[REDUCE[j]], activate, *gather[GATHER[j]], finish)[stage](j)

    igs[...] = ig[...].astype(BF16)
    for step in range(1, 8):
        other = (k + step) % 8
        send(
            igs.at[pl.ds(pl.multiple_of(other * 32, 32), 32)], igr.at[step], base + 9 + step,
            (row, other),
        )
    total = ig[mine, :]
    for step in range(1, 8):
        landed(igr.at[step], base + 9 + step)
        total = total + igr[step].astype(F32)
    ig_out[...] = total

    for copy in sent:
        copy.wait_send()
    for copy in outs:
        copy.wait()


def exchange(tokens, out_grad, token_weight, gate_weight, up_weight, down_weight):
    width, depth = gate_weight.shape
    wide = pl.cdiv(width, LANE) * LANE
    cols = 3 * wide
    n = len(TILES)
    messages = n * PER_CHUNK + COLS
    hbm = pl.BlockSpec(memory_space=pl.ANY)
    vmem = pl.BlockSpec(memory_space=pltpu.VMEM)
    return pl.pallas_call(
        functools.partial(exchange_kernel, width),
        out_shape=(
            pltpu.VMEM((3, wide, 256), BF16),
            pltpu.VMEM((2, 256, depth), BF16),
            jax.ShapeDtypeStruct((32, depth), F32),
        ),
        in_specs=[hbm, hbm, vmem, hbm, hbm, hbm],
        out_specs=(hbm, hbm, vmem),
        scratch_shapes=[
            pltpu.VMEM((width, depth), BF16),
            pltpu.VMEM((width, depth), BF16),
            pltpu.VMEM((width, depth), BF16),
            pltpu.VMEM((2, 256, depth), BF16),
            pltpu.VMEM((2, 2, 4, 16, cols), F32),
            pltpu.VMEM((2, 4, 16, cols), F32),
            pltpu.VMEM((2, 16, cols), BF16),
            pltpu.VMEM((2, 16, cols), BF16),
            pltpu.VMEM((2, 2, 16, cols), BF16),
            pltpu.VMEM((2, 2, 16, cols), BF16),
            pltpu.VMEM((16, cols), F32),
            pltpu.VMEM((4, 16, cols), BF16),
            pltpu.VMEM((4, 16, cols), BF16),
            pltpu.VMEM((2, 2, 4, 16, cols), BF16),
            pltpu.VMEM((3, wide, 256), BF16),
            pltpu.VMEM((256, depth), F32),
            pltpu.VMEM((256, depth), BF16),
            pltpu.VMEM((8, 32, depth), BF16),
            pltpu.SemaphoreType.DMA((messages,)),
            pltpu.SemaphoreType.DMA((messages,)),
            pltpu.SemaphoreType.DMA((5,)),
            pltpu.SemaphoreType.DMA((1 + n,)),
        ],
        compiler_params=pltpu.CompilerParams(
            collective_id=0, has_side_effects=True, vmem_limit_bytes=50 * 1024 * 1024
        ),
        cost_estimate=pl.CostEstimate(
            flops=10 * 256 * depth * width, bytes_accessed=6 * depth * width + 6 * 256 * width,
            transcendentals=0,
        ),
        name="exchange",
    )(tokens, out_grad, token_weight.reshape(1, 256), gate_weight, up_weight, down_weight)


def grads_kernel(r, ab, gate_grad, up_grad, down_grad):
    for part, out in ((1, gate_grad), (2, up_grad), (0, down_grad)):
        out[...] = jnp.dot(
            r[part], ab[0 if part else 1], preferred_element_type=F32
        ).astype(BF16)


def grads(r, ab, width):
    depth = ab.shape[2]
    step = 528
    out = pl.BlockSpec((step, depth), lambda i: (i, 0))
    return pl.pallas_call(
        grads_kernel,
        grid=(pl.cdiv(width, step),),
        in_specs=[
            pl.BlockSpec((3, step, 256), lambda i: (0, i, 0)),
            pl.BlockSpec((2, 256, depth), lambda i: (0, 0, 0)),
        ],
        out_specs=(out, out, out),
        out_shape=(jax.ShapeDtypeStruct((width, depth), BF16),) * 3,
        compiler_params=pltpu.CompilerParams(vmem_limit_bytes=16 * 1024 * 1024),
        name="grads",
    )(r, ab)


def body(tokens, out_grad, token_weight, gate_weight, up_weight, down_weight):
    width = gate_weight.shape[1]
    r, ab, input_grad = exchange(
        tokens, out_grad, token_weight, gate_weight.T, up_weight.T, down_weight
    )
    gate_grad, up_grad, down_grad = grads(r, ab, width)
    return input_grad, gate_grad.T, up_grad.T, down_grad


def solution(mesh):
    return jax.shard_map(
        body,
        mesh=mesh,
        in_specs=(
            P("col", "row"),
            P("col", "row"),
            P(),
            P("row", "col"),
            P("row", "col"),
            P("col", "row"),
        ),
        out_specs=(P("col", "row"), P("row", "col"), P("row", "col"), P("col", "row")),
        check_vma=False,
    )
```

```python
import functools

import jax
import jax.numpy as jnp
from jax import lax
from jax.experimental import pallas as pl
from jax.experimental.pallas import tpu as pltpu
from jax.sharding import PartitionSpec as P

BF16, F32 = jnp.bfloat16, jnp.float32
MESH = pl.DeviceIdType.MESH
LANE = 128
TILES = (3, 3, 4, 4, 2, 5, 4, 4)
REDUCE = ["zx", "zx", "xz", "zx", "xz", "zx", "zx", "xz"]
GATHER = ["xz", "xz", "zx", "zx", "xz", "xz", "zx", "xz"]
ORDER = (
    (0, 0), (0, 1), (0, 2), (0, 3), (0, 4), (1, 0), (0, 5), (1, 1), (0, 6), (2, 0), (1, 2), (2, 1),
    (1, 3), (1, 4), (0, 7), (3, 0), (1, 5), (3, 1), (1, 6), (2, 3), (2, 2), (1, 7), (2, 5), (4, 0),
    (2, 4), (4, 1), (3, 3), (3, 2), (2, 6), (3, 5), (3, 4), (2, 7), (5, 0), (4, 2), (5, 1), (4, 3),
    (3, 6), (4, 4), (4, 5), (3, 7), (6, 0), (5, 2), (4, 6), (5, 4), (6, 1), (5, 5), (5, 3), (4, 7),
    (7, 0), (6, 2), (5, 6), (8, 0), (6, 4), (7, 1), (5, 7), (7, 2), (8, 1), (6, 5), (6, 3), (6, 6),
    (7, 4), (8, 2), (7, 3), (6, 7), (8, 4), (7, 6), (7, 5), (8, 3), (7, 7), (8, 6), (8, 5), (8, 7),
)
NT = (((1,), (1,)), ((), ()))


def chunks_of(width):
    assert sum(TILES) == pl.cdiv(width, LANE)
    out, at = [], 0
    for t in TILES:
        out.append((at * LANE, t * LANE, min(t * LANE, width - at * LANE)))
        at += t
    return out


(
    PAIR, ZA, ZB, ZUP, ZDOWN, X1, GUP, GDOWN, FUP, FDOWN, XA, XB, XC, XD, CA, CB, CC, CD,
) = range(18)
PER_CHUNK = 18
STEPS = ((1, 0), (3, 0), (0, 1), (2, 0), (1, 1), (3, 1), (2, 1))
COLS = 9


def exchange_kernel(
    width,
    tok, og, tw, wg_h, wu_h, wd_h,
    r_out, ab_out, ig_own, *rest,
):
    ig_send = rest[:7]
    (
        wg, wu, wd, ab, pf, pr, zs1, zr1, zs2, zr2, own, xs, xr, res, rt, ig,
        ssem, rsem, lsem, osem,
    ) = rest[7:]
    chunks = chunks_of(width)
    n = len(chunks)
    row, k = lax.axis_index("row"), lax.axis_index("col")
    x, z, c = row // 8, (row // 2) % 4, row % 2
    y, h = k // 2, k % 2
    zp, zm, zo = (z + 1) % 4, (z + 3) % 4, (z + 2) % 4
    yp, ym, yo = (y + 1) % 4, (y + 3) % 4, (y + 2) % 4

    def rdev(xx, zz, cc):
        return (xx * 8 + zz * 2 + cc, k)

    def cdev(yy, hh):
        return (row, yy * 2 + hh)

    sib, xn = rdev(x, z, 1 - c), rdev(1 - x, z, c)
    up, down = rdev(x, zp, c), rdev(x, zm, c)

    sent = []

    def send(src, dst, idx, dev):
        copy = pltpu.make_async_remote_copy(
            src_ref=src, dst_ref=dst, send_sem=ssem.at[idx], recv_sem=rsem.at[idx],
            device_id=dev, device_id_type=MESH,
        )
        copy.start()
        sent.append(copy)

    def landed(ref, idx):
        pltpu.make_async_remote_copy(
            src_ref=ref, dst_ref=ref, send_sem=ssem.at[idx], recv_sem=rsem.at[idx],
            device_id=sib, device_id_type=MESH,
        ).wait_recv()

    mine = pl.ds(pl.multiple_of(k * 32, 32), 32)
    first = [
        pltpu.make_async_copy(tok, ab.at[0, mine], lsem.at[0]),
        pltpu.make_async_copy(og, ab.at[1, mine], lsem.at[1]),
    ]
    weights = [
        pltpu.make_async_copy(wg_h, wg, lsem.at[2]),
        pltpu.make_async_copy(wu_h, wu, lsem.at[3]),
        pltpu.make_async_copy(wd_h, wd, lsem.at[4]),
    ]
    for copy in first + weights:
        copy.start()

    barrier = pltpu.get_barrier_semaphore()
    greeted = [sib, xn, up, down, cdev(yp, h), cdev(ym, h), cdev(y, 1 - h)]
    for dev in greeted:
        pl.semaphore_signal(barrier, inc=1, device_id=dev, device_id_type=MESH)
    for copy in first:
        copy.wait()
    pl.semaphore_wait(barrier, len(greeted))

    base = n * PER_CHUNK

    def block(yy, hh):
        return pl.ds(pl.multiple_of((yy * 2 + hh) * 32, 32), 32)

    def both(yy, hh):
        return ab.at[:, block(yy, hh)]

    def one(part, yy, hh):
        return ab.at[part, block(yy, hh)]

    me = both(y, h)
    send(me, me, base + 2, cdev(y, 1 - h))
    send(me, me, base + 0, cdev(yp, h))
    send(me, me, base + 1, cdev(ym, h))
    landed(both(ym, h), base + 0)
    send(one(0, ym, h), one(0, ym, h), base + 5, cdev(yp, h))
    landed(both(yp, h), base + 1)
    send(one(1, yp, h), one(1, yp, h), base + 6, cdev(ym, h))
    landed(both(y, 1 - h), base + 2)
    send(both(y, 1 - h), both(y, 1 - h), base + 3, cdev(yp, h))
    send(both(y, 1 - h), both(y, 1 - h), base + 4, cdev(ym, h))
    landed(both(ym, 1 - h), base + 3)
    send(one(0, ym, 1 - h), one(0, ym, 1 - h), base + 7, cdev(yp, h))
    landed(both(yp, 1 - h), base + 4)
    send(one(1, yp, 1 - h), one(1, yp, 1 - h), base + 8, cdev(ym, h))
    landed(one(0, yo, h), base + 5)
    landed(one(1, yo, h), base + 6)
    landed(one(0, yo, 1 - h), base + 7)
    landed(one(1, yo, 1 - h), base + 8)
    outs = [pltpu.make_async_copy(ab, ab_out, osem.at[0])]
    outs[0].start()
    for copy in weights:
        copy.wait()

    first_token = c * 128 + x * 64 + z * 16
    lanes = lax.broadcasted_iota(jnp.int32, (16, 256), 1)
    rows = lax.broadcasted_iota(jnp.int32, (16, 256), 0)
    column = jnp.sum(
        jnp.where(lanes == rows + first_token, jnp.broadcast_to(tw[...], (16, 256)), 0.0),
        axis=1, keepdims=True,
    )

    def span(j):
        o, w, _ = chunks[j]
        return slice(3 * o, 3 * o + 3 * w)

    def halves(j):
        o, w, _ = chunks[j]
        cut = 3 * o + (3 * w // LANE // 2) * LANE
        return slice(3 * o, cut), slice(cut, 3 * o + 3 * w)

    def products(j):
        o, w, valid = chunks[j]
        for part in range(3):
            for at in range(0, valid, 256):
                size = min(256, valid - at)
                lo = o + at
                value = lax.dot_general(
                    ab[part // 2], (wg, wu, wd)[part][lo : lo + size, :], NT,
                    preferred_element_type=F32,
                )
                to = 3 * o + part * w + at
                pf[:, :, :, :, to : to + size] = value.reshape(2, 2, 4, 16, size)
            if valid < w:
                pad = slice(3 * o + part * w + valid, 3 * o + part * w + w)
                pf[:, :, :, :, pad] = jnp.zeros((2, 2, 4, 16, w - valid), F32)
        cols = span(j)
        send(
            pf.at[1 - c, :, :, :, cols], pr.at[:, :, :, cols], j * PER_CHUNK + PAIR, sib
        )

    def chip(xx, zz, cols):
        return pf[c, xx, zz, :, cols] + pr[xx, zz, :, cols]

    def chip_sum(xx, zz, cols):
        return chip(xx, zz, cols) + xr[zz, :, cols].astype(F32)

    def zx_far(j):
        m, cols = j * PER_CHUNK, span(j)
        landed(pr.at[:, :, :, cols], m + PAIR)
        zs1[0, :, cols] = chip(0, zo, cols).astype(BF16)
        send(zs1.at[0, :, cols], zr1.at[0, :, cols], m + ZA, up)
        zs1[1, :, cols] = chip(1, zo, cols).astype(BF16)
        send(zs1.at[1, :, cols], zr1.at[1, :, cols], m + ZB, down)

    def zx_near(j):
        m, cols = j * PER_CHUNK, span(j)
        landed(zr1.at[0, :, cols], m + ZA)
        zs2[0, 0, :, cols] = (chip(0, zp, cols) + zr1[0, :, cols].astype(F32)).astype(BF16)
        zs2[0, 1, :, cols] = chip(1, zp, cols).astype(BF16)
        send(zs2.at[0, :, :, cols], zr2.at[0, :, :, cols], m + ZUP, up)
        landed(zr1.at[1, :, cols], m + ZB)
        zs2[1, 0, :, cols] = chip(0, zm, cols).astype(BF16)
        zs2[1, 1, :, cols] = (chip(1, zm, cols) + zr1[1, :, cols].astype(F32)).astype(BF16)
        send(zs2.at[1, :, :, cols], zr2.at[1, :, :, cols], m + ZDOWN, down)

    def zx_cross(j):
        m, cols = j * PER_CHUNK, span(j)
        landed(zr2.at[0, :, :, cols], m + ZUP)
        landed(zr2.at[1, :, :, cols], m + ZDOWN)

        def ring(xx):
            return chip(xx, z, cols) + zr2[0, xx, :, cols].astype(F32) + zr2[1, xx, :, cols].astype(F32)

        xs[0, :, cols] = ring(1 - x).astype(BF16)
        send(xs.at[0, :, cols], xr.at[0, :, cols], m + X1, xn)
        own[:, cols] = ring(x)

    def zx_total(j):
        m, cols = j * PER_CHUNK, span(j)
        landed(xr.at[0, :, cols], m + X1)
        return lambda at: own[:, at] + xr[0, :, at].astype(F32)

    def xz_cross(j):
        m, cols = j * PER_CHUNK, span(j)
        landed(pr.at[:, :, :, cols], m + PAIR)
        xs[:, :, cols] = (pf[c, 1 - x, :, :, cols] + pr[1 - x, :, :, cols]).astype(BF16)
        send(xs.at[:, :, cols], xr.at[:, :, cols], m + X1, xn)

    def xz_far(j):
        m, cols = j * PER_CHUNK, span(j)
        lo, hi = halves(j)
        landed(xr.at[:, :, cols], m + X1)
        zs1[0, :, lo] = chip_sum(x, zo, lo).astype(BF16)
        send(zs1.at[0, :, lo], zr1.at[0, :, lo], m + ZA, up)
        zs1[1, :, hi] = chip_sum(x, zo, hi).astype(BF16)
        send(zs1.at[1, :, hi], zr1.at[1, :, hi], m + ZB, down)

    def xz_near(j):
        m, cols = j * PER_CHUNK, span(j)
        lo, hi = halves(j)
        landed(zr1.at[0, :, lo], m + ZA)
        zs2[0, 0, :, lo] = (chip_sum(x, zp, lo) + zr1[0, :, lo].astype(F32)).astype(BF16)
        zs2[0, 0, :, hi] = chip_sum(x, zp, hi).astype(BF16)
        send(zs2.at[0, 0, :, cols], zr2.at[0, 0, :, cols], m + ZUP, up)
        landed(zr1.at[1, :, hi], m + ZB)
        zs2[1, 0, :, lo] = chip_sum(x, zm, lo).astype(BF16)
        zs2[1, 0, :, hi] = (chip_sum(x, zm, hi) + zr1[1, :, hi].astype(F32)).astype(BF16)
        send(zs2.at[1, 0, :, cols], zr2.at[1, 0, :, cols], m + ZDOWN, down)

    def xz_total(j):
        m, cols = j * PER_CHUNK, span(j)
        landed(zr2.at[0, 0, :, cols], m + ZUP)
        landed(zr2.at[1, 0, :, cols], m + ZDOWN)
        return lambda at: (
            chip_sum(x, z, at) + zr2[0, 0, :, at].astype(F32) + zr2[1, 0, :, at].astype(F32)
        )

    def here(xx, zz, cols):
        return res.at[c, xx, zz, :, cols]

    def push(xx, zz, cols, idx, dev):
        send(here(xx, zz, cols), here(xx, zz, cols), idx, dev)

    def push_pair(zz, cols, idx, dev):
        part = res.at[c, :, zz, :, cols]
        send(part, part, idx, dev)

    def activate(j):
        o, w, _ = chunks[j]
        m, cols = j * PER_CHUNK, span(j)
        total = (xz_total if REDUCE[j] == "xz" else zx_total)(j)

        def place(part):
            return slice(3 * o + part * w, 3 * o + part * w + w)

        gate, linear, back = total(place(0)), total(place(1)), total(place(2))
        sig = jax.nn.sigmoid(gate)
        silu = gate * sig
        scaled = column * back
        for part, value in enumerate((
            column * (silu * linear),
            scaled * linear * sig * (1.0 + gate * (1.0 - sig)),
            scaled * silu,
        )):
            res[c, x, z, :, place(part)] = value.astype(BF16)
        push(x, z, cols, m + XA, xn)
        if GATHER[j] == "zx":
            push(x, z, cols, m + GUP, up)
            push(x, z, cols, m + GDOWN, down)

    def zx_gather_near(j):
        m, cols = j * PER_CHUNK, span(j)
        lo, hi = halves(j)
        landed(here(x, zm, cols), m + GUP)
        push(x, zm, lo, m + FUP, up)
        push(x, zm, cols, m + XB, xn)
        landed(here(x, zp, cols), m + GDOWN)
        push(x, zp, hi, m + FDOWN, down)
        push(x, zp, cols, m + XC, xn)

    def zx_gather_far(j):
        m, cols = j * PER_CHUNK, span(j)
        lo, hi = halves(j)
        landed(here(x, zo, lo), m + FUP)
        landed(here(x, zo, hi), m + FDOWN)
        push(x, zo, cols, m + XD, xn)
        part = res.at[c, x, :, :, cols]
        send(part, part, m + CA, sib)

    def zx_gather_cross(j):
        m, cols = j * PER_CHUNK, span(j)
        landed(here(1 - x, z, cols), m + XA)
        landed(here(1 - x, zm, cols), m + XB)
        landed(here(1 - x, zp, cols), m + XC)
        landed(here(1 - x, zo, cols), m + XD)
        part = res.at[c, 1 - x, :, :, cols]
        send(part, part, m + CB, sib)

    def zx_all(j):
        m, cols = j * PER_CHUNK, span(j)
        landed(res.at[1 - c, x, :, :, cols], m + CA)
        landed(res.at[1 - c, 1 - x, :, :, cols], m + CB)

    def xz_gather_cross(j):
        m, cols = j * PER_CHUNK, span(j)
        landed(here(1 - x, z, cols), m + XA)
        push_pair(z, cols, m + GUP, up)
        push_pair(z, cols, m + GDOWN, down)
        push_pair(z, cols, m + CA, sib)

    def xz_gather_near(j):
        m, cols = j * PER_CHUNK, span(j)
        landed(res.at[c, :, zm, :, cols], m + GUP)
        push(0, zm, cols, m + FUP, up)
        landed(res.at[c, :, zp, :, cols], m + GDOWN)
        push(1, zp, cols, m + FDOWN, down)
        push_pair(zm, cols, m + CB, sib)
        push_pair(zp, cols, m + CC, sib)

    def xz_gather_far(j):
        m, cols = j * PER_CHUNK, span(j)
        landed(here(0, zo, cols), m + FUP)
        landed(here(1, zo, cols), m + FDOWN)
        push_pair(zo, cols, m + CD, sib)

    def xz_all(j):
        m, cols = j * PER_CHUNK, span(j)
        for zz, idx in ((z, CA), (zm, CB), (zp, CC), (zo, CD)):
            landed(res.at[1 - c, :, zz, :, cols], m + idx)

    def finish(j):
        o, w, valid = chunks[j]
        m, cols = j * PER_CHUNK, span(j)
        (zx_all if GATHER[j] == "zx" else xz_all)(j)
        for part, wide in ((1, wg), (2, wu)):
            at = 3 * o + part * w
            piece = res[:, :, :, :, at : at + valid].reshape(256, valid)
            value = jnp.dot(piece, wide[o : o + valid, :], preferred_element_type=F32)
            if j == 0 and part == 1:
                ig[...] = value
            else:
                ig[...] += value
        for part in range(3):
            at = 3 * o + part * w
            rt[part, o : o + w, :] = res[:, :, :, :, at : at + w].reshape(256, w).T
        copy = pltpu.make_async_copy(
            rt.at[:, o : o + w], r_out.at[:, o : o + w], osem.at[1 + j]
        )
        copy.start()
        outs.append(copy)

    reduce = {"zx": (zx_far, zx_near, zx_cross), "xz": (xz_cross, xz_far, xz_near)}
    gather = {
        "zx": (zx_gather_near, zx_gather_far, zx_gather_cross),
        "xz": (xz_gather_cross, xz_gather_near, xz_gather_far),
    }
    for stage, j in ORDER:
        (products, *reduce[REDUCE[j]], activate, *gather[GATHER[j]], finish)[stage](j)

    ig_own[...] = ig[mine, :]
    for share, (dy, dh) in zip(ig_send, STEPS):
        share[...] = ig[block((y + dy) % 4, (h + dh) % 2), :].astype(BF16)

    for copy in sent:
        copy.wait_send()
    for copy in outs:
        copy.wait()


def exchange(tokens, out_grad, token_weight, gate_weight, up_weight, down_weight):
    width, depth = gate_weight.shape
    wide = pl.cdiv(width, LANE) * LANE
    cols = 3 * wide
    n = len(TILES)
    messages = n * PER_CHUNK + COLS
    hbm = pl.BlockSpec(memory_space=pl.ANY)
    vmem = pl.BlockSpec(memory_space=pltpu.VMEM)
    return pl.pallas_call(
        functools.partial(exchange_kernel, width),
        out_shape=(
            pltpu.VMEM((3, wide, 256), BF16),
            pltpu.VMEM((2, 256, depth), BF16),
            jax.ShapeDtypeStruct((32, depth), F32),
            *(jax.ShapeDtypeStruct((32, depth), BF16),) * 7,
        ),
        in_specs=[hbm, hbm, vmem, hbm, hbm, hbm],
        out_specs=(hbm, hbm) + (vmem,) * 8,
        scratch_shapes=[
            pltpu.VMEM((width, depth), BF16),
            pltpu.VMEM((width, depth), BF16),
            pltpu.VMEM((width, depth), BF16),
            pltpu.VMEM((2, 256, depth), BF16),
            pltpu.VMEM((2, 2, 4, 16, cols), F32),
            pltpu.VMEM((2, 4, 16, cols), F32),
            pltpu.VMEM((2, 16, cols), BF16),
            pltpu.VMEM((2, 16, cols), BF16),
            pltpu.VMEM((2, 2, 16, cols), BF16),
            pltpu.VMEM((2, 2, 16, cols), BF16),
            pltpu.VMEM((16, cols), F32),
            pltpu.VMEM((4, 16, cols), BF16),
            pltpu.VMEM((4, 16, cols), BF16),
            pltpu.VMEM((2, 2, 4, 16, cols), BF16),
            pltpu.VMEM((3, wide, 256), BF16),
            pltpu.VMEM((256, depth), F32),
            pltpu.SemaphoreType.DMA((messages,)),
            pltpu.SemaphoreType.DMA((messages,)),
            pltpu.SemaphoreType.DMA((5,)),
            pltpu.SemaphoreType.DMA((1 + n,)),
        ],
        compiler_params=pltpu.CompilerParams(
            collective_id=0, has_side_effects=True, vmem_limit_bytes=50 * 1024 * 1024
        ),
        cost_estimate=pl.CostEstimate(
            flops=10 * 256 * depth * width, bytes_accessed=6 * depth * width + 6 * 256 * width,
            transcendentals=0,
        ),
        name="exchange",
    )(tokens, out_grad, token_weight.reshape(1, 256), gate_weight, up_weight, down_weight)


def grads_kernel(r, ab, gate_grad, up_grad, down_grad):
    for part, out in ((1, gate_grad), (2, up_grad), (0, down_grad)):
        out[...] = jnp.dot(
            r[part], ab[0 if part else 1], preferred_element_type=F32
        ).astype(BF16)


def grads(r, ab, width):
    depth = ab.shape[2]
    step = 528
    out = pl.BlockSpec((step, depth), lambda i: (i, 0))
    return pl.pallas_call(
        grads_kernel,
        grid=(pl.cdiv(width, step),),
        in_specs=[
            pl.BlockSpec((3, step, 256), lambda i: (0, i, 0)),
            pl.BlockSpec((2, 256, depth), lambda i: (0, 0, 0)),
        ],
        out_specs=(out, out, out),
        out_shape=(jax.ShapeDtypeStruct((width, depth), BF16),) * 3,
        compiler_params=pltpu.CompilerParams(vmem_limit_bytes=16 * 1024 * 1024),
        cost_estimate=pl.CostEstimate(
            flops=6 * 256 * depth * width, bytes_accessed=6 * depth * width, transcendentals=0
        ),
        name="grads",
    )(r, ab)


def body(tokens, out_grad, token_weight, gate_weight, up_weight, down_weight):
    width = gate_weight.shape[1]
    r, ab, input_grad, *shares = exchange(
        tokens, out_grad, token_weight, gate_weight.T, up_weight.T, down_weight
    )
    shares = [
        lax.ppermute(
            share, "col",
            [(y * 2 + h, (y + dy) % 4 * 2 + (h + dh) % 2) for y in range(4) for h in range(2)],
        )
        for share, (dy, dh) in zip(shares, STEPS)
    ]
    gate_grad, up_grad, down_grad = grads(r, ab, width)
    for share in shares:
        input_grad = input_grad + share.astype(F32)
    return input_grad, gate_grad.T, up_grad.T, down_grad


def solution(mesh):
    return jax.shard_map(
        body,
        mesh=mesh,
        in_specs=(
            P("col", "row"),
            P("col", "row"),
            P(),
            P("row", "col"),
            P("row", "col"),
            P("col", "row"),
        ),
        out_specs=(P("col", "row"), P("row", "col"), P("row", "col"), P("col", "row")),
        check_vma=False,
    )
```

```python
import functools

import jax
import jax.numpy as jnp
from jax import lax
from jax.experimental import pallas as pl
from jax.experimental.pallas import tpu as pltpu
from jax.sharding import PartitionSpec as P

BF16, F32 = jnp.bfloat16, jnp.float32
MESH = pl.DeviceIdType.MESH
LANE = 128
JOBS = (
    ("E", 4, "xz", "zx"),
    ("E", 5, "zx", "zx"),
    ("L", 4, "zx", "xz"),
    ("L", 5, "zx", "xz"),
    ("T", 3, "zx", "xz"),
    ("T", 1, "xz", "zx"),
    ("T", 2, "zx", "zx"),
    ("T", 3, "zx", "zx"),
    ("T", 2, "zx", "xz"),
)
ORDER = (
    (0, -1), (1, -1), (0, 0), (0, 1), (2, -1), (1, 0), (1, 1), (3, -1), (0, 2), (0, 3), (2, 1),
    (2, 0), (1, 2), (1, 3), (0, 4), (0, 5), (0, 6), (3, 1), (3, 0), (1, 4), (2, 2), (2, 3), (4, 0),
    (4, 1), (2, 4), (3, 2), (1, 5), (1, 6), (0, 7), (3, 3), (0, 8), (5, 0), (4, 2), (5, 1), (2, 5),
    (1, 7), (1, 8), (4, 3), (6, 0), (3, 4), (2, 6), (6, 1), (3, 5), (2, 7), (5, 2), (2, 8), (3, 6),
    (4, 5), (3, 7), (5, 3), (7, 0), (4, 4), (6, 2), (3, 8), (8, 0), (7, 1), (5, 5), (4, 6), (4, 7),
    (6, 3), (5, 4), (4, 8), (8, 1), (7, 2), (6, 5), (5, 6), (5, 7), (5, 8), (7, 3), (8, 2), (7, 5),
    (6, 4), (6, 6), (8, 3), (8, 5), (6, 7), (6, 8), (7, 6), (7, 4), (7, 8), (7, 7), (8, 6), (8, 4),
    (8, 8), (8, 7),
)
NT = (((1,), (1,)), ((), ()))


def places_of(width):
    out, at, pairs, taken = [], 0, 0, 0
    for kind, tiles, _, _ in JOBS:
        size = tiles * LANE
        if kind == "E":
            unit, pairs = pairs, pairs + 2 * size
        elif kind == "L":
            unit, taken = taken, taken + 2 * size
        else:
            assert taken == pairs or taken == 0
            unit = max(pairs, units_end(out))
        out.append((kind, at, unit, size, min(size, width - unit)))
        at += 3 * size
    assert taken == pairs and at == 3 * LANE * pl.cdiv(width, LANE)
    return out


def units_end(places):
    return max((unit + size for kind, _, unit, size, _ in places if kind == "T"), default=0)


(
    PAIR, PB, PC, PD, ZA, ZB, ZUP, ZDOWN, X1,
    GUP, GDOWN, FUP, FDOWN, XA, XB, XC, XD, CA, CB, CC, CD,
) = range(21)
PER_CHUNK = 21
COLS = 9 + 8


def exchange_kernel(
    width,
    tok, og, tw, wg_h, wu_h, wd_h,
    r_out, ab_out, ig_out,
    wg, wu, wd, ab, pf, pr, zs1, zr1, zs2, zr2, own, xs, xr, res, rt, ig, igs, igr,
    ssem, rsem, lsem, osem,
):
    places = places_of(width)
    n = len(places)
    cuts = [unit for kind, _, unit, _, _ in places if kind == "E"]
    cuts += [max(unit + 2 * size for kind, _, unit, size, _ in places if kind == "E"), width]
    row, k = lax.axis_index("row"), lax.axis_index("col")
    x, z, c = row // 8, (row // 2) % 4, row % 2
    y, h = k // 2, k % 2
    zp, zm, zo = (z + 1) % 4, (z + 3) % 4, (z + 2) % 4
    yp, ym, yo = (y + 1) % 4, (y + 3) % 4, (y + 2) % 4

    def rdev(xx, zz, cc):
        return (xx * 8 + zz * 2 + cc, k)

    def cdev(yy, hh):
        return (row, yy * 2 + hh)

    sib, xn = rdev(x, z, 1 - c), rdev(1 - x, z, c)
    up, down = rdev(x, zp, c), rdev(x, zm, c)

    def owner(slot):
        return ((y, h), (ym, h), (yp, h), (y, 1 - h), (ym, 1 - h), (yp, 1 - h), (yo, h), (yo, 1 - h))[slot]

    sent = []

    def send(src, dst, idx, dev):
        copy = pltpu.make_async_remote_copy(
            src_ref=src, dst_ref=dst, send_sem=ssem.at[idx], recv_sem=rsem.at[idx],
            device_id=dev, device_id_type=MESH,
        )
        copy.start()
        sent.append(copy)

    def landed(ref, idx):
        pltpu.make_async_remote_copy(
            src_ref=ref, dst_ref=ref, send_sem=ssem.at[idx], recv_sem=rsem.at[idx],
            device_id=sib, device_id_type=MESH,
        ).wait_recv()

    first = [
        pltpu.make_async_copy(tok, ab.at[0, :32], lsem.at[0]),
        pltpu.make_async_copy(og, ab.at[1, :32], lsem.at[1]),
    ]
    weights = [
        [
            pltpu.make_async_copy(src.at[rows], dst.at[rows], lsem.at[2 + 3 * i + w])
            for w, (src, dst) in enumerate(((wg_h, wg), (wu_h, wu), (wd_h, wd)))
        ]
        for i, rows in enumerate(pl.ds(a, b - a) for a, b in zip(cuts, cuts[1:]))
    ]
    for copy in first + sum(weights, []):
        copy.start()

    barrier = pltpu.get_barrier_semaphore()
    greeted = [sib, xn, up, down]
    for slot in range(1, 8):
        greeted.append(cdev(*owner(slot)))
    for dev in greeted:
        pl.semaphore_signal(barrier, inc=1, device_id=dev, device_id_type=MESH)
    ig[...] = jnp.zeros_like(ig)
    for copy in first:
        copy.wait()
    pl.semaphore_wait(barrier, len(greeted))

    base = n * PER_CHUNK

    def both(slot):
        return ab.at[:, slot * 32 : slot * 32 + 32]

    def one(part, slot):
        return ab.at[part, slot * 32 : slot * 32 + 32]

    send(both(0), both(3), base + 2, cdev(y, 1 - h))
    send(both(0), both(1), base + 0, cdev(yp, h))
    send(both(0), both(2), base + 1, cdev(ym, h))

    def col_near():
        landed(both(1), base + 0)
        send(one(0, 1), one(0, 6), base + 5, cdev(yp, h))
        landed(both(2), base + 1)
        send(one(1, 2), one(1, 6), base + 6, cdev(ym, h))

    def col_cross():
        landed(both(3), base + 2)
        send(both(3), both(4), base + 3, cdev(yp, h))
        send(both(3), both(5), base + 4, cdev(ym, h))

    def col_next():
        landed(both(4), base + 3)
        send(one(0, 4), one(0, 7), base + 7, cdev(yp, h))
        landed(both(5), base + 4)
        send(one(1, 5), one(1, 7), base + 8, cdev(ym, h))

    outs = []

    def col_far():
        landed(one(0, 6), base + 5)
        landed(one(1, 6), base + 6)
        landed(one(0, 7), base + 7)
        landed(one(1, 7), base + 8)
        copy = pltpu.make_async_copy(ab, ab_out, osem.at[0])
        copy.start()
        outs.append(copy)

    def column_of(half):
        lanes = lax.broadcasted_iota(jnp.int32, (16, 256), 1)
        rows = lax.broadcasted_iota(jnp.int32, (16, 256), 0)
        place, among = x * 2 + z // 2, 0
        for i in range(4):
            yy, hh = owner(4 * half + i)
            among = among + jnp.where(place == i, (yy * 2 + hh) * 32, 0)
        at = rows + (among + (z % 2) * 16)
        return jnp.sum(
            jnp.where(lanes == at, jnp.broadcast_to(tw[...], (16, 256)), 0.0), axis=1, keepdims=True
        )

    columns = {"E": column_of(0), "L": column_of(1)}
    columns["T"] = jnp.where(c == 0, columns["E"], columns["L"])

    def span(j):
        _, at, _, size, _ = places[j]
        return slice(at, at + 3 * size)

    def halves(j):
        _, at, _, size, _ = places[j]
        cut = at + (3 * size // LANE // 2) * LANE
        return slice(at, cut), slice(cut, at + 3 * size)

    def products(j):
        kind, base_at, unit, size, valid = places[j]
        m, cols = j * PER_CHUNK, span(j)
        for group in weights[: j + 1 if kind == "E" else None]:
            while group:
                group.pop(0).wait()
        rows = {"E": slice(0, 128), "L": slice(128, 256), "T": slice(0, 256)}[kind]
        for part in range(3):
            side, wide = ab.at[part // 2], (wg, wu, wd)[part]
            for half in range(1 if kind == "T" else 2):
                for at in range(0, valid, 256):
                    span_ = min(256, valid - at)
                    lo = unit + half * size + at
                    value = lax.dot_general(
                        side[rows, :], wide[lo : lo + span_, :], NT, preferred_element_type=F32
                    )
                    to = base_at + part * size + at
                    if kind == "T":
                        pf[:, :, :, :, to : to + span_] = value.reshape(2, 2, 4, 16, span_)
                    else:
                        pf[half, :, :, :, to : to + span_] = value.reshape(2, 4, 16, span_)
            if valid < size:
                pad = slice(base_at + part * size + valid, base_at + part * size + size)
                pf[:, :, :, :, pad] = jnp.zeros((2, 2, 4, 16, size - valid), F32)
        if JOBS[j][2] == "zx":
            for zz, idx in ((zo, PAIR), (zp, PB), (zm, PC), (z, PD)):
                send(pf.at[1 - c, :, zz, :, cols], pr.at[:, zz, :, cols], m + idx, sib)
        else:
            for xx, idx in ((1 - x, PAIR), (x, PB)):
                send(pf.at[1 - c, xx, :, :, cols], pr.at[xx, :, :, cols], m + idx, sib)

    def chip(xx, zz, cols):
        return pf[c, xx, zz, :, cols] + pr[xx, zz, :, cols]

    def chip_sum(xx, zz, cols):
        return chip(xx, zz, cols) + xr[zz, :, cols].astype(F32)

    def zx_far(j):
        m, cols = j * PER_CHUNK, span(j)
        landed(pr.at[:, zo, :, cols], m + PAIR)
        zs1[0, :, cols] = chip(0, zo, cols).astype(BF16)
        send(zs1.at[0, :, cols], zr1.at[0, :, cols], m + ZA, up)
        zs1[1, :, cols] = chip(1, zo, cols).astype(BF16)
        send(zs1.at[1, :, cols], zr1.at[1, :, cols], m + ZB, down)

    def zx_near(j):
        m, cols = j * PER_CHUNK, span(j)
        landed(pr.at[:, zp, :, cols], m + PB)
        landed(zr1.at[0, :, cols], m + ZA)
        zs2[0, 0, :, cols] = (chip(0, zp, cols) + zr1[0, :, cols].astype(F32)).astype(BF16)
        zs2[0, 1, :, cols] = chip(1, zp, cols).astype(BF16)
        send(zs2.at[0, :, :, cols], zr2.at[0, :, :, cols], m + ZUP, up)
        landed(pr.at[:, zm, :, cols], m + PC)
        landed(zr1.at[1, :, cols], m + ZB)
        zs2[1, 0, :, cols] = chip(0, zm, cols).astype(BF16)
        zs2[1, 1, :, cols] = (chip(1, zm, cols) + zr1[1, :, cols].astype(F32)).astype(BF16)
        send(zs2.at[1, :, :, cols], zr2.at[1, :, :, cols], m + ZDOWN, down)

    def zx_cross(j):
        m, cols = j * PER_CHUNK, span(j)
        landed(pr.at[:, z, :, cols], m + PD)
        landed(zr2.at[0, :, :, cols], m + ZUP)
        landed(zr2.at[1, :, :, cols], m + ZDOWN)

        def ring(xx):
            return chip(xx, z, cols) + zr2[0, xx, :, cols].astype(F32) + zr2[1, xx, :, cols].astype(F32)

        xs[0, :, cols] = ring(1 - x).astype(BF16)
        send(xs.at[0, :, cols], xr.at[0, :, cols], m + X1, xn)
        own[:, cols] = ring(x)

    def zx_total(j):
        m, cols = j * PER_CHUNK, span(j)
        landed(xr.at[0, :, cols], m + X1)
        return lambda at: own[:, at] + xr[0, :, at].astype(F32)

    def xz_cross(j):
        m, cols = j * PER_CHUNK, span(j)
        landed(pr.at[1 - x, :, :, cols], m + PAIR)
        xs[:, :, cols] = (pf[c, 1 - x, :, :, cols] + pr[1 - x, :, :, cols]).astype(BF16)
        send(xs.at[:, :, cols], xr.at[:, :, cols], m + X1, xn)

    def xz_far(j):
        m, cols = j * PER_CHUNK, span(j)
        lo, hi = halves(j)
        landed(pr.at[x, :, :, cols], m + PB)
        landed(xr.at[:, :, cols], m + X1)
        zs1[0, :, lo] = chip_sum(x, zo, lo).astype(BF16)
        send(zs1.at[0, :, lo], zr1.at[0, :, lo], m + ZA, up)
        zs1[1, :, hi] = chip_sum(x, zo, hi).astype(BF16)
        send(zs1.at[1, :, hi], zr1.at[1, :, hi], m + ZB, down)

    def xz_near(j):
        m, cols = j * PER_CHUNK, span(j)
        lo, hi = halves(j)
        landed(zr1.at[0, :, lo], m + ZA)
        zs2[0, 0, :, lo] = (chip_sum(x, zp, lo) + zr1[0, :, lo].astype(F32)).astype(BF16)
        zs2[0, 0, :, hi] = chip_sum(x, zp, hi).astype(BF16)
        send(zs2.at[0, 0, :, cols], zr2.at[0, 0, :, cols], m + ZUP, up)
        landed(zr1.at[1, :, hi], m + ZB)
        zs2[1, 0, :, lo] = chip_sum(x, zm, lo).astype(BF16)
        zs2[1, 0, :, hi] = (chip_sum(x, zm, hi) + zr1[1, :, hi].astype(F32)).astype(BF16)
        send(zs2.at[1, 0, :, cols], zr2.at[1, 0, :, cols], m + ZDOWN, down)

    def xz_total(j):
        m, cols = j * PER_CHUNK, span(j)
        landed(zr2.at[0, 0, :, cols], m + ZUP)
        landed(zr2.at[1, 0, :, cols], m + ZDOWN)
        return lambda at: (
            chip_sum(x, z, at) + zr2[0, 0, :, at].astype(F32) + zr2[1, 0, :, at].astype(F32)
        )

    def here(xx, zz, cols):
        return res.at[c, xx, zz, :, cols]

    def push(xx, zz, cols, idx, dev):
        send(here(xx, zz, cols), here(xx, zz, cols), idx, dev)

    def push_pair(zz, cols, idx, dev):
        part = res.at[c, :, zz, :, cols]
        send(part, part, idx, dev)

    def activate(j):
        kind, base_at, _, size, _ = places[j]
        m, cols = j * PER_CHUNK, span(j)
        total = (xz_total if JOBS[j][2] == "xz" else zx_total)(j)
        column = columns[kind]

        def place(part):
            return slice(base_at + part * size, base_at + part * size + size)

        gate, linear, back = total(place(0)), total(place(1)), total(place(2))
        sig = jax.nn.sigmoid(gate)
        silu = gate * sig
        scaled = column * back
        for part, value in enumerate((
            column * (silu * linear),
            scaled * linear * sig * (1.0 + gate * (1.0 - sig)),
            scaled * silu,
        )):
            res[c, x, z, :, place(part)] = value.astype(BF16)
        push(x, z, cols, m + XA, xn)
        if JOBS[j][3] == "zx":
            push(x, z, cols, m + GUP, up)
            push(x, z, cols, m + GDOWN, down)

    def zx_gather_near(j):
        m, cols = j * PER_CHUNK, span(j)
        lo, hi = halves(j)
        landed(here(x, zm, cols), m + GUP)
        push(x, zm, lo, m + FUP, up)
        push(x, zm, cols, m + XB, xn)
        landed(here(x, zp, cols), m + GDOWN)
        push(x, zp, hi, m + FDOWN, down)
        push(x, zp, cols, m + XC, xn)

    def zx_gather_far(j):
        m, cols = j * PER_CHUNK, span(j)
        lo, hi = halves(j)
        landed(here(x, zo, lo), m + FUP)
        landed(here(x, zo, hi), m + FDOWN)
        push(x, zo, cols, m + XD, xn)
        part = res.at[c, x, :, :, cols]
        send(part, part, m + CA, sib)

    def zx_gather_cross(j):
        m, cols = j * PER_CHUNK, span(j)
        landed(here(1 - x, z, cols), m + XA)
        landed(here(1 - x, zm, cols), m + XB)
        landed(here(1 - x, zp, cols), m + XC)
        landed(here(1 - x, zo, cols), m + XD)
        part = res.at[c, 1 - x, :, :, cols]
        send(part, part, m + CB, sib)

    def zx_all(j):
        m, cols = j * PER_CHUNK, span(j)
        landed(res.at[1 - c, x, :, :, cols], m + CA)
        landed(res.at[1 - c, 1 - x, :, :, cols], m + CB)

    def xz_gather_cross(j):
        m, cols = j * PER_CHUNK, span(j)
        landed(here(1 - x, z, cols), m + XA)
        push_pair(z, cols, m + GUP, up)
        push_pair(z, cols, m + GDOWN, down)
        push_pair(z, cols, m + CA, sib)

    def xz_gather_near(j):
        m, cols = j * PER_CHUNK, span(j)
        landed(res.at[c, :, zm, :, cols], m + GUP)
        push(0, zm, cols, m + FUP, up)
        landed(res.at[c, :, zp, :, cols], m + GDOWN)
        push(1, zp, cols, m + FDOWN, down)
        push_pair(zm, cols, m + CB, sib)
        push_pair(zp, cols, m + CC, sib)

    def xz_gather_far(j):
        m, cols = j * PER_CHUNK, span(j)
        landed(here(0, zo, cols), m + FUP)
        landed(here(1, zo, cols), m + FDOWN)
        push_pair(zo, cols, m + CD, sib)

    def xz_all(j):
        m, cols = j * PER_CHUNK, span(j)
        for zz, idx in ((z, CA), (zm, CB), (zp, CC), (zo, CD)):
            landed(res.at[1 - c, :, zz, :, cols], m + idx)

    def finish(j):
        kind, base_at, unit, size, valid = places[j]
        (zx_all if JOBS[j][3] == "zx" else xz_all)(j)
        if kind == "T":
            pieces = [(slice(0, 256), unit, lambda at: res[:, :, :, :, at].reshape(256, -1))]
            tokens, units = pl.ds(0, 256), pl.ds(unit, size)
        else:
            start = 128 * (kind == "L")
            pieces = [
                (
                    slice(start, start + 128), unit + half * size,
                    lambda at, half=half: res[half, :, :, :, at].reshape(128, -1),
                )
                for half in range(2)
            ]
            tokens, units = pl.ds(start, 128), pl.ds(unit, 2 * size)
        for rows, lo, piece in pieces:
            for part, wide in ((1, wg), (2, wu)):
                at = base_at + part * size
                ig[rows, :] += jnp.dot(
                    piece(slice(at, at + valid)), wide[lo : lo + valid, :],
                    preferred_element_type=F32,
                )
            for part in range(3):
                at = base_at + part * size
                rt[part, lo : lo + size, rows] = piece(slice(at, at + size)).T
        copy = pltpu.make_async_copy(
            rt.at[:, units, tokens], r_out.at[:, units, tokens], osem.at[1 + j]
        )
        copy.start()
        outs.append(copy)

    reduce = {"zx": (zx_far, zx_near, zx_cross), "xz": (xz_cross, xz_far, xz_near)}
    gather = {
        "zx": (zx_gather_near, zx_gather_far, zx_gather_cross),
        "xz": (xz_gather_cross, xz_gather_near, xz_gather_far),
    }
    col = (col_near, col_cross, col_next, col_far)
    for stage, j in ORDER:
        if j < 0:
            col[stage]()
        else:
            _, _, over, back = JOBS[j]
            (products, *reduce[over], activate, *gather[back], finish)[stage](j)

    igs[...] = ig[...].astype(BF16)
    for slot in range(1, 8):
        send(
            igs.at[slot * 32 : slot * 32 + 32], igr.at[slot], base + 9 + slot, cdev(*owner(slot))
        )
    total = ig[:32, :]
    for slot in range(1, 8):
        landed(igr.at[slot], base + 9 + slot)
        total = total + igr[slot].astype(F32)
    ig_out[...] = total

    for copy in sent:
        copy.wait_send()
    for copy in outs:
        copy.wait()


def exchange(tokens, out_grad, token_weight, gate_weight, up_weight, down_weight):
    width, depth = gate_weight.shape
    wide = pl.cdiv(width, LANE) * LANE
    cols = 3 * wide
    n = len(JOBS)
    messages = n * PER_CHUNK + COLS
    hbm = pl.BlockSpec(memory_space=pl.ANY)
    vmem = pl.BlockSpec(memory_space=pltpu.VMEM)
    return pl.pallas_call(
        functools.partial(exchange_kernel, width),
        out_shape=(
            pltpu.VMEM((3, wide, 256), BF16),
            pltpu.VMEM((2, 256, depth), BF16),
            jax.ShapeDtypeStruct((32, depth), F32),
        ),
        in_specs=[hbm, hbm, vmem, hbm, hbm, hbm],
        out_specs=(hbm, hbm, vmem),
        scratch_shapes=[
            pltpu.VMEM((width, depth), BF16),
            pltpu.VMEM((width, depth), BF16),
            pltpu.VMEM((width, depth), BF16),
            pltpu.VMEM((2, 256, depth), BF16),
            pltpu.VMEM((2, 2, 4, 16, cols), F32),
            pltpu.VMEM((2, 4, 16, cols), F32),
            pltpu.VMEM((2, 16, cols), BF16),
            pltpu.VMEM((2, 16, cols), BF16),
            pltpu.VMEM((2, 2, 16, cols), BF16),
            pltpu.VMEM((2, 2, 16, cols), BF16),
            pltpu.VMEM((16, cols), F32),
            pltpu.VMEM((4, 16, cols), BF16),
            pltpu.VMEM((4, 16, cols), BF16),
            pltpu.VMEM((2, 2, 4, 16, cols), BF16),
            pltpu.VMEM((3, wide, 256), BF16),
            pltpu.VMEM((256, depth), F32),
            pltpu.VMEM((256, depth), BF16),
            pltpu.VMEM((8, 32, depth), BF16),
            pltpu.SemaphoreType.DMA((messages,)),
            pltpu.SemaphoreType.DMA((messages,)),
            pltpu.SemaphoreType.DMA((2 + 3 * n,)),
            pltpu.SemaphoreType.DMA((1 + n,)),
        ],
        compiler_params=pltpu.CompilerParams(
            collective_id=0, has_side_effects=True, vmem_limit_bytes=50 * 1024 * 1024
        ),
        cost_estimate=pl.CostEstimate(
            flops=10 * 256 * depth * width, bytes_accessed=6 * depth * width + 6 * 256 * width,
            transcendentals=0,
        ),
        name="exchange",
    )(tokens, out_grad, token_weight.reshape(1, 256), gate_weight, up_weight, down_weight)


def grads_kernel(r, ab, gate_grad, up_grad, down_grad):
    for part, out in ((1, gate_grad), (2, up_grad), (0, down_grad)):
        out[...] = jnp.dot(
            r[part], ab[0 if part else 1], preferred_element_type=F32
        ).astype(BF16)


def grads(r, ab, width):
    depth = ab.shape[2]
    step = 528
    out = pl.BlockSpec((step, depth), lambda i: (i, 0))
    return pl.pallas_call(
        grads_kernel,
        grid=(pl.cdiv(width, step),),
        in_specs=[
            pl.BlockSpec((3, step, 256), lambda i: (0, i, 0)),
            pl.BlockSpec((2, 256, depth), lambda i: (0, 0, 0)),
        ],
        out_specs=(out, out, out),
        out_shape=(jax.ShapeDtypeStruct((width, depth), BF16),) * 3,
        compiler_params=pltpu.CompilerParams(vmem_limit_bytes=16 * 1024 * 1024),
        name="grads",
    )(r, ab)


def body(tokens, out_grad, token_weight, gate_weight, up_weight, down_weight):
    width = gate_weight.shape[1]
    r, ab, input_grad = exchange(
        tokens, out_grad, token_weight, gate_weight.T, up_weight.T, down_weight
    )
    gate_grad, up_grad, down_grad = grads(r, ab, width)
    return input_grad, gate_grad.T, up_grad.T, down_grad


def solution(mesh):
    return jax.shard_map(
        body,
        mesh=mesh,
        in_specs=(
            P("col", "row"),
            P("col", "row"),
            P(),
            P("row", "col"),
            P("row", "col"),
            P("col", "row"),
        ),
        out_specs=(P("col", "row"), P("row", "col"), P("row", "col"), P("col", "row")),
        check_vma=False,
    )
```

```python
import functools

import jax
import jax.numpy as jnp
from jax import lax
from jax.experimental import pallas as pl
from jax.experimental.pallas import tpu as pltpu
from jax.sharding import PartitionSpec as P

BF16, F32 = jnp.bfloat16, jnp.float32
MESH = pl.DeviceIdType.MESH
LANE = 128
JOBS = (
    ("E", 4, "zx", "zx"),
    ("L", 4, "xz", "zx"),
    ("T", 4, "zx", "xz"),
    ("T", 3, "zx", "xz"),
    ("T", 4, "xz", "zx"),
    ("T", 3, "zx", "xz"),
    ("T", 3, "zx", "xz"),
    ("T", 2, "xz", "zx"),
    ("T", 2, "zx", "zx"),
)
ORDER = (
    (0, -1), (1, -1), (0, 0), (1, 0), (2, -1), (2, 0), (3, -1), (0, 1), (1, 1), (3, 0), (0, 2),
    (1, 2), (0, 3), (1, 3), (2, 1), (0, 4), (2, 2), (4, 0), (1, 4), (0, 5), (2, 3), (1, 5), (0, 6),
    (3, 2), (2, 4), (1, 6), (3, 1), (3, 3), (5, 0), (2, 5), (0, 7), (2, 6), (1, 7), (4, 2), (0, 8),
    (4, 1), (1, 8), (4, 3), (2, 7), (3, 4), (6, 0), (2, 8), (3, 5), (5, 2), (3, 6), (5, 1), (5, 3),
    (7, 0), (4, 4), (3, 8), (3, 7), (4, 5), (4, 6), (6, 2), (6, 1), (6, 3), (5, 4), (8, 0), (4, 7),
    (4, 8), (5, 5), (5, 6), (7, 2), (9, 0), (7, 1), (10, 0), (7, 3), (6, 4), (5, 8), (6, 5), (5, 7),
    (8, 2), (6, 6), (8, 1), (8, 3), (7, 4), (6, 8), (9, 2), (10, 2), (7, 5), (9, 1), (9, 3), (6, 7),
    (10, 1), (8, 4), (7, 6), (7, 8), (10, 3), (8, 5), (7, 7), (9, 4), (8, 6), (8, 8), (10, 4),
    (9, 5), (10, 5), (8, 7), (9, 6), (9, 8), (10, 6), (10, 8), (9, 7), (4, -1), (10, 7),
)
NT = (((1,), (1,)), ((), ()))


def places_of(width):
    out, at, pairs, taken = [], 0, 0, 0
    for kind, tiles, _, _ in JOBS:
        size = tiles * LANE
        if kind == "E":
            unit, pairs = pairs, pairs + 2 * size
        elif kind == "L":
            unit, taken = taken, taken + 2 * size
        else:
            assert taken == pairs or taken == 0
            unit = max(pairs, units_end(out))
        out.append((kind, at, unit, size, min(size, width - unit)))
        at += 3 * size
    assert taken == pairs and at == 3 * LANE * pl.cdiv(width, LANE)
    return out


def units_end(places):
    return max((unit + size for kind, _, unit, size, _ in places if kind == "T"), default=0)


(
    PAIR, PB, PC, PD, ZA, ZB, ZUP, ZDOWN, X1,
    GUP, GDOWN, FUP, FDOWN, XA, XB, XC, XD, CA, CB, CC, CD,
) = range(21)
PER_CHUNK = 21
COLS = 9 + 8


def exchange_kernel(
    width,
    tok, og, tw, wg_h, wu_h, wd_h,
    r_out, ab_out, ig_out,
    wgu, wd, ab, pf, pr, zs1, zr1, zs2, zr2, own, xs, xr, res, rt, ig, igs, igr,
    ssem, rsem, lsem, osem,
):
    places = places_of(width)
    n = len(places)
    row, k = lax.axis_index("row"), lax.axis_index("col")
    x, z, c = row // 8, (row // 2) % 4, row % 2
    y, h = k // 2, k % 2
    zp, zm, zo = (z + 1) % 4, (z + 3) % 4, (z + 2) % 4
    yp, ym, yo = (y + 1) % 4, (y + 3) % 4, (y + 2) % 4

    def rdev(xx, zz, cc):
        return (xx * 8 + zz * 2 + cc, k)

    def cdev(yy, hh):
        return (row, yy * 2 + hh)

    sib, xn = rdev(x, z, 1 - c), rdev(1 - x, z, c)
    up, down = rdev(x, zp, c), rdev(x, zm, c)

    def owner(slot):
        return ((y, h), (ym, h), (yp, h), (y, 1 - h), (ym, 1 - h), (yp, 1 - h), (yo, h), (yo, 1 - h))[slot]

    sent = []

    def send(src, dst, idx, dev):
        copy = pltpu.make_async_remote_copy(
            src_ref=src, dst_ref=dst, send_sem=ssem.at[idx], recv_sem=rsem.at[idx],
            device_id=dev, device_id_type=MESH,
        )
        copy.start()
        sent.append(copy)

    def landed(ref, idx):
        pltpu.make_async_remote_copy(
            src_ref=ref, dst_ref=ref, send_sem=ssem.at[idx], recv_sem=rsem.at[idx],
            device_id=sib, device_id_type=MESH,
        ).wait_recv()

    first = [
        pltpu.make_async_copy(tok, ab.at[0, :32], lsem.at[0]),
        pltpu.make_async_copy(og, ab.at[1, :32], lsem.at[1]),
    ]
    weights = [[] for _ in places]
    for j, (kind, _, unit, size, valid) in enumerate(places):
        if kind == "L":
            continue
        for lo in (unit,) if kind == "T" else (unit, unit + size):
            for src, dst, to in (
                (wg_h, wgu, 2 * lo), (wu_h, wgu, 2 * lo + size), (wd_h, wd, lo)
            ):
                weights[j].append(pltpu.make_async_copy(
                    src.at[pl.ds(lo, valid)], dst.at[pl.ds(to, valid)],
                    lsem.at[2 + 6 * j + len(weights[j])],
                ))
                if valid < size:
                    dst[to + valid : to + size, :] = jnp.zeros((size - valid, dst.shape[1]), BF16)
    for copy in first + sum(weights, []):
        copy.start()

    barrier = pltpu.get_barrier_semaphore()
    greeted = [sib, xn, up, down]
    for slot in range(1, 8):
        greeted.append(cdev(*owner(slot)))
    for dev in greeted:
        pl.semaphore_signal(barrier, inc=1, device_id=dev, device_id_type=MESH)
    ig[...] = jnp.zeros_like(ig)
    for copy in first:
        copy.wait()
    pl.semaphore_wait(barrier, len(greeted))

    base = n * PER_CHUNK

    def both(slot):
        return ab.at[:, slot * 32 : slot * 32 + 32]

    def one(part, slot):
        return ab.at[part, slot * 32 : slot * 32 + 32]

    send(both(0), both(3), base + 2, cdev(y, 1 - h))
    send(both(0), both(1), base + 0, cdev(yp, h))
    send(both(0), both(2), base + 1, cdev(ym, h))

    def col_near():
        landed(both(1), base + 0)
        send(one(0, 1), one(0, 6), base + 5, cdev(yp, h))
        landed(both(2), base + 1)
        send(one(1, 2), one(1, 6), base + 6, cdev(ym, h))

    def col_cross():
        landed(both(3), base + 2)
        send(both(3), both(4), base + 3, cdev(yp, h))
        send(both(3), both(5), base + 4, cdev(ym, h))

    def col_next():
        landed(both(4), base + 3)
        send(one(0, 4), one(0, 7), base + 7, cdev(yp, h))
        landed(both(5), base + 4)
        send(one(1, 5), one(1, 7), base + 8, cdev(ym, h))

    outs = []

    def col_far():
        landed(one(0, 6), base + 5)
        landed(one(1, 6), base + 6)
        landed(one(0, 7), base + 7)
        landed(one(1, 7), base + 8)
        copy = pltpu.make_async_copy(ab, ab_out, osem.at[0])
        copy.start()
        outs.append(copy)

    def column_of(half):
        lanes = lax.broadcasted_iota(jnp.int32, (16, 256), 1)
        rows = lax.broadcasted_iota(jnp.int32, (16, 256), 0)
        place, among = x * 2 + z // 2, 0
        for i in range(4):
            yy, hh = owner(4 * half + i)
            among = among + jnp.where(place == i, (yy * 2 + hh) * 32, 0)
        at = rows + (among + (z % 2) * 16)
        return jnp.sum(
            jnp.where(lanes == at, jnp.broadcast_to(tw[...], (16, 256)), 0.0), axis=1, keepdims=True
        )

    columns = {"E": column_of(0), "L": column_of(1)}
    columns["T"] = jnp.where(c == 0, columns["E"], columns["L"])

    def span(j):
        _, at, _, size, _ = places[j]
        return slice(at, at + 3 * size)

    def halves(j):
        _, at, _, size, _ = places[j]
        cut = at + (3 * size // LANE // 2) * LANE
        return slice(at, cut), slice(cut, at + 3 * size)

    def multiply(j, side, wide, first, count, to):
        kind, _, unit, size, _ = places[j]
        rows = {"E": slice(0, 128), "L": slice(128, 256), "T": slice(0, 256)}[kind]

        def block(half, lo, at, width):
            value = lax.dot_general(
                ab[side, rows, :], wide[pl.ds(lo, width), :], NT, preferred_element_type=F32
            )
            if kind == "T":
                pf[:, :, :, :, pl.ds(at, width)] = value.reshape(2, 2, 4, 16, width)
            else:
                pf[half, :, :, :, pl.ds(at, width)] = value.reshape(2, 4, 16, width)

        for half in range(1 if kind == "T" else 2):
            lo = first + half * count

            @pl.loop(0, count // 256)
            def _(i):
                block(half, pl.multiple_of(lo + i * 256, 128), pl.multiple_of(to + i * 256, 128), 256)

            if count % 256:
                block(half, lo + count - 128, to + count - 128, 128)

    def products(j):
        kind, base_at, unit, size, _ = places[j]
        for copy in weights[j]:
            copy.wait()
        multiply(j, 0, wgu, 2 * unit, 2 * size, base_at)

    def back_products(j):
        _, base_at, unit, size, _ = places[j]
        m, cols = j * PER_CHUNK, span(j)
        multiply(j, 1, wd, unit, size, base_at + 2 * size)
        if JOBS[j][2] == "zx":
            for zz, idx in ((zo, PAIR), (zp, PB), (zm, PC), (z, PD)):
                send(pf.at[1 - c, :, zz, :, cols], pr.at[:, zz, :, cols], m + idx, sib)
        else:
            for xx, idx in ((1 - x, PAIR), (x, PB)):
                send(pf.at[1 - c, xx, :, :, cols], pr.at[xx, :, :, cols], m + idx, sib)

    def chip(xx, zz, cols):
        return pf[c, xx, zz, :, cols] + pr[xx, zz, :, cols]

    def chip_sum(xx, zz, cols):
        return chip(xx, zz, cols) + xr[zz, :, cols].astype(F32)

    def zx_far(j):
        m, cols = j * PER_CHUNK, span(j)
        landed(pr.at[:, zo, :, cols], m + PAIR)
        zs1[0, :, cols] = chip(0, zo, cols).astype(BF16)
        send(zs1.at[0, :, cols], zr1.at[0, :, cols], m + ZA, up)
        zs1[1, :, cols] = chip(1, zo, cols).astype(BF16)
        send(zs1.at[1, :, cols], zr1.at[1, :, cols], m + ZB, down)

    def zx_near(j):
        m, cols = j * PER_CHUNK, span(j)
        landed(pr.at[:, zp, :, cols], m + PB)
        landed(zr1.at[0, :, cols], m + ZA)
        zs2[0, 0, :, cols] = (chip(0, zp, cols) + zr1[0, :, cols].astype(F32)).astype(BF16)
        zs2[0, 1, :, cols] = chip(1, zp, cols).astype(BF16)
        send(zs2.at[0, :, :, cols], zr2.at[0, :, :, cols], m + ZUP, up)
        landed(pr.at[:, zm, :, cols], m + PC)
        landed(zr1.at[1, :, cols], m + ZB)
        zs2[1, 0, :, cols] = chip(0, zm, cols).astype(BF16)
        zs2[1, 1, :, cols] = (chip(1, zm, cols) + zr1[1, :, cols].astype(F32)).astype(BF16)
        send(zs2.at[1, :, :, cols], zr2.at[1, :, :, cols], m + ZDOWN, down)

    def zx_cross(j):
        m, cols = j * PER_CHUNK, span(j)
        landed(pr.at[:, z, :, cols], m + PD)
        landed(zr2.at[0, :, :, cols], m + ZUP)
        landed(zr2.at[1, :, :, cols], m + ZDOWN)

        def ring(xx):
            return chip(xx, z, cols) + zr2[0, xx, :, cols].astype(F32) + zr2[1, xx, :, cols].astype(F32)

        xs[0, :, cols] = ring(1 - x).astype(BF16)
        send(xs.at[0, :, cols], xr.at[0, :, cols], m + X1, xn)
        own[:, cols] = ring(x)

    def zx_total(j):
        m, cols = j * PER_CHUNK, span(j)
        landed(xr.at[0, :, cols], m + X1)
        return lambda at: own[:, at] + xr[0, :, at].astype(F32)

    def xz_cross(j):
        m, cols = j * PER_CHUNK, span(j)
        landed(pr.at[1 - x, :, :, cols], m + PAIR)
        xs[:, :, cols] = (pf[c, 1 - x, :, :, cols] + pr[1 - x, :, :, cols]).astype(BF16)
        send(xs.at[:, :, cols], xr.at[:, :, cols], m + X1, xn)

    def xz_far(j):
        m, cols = j * PER_CHUNK, span(j)
        lo, hi = halves(j)
        landed(pr.at[x, :, :, cols], m + PB)
        landed(xr.at[:, :, cols], m + X1)
        zs1[0, :, lo] = chip_sum(x, zo, lo).astype(BF16)
        send(zs1.at[0, :, lo], zr1.at[0, :, lo], m + ZA, up)
        zs1[1, :, hi] = chip_sum(x, zo, hi).astype(BF16)
        send(zs1.at[1, :, hi], zr1.at[1, :, hi], m + ZB, down)

    def xz_near(j):
        m, cols = j * PER_CHUNK, span(j)
        lo, hi = halves(j)
        landed(zr1.at[0, :, lo], m + ZA)
        zs2[0, 0, :, lo] = (chip_sum(x, zp, lo) + zr1[0, :, lo].astype(F32)).astype(BF16)
        zs2[0, 0, :, hi] = chip_sum(x, zp, hi).astype(BF16)
        send(zs2.at[0, 0, :, cols], zr2.at[0, 0, :, cols], m + ZUP, up)
        landed(zr1.at[1, :, hi], m + ZB)
        zs2[1, 0, :, lo] = chip_sum(x, zm, lo).astype(BF16)
        zs2[1, 0, :, hi] = (chip_sum(x, zm, hi) + zr1[1, :, hi].astype(F32)).astype(BF16)
        send(zs2.at[1, 0, :, cols], zr2.at[1, 0, :, cols], m + ZDOWN, down)

    def xz_total(j):
        m, cols = j * PER_CHUNK, span(j)
        landed(zr2.at[0, 0, :, cols], m + ZUP)
        landed(zr2.at[1, 0, :, cols], m + ZDOWN)
        return lambda at: (
            chip_sum(x, z, at) + zr2[0, 0, :, at].astype(F32) + zr2[1, 0, :, at].astype(F32)
        )

    def here(xx, zz, cols):
        return res.at[c, xx, zz, :, cols]

    def push(xx, zz, cols, idx, dev):
        send(here(xx, zz, cols), here(xx, zz, cols), idx, dev)

    def push_pair(zz, cols, idx, dev):
        part = res.at[c, :, zz, :, cols]
        send(part, part, idx, dev)

    def activate(j):
        kind, base_at, _, size, _ = places[j]
        m, cols = j * PER_CHUNK, span(j)
        total = (xz_total if JOBS[j][2] == "xz" else zx_total)(j)
        column = columns[kind]

        def place(part):
            return slice(base_at + part * size, base_at + part * size + size)

        gate, linear, back = total(place(0)), total(place(1)), total(place(2))
        sig = jax.nn.sigmoid(gate)
        silu = gate * sig
        scaled = column * back
        for part, value in enumerate((
            scaled * linear * sig * (1.0 + gate * (1.0 - sig)),
            scaled * silu,
            column * (silu * linear),
        )):
            res[c, x, z, :, place(part)] = value.astype(BF16)
        push(x, z, cols, m + XA, xn)
        if JOBS[j][3] == "zx":
            push(x, z, cols, m + GUP, up)
            push(x, z, cols, m + GDOWN, down)

    def zx_gather_near(j):
        m, cols = j * PER_CHUNK, span(j)
        lo, hi = halves(j)
        landed(here(x, zm, cols), m + GUP)
        push(x, zm, lo, m + FUP, up)
        push(x, zm, cols, m + XB, xn)
        landed(here(x, zp, cols), m + GDOWN)
        push(x, zp, hi, m + FDOWN, down)
        push(x, zp, cols, m + XC, xn)

    def zx_gather_far(j):
        m, cols = j * PER_CHUNK, span(j)
        lo, hi = halves(j)
        landed(here(x, zo, lo), m + FUP)
        landed(here(x, zo, hi), m + FDOWN)
        push(x, zo, cols, m + XD, xn)
        part = res.at[c, x, :, :, cols]
        send(part, part, m + CA, sib)

    def zx_gather_cross(j):
        m, cols = j * PER_CHUNK, span(j)
        landed(here(1 - x, z, cols), m + XA)
        landed(here(1 - x, zm, cols), m + XB)
        landed(here(1 - x, zp, cols), m + XC)
        landed(here(1 - x, zo, cols), m + XD)
        part = res.at[c, 1 - x, :, :, cols]
        send(part, part, m + CB, sib)

    def zx_all(j):
        m, cols = j * PER_CHUNK, span(j)
        landed(res.at[1 - c, x, :, :, cols], m + CA)
        landed(res.at[1 - c, 1 - x, :, :, cols], m + CB)

    def xz_gather_cross(j):
        m, cols = j * PER_CHUNK, span(j)
        landed(here(1 - x, z, cols), m + XA)
        push_pair(z, cols, m + GUP, up)
        push_pair(z, cols, m + GDOWN, down)
        push_pair(z, cols, m + CA, sib)

    def xz_gather_near(j):
        m, cols = j * PER_CHUNK, span(j)
        landed(res.at[c, :, zm, :, cols], m + GUP)
        push(0, zm, cols, m + FUP, up)
        landed(res.at[c, :, zp, :, cols], m + GDOWN)
        push(1, zp, cols, m + FDOWN, down)
        push_pair(zm, cols, m + CB, sib)
        push_pair(zp, cols, m + CC, sib)

    def xz_gather_far(j):
        m, cols = j * PER_CHUNK, span(j)
        landed(here(0, zo, cols), m + FUP)
        landed(here(1, zo, cols), m + FDOWN)
        push_pair(zo, cols, m + CD, sib)

    def xz_all(j):
        m, cols = j * PER_CHUNK, span(j)
        for zz, idx in ((z, CA), (zm, CB), (zp, CC), (zo, CD)):
            landed(res.at[1 - c, :, zz, :, cols], m + idx)

    def finish(j):
        kind, base_at, unit, size, _ = places[j]
        (zx_all if JOBS[j][3] == "zx" else xz_all)(j)
        at = slice(base_at, base_at + 2 * size)
        if kind == "T":
            piece = res[:, :, :, :, at].reshape(256, 2 * size)
            ig[...] += jnp.dot(
                piece, wgu[2 * unit : 2 * unit + 2 * size, :], preferred_element_type=F32
            )
        else:
            start = 128 * (kind == "L")
            lo = 2 * unit
            value = jnp.dot(
                res[0, :, :, :, at].reshape(128, 2 * size), wgu[lo : lo + 2 * size, :],
                preferred_element_type=F32,
            )
            lo += 2 * size
            value += jnp.dot(
                res[1, :, :, :, at].reshape(128, 2 * size), wgu[lo : lo + 2 * size, :],
                preferred_element_type=F32,
            )
            ig[start : start + 128, :] += value

    def transposes(j):
        kind, base_at, unit, size, _ = places[j]
        for part in range(3):
            at = base_at + part * size

            @pl.loop(0, size // LANE)
            def _(i):
                cols = pl.ds(pl.multiple_of(at + i * LANE, LANE), LANE)
                if kind == "T":
                    to = pl.ds(pl.multiple_of(unit + i * LANE, LANE), LANE)
                    rt[part, to, :] = res[:, :, :, :, cols].reshape(256, LANE).T
                else:
                    start = 128 * (kind == "L")
                    for half in range(2):
                        to = pl.ds(pl.multiple_of(unit + half * size + i * LANE, LANE), LANE)
                        rt[part, to, start : start + 128] = (
                            res[half, :, :, :, cols].reshape(128, LANE).T
                        )

        if kind == "T":
            tokens, units = pl.ds(0, 256), pl.ds(unit, size)
        else:
            tokens, units = pl.ds(128 * (kind == "L"), 128), pl.ds(unit, 2 * size)
        copy = pltpu.make_async_copy(
            rt.at[:, units, tokens], r_out.at[:, units, tokens], osem.at[1 + j]
        )
        copy.start()
        outs.append(copy)

    def col_send():
        igs[...] = ig[...].astype(BF16)
        for slot in range(1, 8):
            send(
                igs.at[slot * 32 : slot * 32 + 32], igr.at[slot], base + 9 + slot,
                cdev(*owner(slot)),
            )

    reduce = {"zx": (zx_far, zx_near, zx_cross), "xz": (xz_cross, xz_far, xz_near)}
    gather = {
        "zx": (zx_gather_near, zx_gather_far, zx_gather_cross),
        "xz": (xz_gather_cross, xz_gather_near, xz_gather_far),
    }
    col = (col_near, col_cross, col_next, col_far, col_send)
    for stage, j in ORDER:
        if j < 0:
            col[stage]()
        else:
            _, _, over, back = JOBS[j]
            (
                products, back_products, *reduce[over], activate, *gather[back], finish, transposes,
            )[stage](j)

    total = ig[:32, :]
    for slot in range(1, 8):
        landed(igr.at[slot], base + 9 + slot)
        total = total + igr[slot].astype(F32)
    ig_out[...] = total

    for copy in sent:
        copy.wait_send()
    for copy in outs:
        copy.wait()


def exchange(tokens, out_grad, token_weight, gate_weight, up_weight, down_weight):
    width, depth = gate_weight.shape
    wide = pl.cdiv(width, LANE) * LANE
    cols = 3 * wide
    n = len(JOBS)
    messages = n * PER_CHUNK + COLS
    hbm = pl.BlockSpec(memory_space=pl.ANY)
    vmem = pl.BlockSpec(memory_space=pltpu.VMEM)
    return pl.pallas_call(
        functools.partial(exchange_kernel, width),
        out_shape=(
            pltpu.VMEM((3, wide, 256), BF16),
            pltpu.VMEM((2, 256, depth), BF16),
            jax.ShapeDtypeStruct((32, depth), F32),
        ),
        in_specs=[hbm, hbm, vmem, hbm, hbm, hbm],
        out_specs=(hbm, hbm, vmem),
        scratch_shapes=[
            pltpu.VMEM((2 * wide, depth), BF16),
            pltpu.VMEM((wide, depth), BF16),
            pltpu.VMEM((2, 256, depth), BF16),
            pltpu.VMEM((2, 2, 4, 16, cols), F32),
            pltpu.VMEM((2, 4, 16, cols), F32),
            pltpu.VMEM((2, 16, cols), BF16),
            pltpu.VMEM((2, 16, cols), BF16),
            pltpu.VMEM((2, 2, 16, cols), BF16),
            pltpu.VMEM((2, 2, 16, cols), BF16),
            pltpu.VMEM((16, cols), F32),
            pltpu.VMEM((4, 16, cols), BF16),
            pltpu.VMEM((4, 16, cols), BF16),
            pltpu.VMEM((2, 2, 4, 16, cols), BF16),
            pltpu.VMEM((3, wide, 256), BF16),
            pltpu.VMEM((256, depth), F32),
            pltpu.VMEM((256, depth), BF16),
            pltpu.VMEM((8, 32, depth), BF16),
            pltpu.SemaphoreType.DMA((messages,)),
            pltpu.SemaphoreType.DMA((messages,)),
            pltpu.SemaphoreType.DMA((2 + 6 * n,)),
            pltpu.SemaphoreType.DMA((1 + n,)),
        ],
        compiler_params=pltpu.CompilerParams(
            collective_id=0, has_side_effects=True, vmem_limit_bytes=50 * 1024 * 1024
        ),
        cost_estimate=pl.CostEstimate(
            flops=10 * 256 * depth * width, bytes_accessed=6 * depth * width + 6 * 256 * width,
            transcendentals=0,
        ),
        name="exchange",
    )(tokens, out_grad, token_weight.reshape(1, 256), gate_weight, up_weight, down_weight)


GRAD_ROWS = 336


def grads_kernel(r_h, ab_h, gate_grad, up_grad, down_grad, r, ab, out, isem, osem):
    step = GRAD_ROWS
    n = gate_grad.shape[0] // step

    def load(i):
        rows = pl.ds(pl.multiple_of(i * step, 16), step)
        return pltpu.make_async_copy(r_h.at[:, rows], r.at[:, rows], isem.at[i])

    def store(i, part):
        rows = pl.ds(pl.multiple_of(i * step, 16), step)
        to = (gate_grad, up_grad, down_grad)[part]
        return pltpu.make_async_copy(out.at[part, rows], to.at[rows], osem.at[3 * i + part])

    sides = pltpu.make_async_copy(ab_h, ab, isem.at[n])
    sides.start()
    for i in range(n):
        load(i).start()
    sides.wait()

    @pl.loop(0, n)
    def _(i):
        load(i).wait()
        rows = pl.ds(pl.multiple_of(i * step, 16), step)
        for part in range(3):
            out[part, rows, :] = jnp.dot(
                r[part, rows, :], ab[part // 2], preferred_element_type=F32
            ).astype(BF16)
            store(i, part).start()

    for i in range(n):
        for part in range(3):
            store(i, part).wait()


def grads(r, ab, width):
    depth = ab.shape[2]
    assert width % GRAD_ROWS == 0
    n = width // GRAD_ROWS
    hbm = pl.BlockSpec(memory_space=pl.ANY)
    return pl.pallas_call(
        grads_kernel,
        in_specs=[hbm, hbm],
        out_specs=(hbm, hbm, hbm),
        out_shape=(pltpu.HBM((width, depth), BF16),) * 3,
        scratch_shapes=[
            pltpu.VMEM(r.shape, BF16),
            pltpu.VMEM(ab.shape, BF16),
            pltpu.VMEM((3, width, depth), BF16),
            pltpu.SemaphoreType.DMA((n + 1,)),
            pltpu.SemaphoreType.DMA((3 * n,)),
        ],
        compiler_params=pltpu.CompilerParams(vmem_limit_bytes=24 * 1024 * 1024),
        name="grads",
    )(r, ab)


def body(tokens, out_grad, token_weight, gate_weight, up_weight, down_weight):
    width = gate_weight.shape[1]
    r, ab, input_grad = exchange(
        tokens, out_grad, token_weight, gate_weight.T, up_weight.T, down_weight
    )
    gate_grad, up_grad, down_grad = grads(r, ab, width)
    return input_grad, gate_grad.T, up_grad.T, down_grad


def solution(mesh):
    return jax.shard_map(
        body,
        mesh=mesh,
        in_specs=(
            P("col", "row"),
            P("col", "row"),
            P(),
            P("row", "col"),
            P("row", "col"),
            P("col", "row"),
        ),
        out_specs=(P("col", "row"), P("row", "col"), P("row", "col"), P("col", "row")),
        check_vma=False,
    )
```

```python
import functools

import jax
import jax.numpy as jnp
from jax import lax
from jax.experimental import pallas as pl
from jax.experimental.pallas import tpu as pltpu
from jax.sharding import PartitionSpec as P

BF16, F32 = jnp.bfloat16, jnp.float32
MESH = pl.DeviceIdType.MESH
LANE = 128
JOBS = (
    ("E", 4, "zx", "zx"),
    ("L", 4, "xz", "zx"),
    ("T", 4, "zx", "xz"),
    ("T", 3, "zx", "xz"),
    ("T", 4, "xz", "zx"),
    ("T", 3, "zx", "xz"),
    ("T", 3, "zx", "xz"),
    ("T", 2, "xz", "zx"),
    ("T", 2, "zx", "zx"),
)
ORDER = (
    (0, -1), (1, -1), (0, 0), (1, 0), (2, -1), (2, 0), (3, -1), (0, 1), (1, 1), (3, 0), (0, 2),
    (1, 2), (0, 3), (1, 3), (2, 1), (0, 4), (2, 2), (4, 0), (1, 4), (0, 5), (2, 3), (1, 5), (0, 6),
    (3, 2), (2, 4), (1, 6), (3, 1), (3, 3), (5, 0), (2, 5), (0, 7), (2, 6), (1, 7), (4, 2), (0, 8),
    (4, 1), (1, 8), (4, 3), (2, 7), (3, 4), (6, 0), (2, 8), (3, 5), (5, 2), (3, 6), (5, 1), (5, 3),
    (7, 0), (4, 4), (3, 8), (3, 7), (4, 5), (4, 6), (6, 2), (6, 1), (6, 3), (5, 4), (8, 0), (4, 7),
    (4, 8), (5, 5), (5, 6), (7, 2), (9, 0), (7, 1), (10, 0), (7, 3), (6, 4), (5, 8), (6, 5), (5, 7),
    (8, 2), (6, 6), (8, 1), (8, 3), (7, 4), (6, 8), (9, 2), (10, 2), (7, 5), (9, 1), (9, 3), (6, 7),
    (10, 1), (8, 4), (7, 6), (7, 8), (10, 3), (8, 5), (7, 7), (9, 4), (8, 6), (8, 8), (10, 4),
    (9, 5), (10, 5), (8, 7), (9, 6), (9, 8), (10, 6), (10, 8), (9, 7), (4, -1), (10, 7),
)
NT = (((1,), (1,)), ((), ()))


def places_of(width):
    out, at, pairs, taken = [], 0, 0, 0
    for kind, tiles, _, _ in JOBS:
        size = tiles * LANE
        if kind == "E":
            unit, pairs = pairs, pairs + 2 * size
        elif kind == "L":
            unit, taken = taken, taken + 2 * size
        else:
            assert taken == pairs or taken == 0
            unit = max(pairs, units_end(out))
        out.append((kind, at, unit, size, min(size, width - unit)))
        at += 3 * size
    assert taken == pairs and at == 3 * LANE * pl.cdiv(width, LANE)
    return out


def units_end(places):
    return max((unit + size for kind, _, unit, size, _ in places if kind == "T"), default=0)


(
    PAIR, PB, PC, PD, ZA, ZB, ZUP, ZDOWN, X1,
    GUP, GDOWN, FUP, FDOWN, XA, XB, XC, XD, CA, CB, CC, CD,
) = range(21)
PER_CHUNK = 21
COLS = 9 + 8


def exchange_kernel(
    width,
    tok, og, tw, wg_h, wu_h, wd_h,
    r_out, ab_out, ig_out,
    wgu, wd, ab, pf, pr, zs1, zr1, zs2, zr2, own, xs, xr, res, rt, ig, igs, igr,
    ssem, rsem, lsem, osem,
):
    places = places_of(width)
    n = len(places)
    row, k = lax.axis_index("row"), lax.axis_index("col")
    x, z, c = row // 8, (row // 2) % 4, row % 2
    y, h = k // 2, k % 2
    zp, zm, zo = (z + 1) % 4, (z + 3) % 4, (z + 2) % 4
    yp, ym, yo = (y + 1) % 4, (y + 3) % 4, (y + 2) % 4

    def rdev(xx, zz, cc):
        return (xx * 8 + zz * 2 + cc, k)

    def cdev(yy, hh):
        return (row, yy * 2 + hh)

    sib, xn = rdev(x, z, 1 - c), rdev(1 - x, z, c)
    up, down = rdev(x, zp, c), rdev(x, zm, c)

    def owner(slot):
        return ((y, h), (ym, h), (yp, h), (y, 1 - h), (ym, 1 - h), (yp, 1 - h), (yo, h), (yo, 1 - h))[slot]

    sent = []

    def send(src, dst, idx, dev):
        copy = pltpu.make_async_remote_copy(
            src_ref=src, dst_ref=dst, send_sem=ssem.at[idx], recv_sem=rsem.at[idx],
            device_id=dev, device_id_type=MESH,
        )
        copy.start()
        sent.append(copy)

    def landed(ref, idx):
        pltpu.make_async_remote_copy(
            src_ref=ref, dst_ref=ref, send_sem=ssem.at[idx], recv_sem=rsem.at[idx],
            device_id=sib, device_id_type=MESH,
        ).wait_recv()

    first = [
        pltpu.make_async_copy(tok, ab.at[0, :32], lsem.at[0]),
        pltpu.make_async_copy(og, ab.at[1, :32], lsem.at[1]),
    ]
    weights = [[] for _ in places]
    for j, (kind, _, unit, size, valid) in enumerate(places):
        if kind == "L":
            continue
        for lo in (unit,) if kind == "T" else (unit, unit + size):
            for src, dst, to in (
                (wg_h, wgu, 2 * lo), (wu_h, wgu, 2 * lo + size), (wd_h, wd, lo)
            ):
                weights[j].append(pltpu.make_async_copy(
                    src.at[pl.ds(lo, valid)], dst.at[pl.ds(to, valid)],
                    lsem.at[2 + 6 * j + len(weights[j])],
                ))
                if valid < size:
                    dst[to + valid : to + size, :] = jnp.zeros((size - valid, dst.shape[1]), BF16)
    for copy in first + sum(weights, []):
        copy.start()

    barrier = pltpu.get_barrier_semaphore()
    greeted = [sib, xn, up, down]
    for slot in range(1, 8):
        greeted.append(cdev(*owner(slot)))
    for dev in greeted:
        pl.semaphore_signal(barrier, inc=1, device_id=dev, device_id_type=MESH)
    ig[...] = jnp.zeros_like(ig)
    for copy in first:
        copy.wait()
    pl.semaphore_wait(barrier, len(greeted))

    base = n * PER_CHUNK

    def both(slot):
        return ab.at[:, slot * 32 : slot * 32 + 32]

    def one(part, slot):
        return ab.at[part, slot * 32 : slot * 32 + 32]

    send(both(0), both(3), base + 2, cdev(y, 1 - h))
    send(both(0), both(1), base + 0, cdev(yp, h))
    send(both(0), both(2), base + 1, cdev(ym, h))

    def col_near():
        landed(both(1), base + 0)
        send(one(0, 1), one(0, 6), base + 5, cdev(yp, h))
        landed(both(2), base + 1)
        send(one(1, 2), one(1, 6), base + 6, cdev(ym, h))

    def col_cross():
        landed(both(3), base + 2)
        send(both(3), both(4), base + 3, cdev(yp, h))
        send(both(3), both(5), base + 4, cdev(ym, h))

    def col_next():
        landed(both(4), base + 3)
        send(one(0, 4), one(0, 7), base + 7, cdev(yp, h))
        landed(both(5), base + 4)
        send(one(1, 5), one(1, 7), base + 8, cdev(ym, h))

    outs = []

    def col_far():
        landed(one(0, 6), base + 5)
        landed(one(1, 6), base + 6)
        landed(one(0, 7), base + 7)
        landed(one(1, 7), base + 8)
        copy = pltpu.make_async_copy(ab, ab_out, osem.at[0])
        copy.start()
        outs.append(copy)

    def column_of(half):
        lanes = lax.broadcasted_iota(jnp.int32, (16, 256), 1)
        rows = lax.broadcasted_iota(jnp.int32, (16, 256), 0)
        place, among = x * 2 + z // 2, 0
        for i in range(4):
            yy, hh = owner(4 * half + i)
            among = among + jnp.where(place == i, (yy * 2 + hh) * 32, 0)
        at = rows + (among + (z % 2) * 16)
        return jnp.sum(
            jnp.where(lanes == at, jnp.broadcast_to(tw[...], (16, 256)), 0.0), axis=1, keepdims=True
        )

    columns = {"E": column_of(0), "L": column_of(1)}
    columns["T"] = jnp.where(c == 0, columns["E"], columns["L"])

    def span(j):
        _, at, _, size, _ = places[j]
        return slice(at, at + 3 * size)

    def halves(j):
        _, at, _, size, _ = places[j]
        cut = at + (3 * size // LANE // 2) * LANE
        return slice(at, cut), slice(cut, at + 3 * size)

    def multiply(j, side, wide, first, count, to):
        kind, _, unit, size, _ = places[j]
        rows = {"E": slice(0, 128), "L": slice(128, 256), "T": slice(0, 256)}[kind]

        def block(half, lo, at, width):
            value = lax.dot_general(
                ab[side, rows, :], wide[lo : lo + width, :], NT, preferred_element_type=F32
            )
            if kind == "T":
                pf[:, :, :, :, at : at + width] = value.reshape(2, 2, 4, 16, width)
            else:
                pf[half, :, :, :, at : at + width] = value.reshape(2, 4, 16, width)

        for half in range(1 if kind == "T" else 2):
            lo = first + half * count

            for at in range(0, count, 256):
                block(half, lo + at, to + at, min(256, count - at))

    def products(j):
        kind, base_at, unit, size, _ = places[j]
        for copy in weights[j]:
            copy.wait()
        multiply(j, 0, wgu, 2 * unit, 2 * size, base_at)

    def back_products(j):
        _, base_at, unit, size, _ = places[j]
        m, cols = j * PER_CHUNK, span(j)
        multiply(j, 1, wd, unit, size, base_at + 2 * size)
        if JOBS[j][2] == "zx":
            for zz, idx in ((zo, PAIR), (zp, PB), (zm, PC), (z, PD)):
                send(pf.at[1 - c, :, zz, :, cols], pr.at[:, zz, :, cols], m + idx, sib)
        else:
            for xx, idx in ((1 - x, PAIR), (x, PB)):
                send(pf.at[1 - c, xx, :, :, cols], pr.at[xx, :, :, cols], m + idx, sib)

    def chip(xx, zz, cols):
        return pf[c, xx, zz, :, cols] + pr[xx, zz, :, cols]

    def chip_sum(xx, zz, cols):
        return chip(xx, zz, cols) + xr[zz, :, cols].astype(F32)

    def zx_far(j):
        m, cols = j * PER_CHUNK, span(j)
        landed(pr.at[:, zo, :, cols], m + PAIR)
        zs1[0, :, cols] = chip(0, zo, cols).astype(BF16)
        send(zs1.at[0, :, cols], zr1.at[0, :, cols], m + ZA, up)
        zs1[1, :, cols] = chip(1, zo, cols).astype(BF16)
        send(zs1.at[1, :, cols], zr1.at[1, :, cols], m + ZB, down)

    def zx_near(j):
        m, cols = j * PER_CHUNK, span(j)
        landed(pr.at[:, zp, :, cols], m + PB)
        landed(zr1.at[0, :, cols], m + ZA)
        zs2[0, 0, :, cols] = (chip(0, zp, cols) + zr1[0, :, cols].astype(F32)).astype(BF16)
        zs2[0, 1, :, cols] = chip(1, zp, cols).astype(BF16)
        send(zs2.at[0, :, :, cols], zr2.at[0, :, :, cols], m + ZUP, up)
        landed(pr.at[:, zm, :, cols], m + PC)
        landed(zr1.at[1, :, cols], m + ZB)
        zs2[1, 0, :, cols] = chip(0, zm, cols).astype(BF16)
        zs2[1, 1, :, cols] = (chip(1, zm, cols) + zr1[1, :, cols].astype(F32)).astype(BF16)
        send(zs2.at[1, :, :, cols], zr2.at[1, :, :, cols], m + ZDOWN, down)

    def zx_cross(j):
        m, cols = j * PER_CHUNK, span(j)
        landed(pr.at[:, z, :, cols], m + PD)
        landed(zr2.at[0, :, :, cols], m + ZUP)
        landed(zr2.at[1, :, :, cols], m + ZDOWN)

        def ring(xx):
            return chip(xx, z, cols) + zr2[0, xx, :, cols].astype(F32) + zr2[1, xx, :, cols].astype(F32)

        xs[0, :, cols] = ring(1 - x).astype(BF16)
        send(xs.at[0, :, cols], xr.at[0, :, cols], m + X1, xn)
        own[:, cols] = ring(x)

    def zx_total(j):
        m, cols = j * PER_CHUNK, span(j)
        landed(xr.at[0, :, cols], m + X1)
        return lambda at: own[:, at] + xr[0, :, at].astype(F32)

    def xz_cross(j):
        m, cols = j * PER_CHUNK, span(j)
        landed(pr.at[1 - x, :, :, cols], m + PAIR)
        xs[:, :, cols] = (pf[c, 1 - x, :, :, cols] + pr[1 - x, :, :, cols]).astype(BF16)
        send(xs.at[:, :, cols], xr.at[:, :, cols], m + X1, xn)

    def xz_far(j):
        m, cols = j * PER_CHUNK, span(j)
        lo, hi = halves(j)
        landed(pr.at[x, :, :, cols], m + PB)
        landed(xr.at[:, :, cols], m + X1)
        zs1[0, :, lo] = chip_sum(x, zo, lo).astype(BF16)
        send(zs1.at[0, :, lo], zr1.at[0, :, lo], m + ZA, up)
        zs1[1, :, hi] = chip_sum(x, zo, hi).astype(BF16)
        send(zs1.at[1, :, hi], zr1.at[1, :, hi], m + ZB, down)

    def xz_near(j):
        m, cols = j * PER_CHUNK, span(j)
        lo, hi = halves(j)
        landed(zr1.at[0, :, lo], m + ZA)
        zs2[0, 0, :, lo] = (chip_sum(x, zp, lo) + zr1[0, :, lo].astype(F32)).astype(BF16)
        zs2[0, 0, :, hi] = chip_sum(x, zp, hi).astype(BF16)
        send(zs2.at[0, 0, :, cols], zr2.at[0, 0, :, cols], m + ZUP, up)
        landed(zr1.at[1, :, hi], m + ZB)
        zs2[1, 0, :, lo] = chip_sum(x, zm, lo).astype(BF16)
        zs2[1, 0, :, hi] = (chip_sum(x, zm, hi) + zr1[1, :, hi].astype(F32)).astype(BF16)
        send(zs2.at[1, 0, :, cols], zr2.at[1, 0, :, cols], m + ZDOWN, down)

    def xz_total(j):
        m, cols = j * PER_CHUNK, span(j)
        landed(zr2.at[0, 0, :, cols], m + ZUP)
        landed(zr2.at[1, 0, :, cols], m + ZDOWN)
        return lambda at: (
            chip_sum(x, z, at) + zr2[0, 0, :, at].astype(F32) + zr2[1, 0, :, at].astype(F32)
        )

    def here(xx, zz, cols):
        return res.at[c, xx, zz, :, cols]

    def push(xx, zz, cols, idx, dev):
        send(here(xx, zz, cols), here(xx, zz, cols), idx, dev)

    def push_pair(zz, cols, idx, dev):
        part = res.at[c, :, zz, :, cols]
        send(part, part, idx, dev)

    def activate(j):
        kind, base_at, _, size, _ = places[j]
        m, cols = j * PER_CHUNK, span(j)
        total = (xz_total if JOBS[j][2] == "xz" else zx_total)(j)
        column = columns[kind]

        def place(part):
            return slice(base_at + part * size, base_at + part * size + size)

        gate, linear, back = total(place(0)), total(place(1)), total(place(2))
        sig = jax.nn.sigmoid(gate)
        silu = gate * sig
        scaled = column * back
        for part, value in enumerate((
            scaled * linear * sig * (1.0 + gate * (1.0 - sig)),
            scaled * silu,
            column * (silu * linear),
        )):
            res[c, x, z, :, place(part)] = value.astype(BF16)
        push(x, z, cols, m + XA, xn)
        if JOBS[j][3] == "zx":
            push(x, z, cols, m + GUP, up)
            push(x, z, cols, m + GDOWN, down)

    def zx_gather_near(j):
        m, cols = j * PER_CHUNK, span(j)
        lo, hi = halves(j)
        landed(here(x, zm, cols), m + GUP)
        push(x, zm, lo, m + FUP, up)
        push(x, zm, cols, m + XB, xn)
        landed(here(x, zp, cols), m + GDOWN)
        push(x, zp, hi, m + FDOWN, down)
        push(x, zp, cols, m + XC, xn)

    def zx_gather_far(j):
        m, cols = j * PER_CHUNK, span(j)
        lo, hi = halves(j)
        landed(here(x, zo, lo), m + FUP)
        landed(here(x, zo, hi), m + FDOWN)
        push(x, zo, cols, m + XD, xn)
        part = res.at[c, x, :, :, cols]
        send(part, part, m + CA, sib)

    def zx_gather_cross(j):
        m, cols = j * PER_CHUNK, span(j)
        landed(here(1 - x, z, cols), m + XA)
        landed(here(1 - x, zm, cols), m + XB)
        landed(here(1 - x, zp, cols), m + XC)
        landed(here(1 - x, zo, cols), m + XD)
        part = res.at[c, 1 - x, :, :, cols]
        send(part, part, m + CB, sib)

    def zx_all(j):
        m, cols = j * PER_CHUNK, span(j)
        landed(res.at[1 - c, x, :, :, cols], m + CA)
        landed(res.at[1 - c, 1 - x, :, :, cols], m + CB)

    def xz_gather_cross(j):
        m, cols = j * PER_CHUNK, span(j)
        landed(here(1 - x, z, cols), m + XA)
        push_pair(z, cols, m + GUP, up)
        push_pair(z, cols, m + GDOWN, down)
        push_pair(z, cols, m + CA, sib)

    def xz_gather_near(j):
        m, cols = j * PER_CHUNK, span(j)
        landed(res.at[c, :, zm, :, cols], m + GUP)
        push(0, zm, cols, m + FUP, up)
        landed(res.at[c, :, zp, :, cols], m + GDOWN)
        push(1, zp, cols, m + FDOWN, down)
        push_pair(zm, cols, m + CB, sib)
        push_pair(zp, cols, m + CC, sib)

    def xz_gather_far(j):
        m, cols = j * PER_CHUNK, span(j)
        landed(here(0, zo, cols), m + FUP)
        landed(here(1, zo, cols), m + FDOWN)
        push_pair(zo, cols, m + CD, sib)

    def xz_all(j):
        m, cols = j * PER_CHUNK, span(j)
        for zz, idx in ((z, CA), (zm, CB), (zp, CC), (zo, CD)):
            landed(res.at[1 - c, :, zz, :, cols], m + idx)

    def finish(j):
        kind, base_at, unit, size, _ = places[j]
        (zx_all if JOBS[j][3] == "zx" else xz_all)(j)
        at = slice(base_at, base_at + 2 * size)
        if kind == "T":
            piece = res[:, :, :, :, at].reshape(256, 2 * size)
            ig[...] += jnp.dot(
                piece, wgu[2 * unit : 2 * unit + 2 * size, :], preferred_element_type=F32
            )
        else:
            start = 128 * (kind == "L")
            lo = 2 * unit
            value = jnp.dot(
                res[0, :, :, :, at].reshape(128, 2 * size), wgu[lo : lo + 2 * size, :],
                preferred_element_type=F32,
            )
            lo += 2 * size
            value += jnp.dot(
                res[1, :, :, :, at].reshape(128, 2 * size), wgu[lo : lo + 2 * size, :],
                preferred_element_type=F32,
            )
            ig[start : start + 128, :] += value

    def transposes(j):
        kind, base_at, unit, size, _ = places[j]
        for part in range(3):
            cols = slice(base_at + part * size, base_at + part * size + size)
            if kind == "T":
                rt[part, unit : unit + size, :] = res[:, :, :, :, cols].reshape(256, size).T
            else:
                start = 128 * (kind == "L")
                for lo, half in ((unit, 0), (unit + size, 1)):
                    rt[part, lo : lo + size, start : start + 128] = (
                        res[half, :, :, :, cols].reshape(128, size).T
                    )
        if kind == "T":
            tokens, units = pl.ds(0, 256), pl.ds(unit, size)
        else:
            tokens, units = pl.ds(128 * (kind == "L"), 128), pl.ds(unit, 2 * size)
        copy = pltpu.make_async_copy(
            rt.at[:, units, tokens], r_out.at[:, units, tokens], osem.at[1 + j]
        )
        copy.start()
        outs.append(copy)

    def col_send():
        igs[...] = ig[...].astype(BF16)
        for slot in range(1, 8):
            send(
                igs.at[slot * 32 : slot * 32 + 32], igr.at[slot], base + 9 + slot,
                cdev(*owner(slot)),
            )

    reduce = {"zx": (zx_far, zx_near, zx_cross), "xz": (xz_cross, xz_far, xz_near)}
    gather = {
        "zx": (zx_gather_near, zx_gather_far, zx_gather_cross),
        "xz": (xz_gather_cross, xz_gather_near, xz_gather_far),
    }
    col = (col_near, col_cross, col_next, col_far, col_send)
    for stage, j in ORDER:
        if j < 0:
            col[stage]()
        else:
            _, _, over, back = JOBS[j]
            (
                products, back_products, *reduce[over], activate, *gather[back], finish, transposes,
            )[stage](j)

    total = ig[:32, :]
    for slot in range(1, 8):
        landed(igr.at[slot], base + 9 + slot)
        total = total + igr[slot].astype(F32)
    ig_out[...] = total

    for copy in sent:
        copy.wait_send()
    for copy in outs:
        copy.wait()


def exchange(tokens, out_grad, token_weight, gate_weight, up_weight, down_weight):
    width, depth = gate_weight.shape
    wide = pl.cdiv(width, LANE) * LANE
    cols = 3 * wide
    n = len(JOBS)
    messages = n * PER_CHUNK + COLS
    hbm = pl.BlockSpec(memory_space=pl.ANY)
    vmem = pl.BlockSpec(memory_space=pltpu.VMEM)
    return pl.pallas_call(
        functools.partial(exchange_kernel, width),
        out_shape=(
            pltpu.VMEM((3, wide, 256), BF16),
            pltpu.VMEM((2, 256, depth), BF16),
            jax.ShapeDtypeStruct((32, depth), F32),
        ),
        in_specs=[hbm, hbm, vmem, hbm, hbm, hbm],
        out_specs=(hbm, hbm, vmem),
        scratch_shapes=[
            pltpu.VMEM((2 * wide, depth), BF16),
            pltpu.VMEM((wide, depth), BF16),
            pltpu.VMEM((2, 256, depth), BF16),
            pltpu.VMEM((2, 2, 4, 16, cols), F32),
            pltpu.VMEM((2, 4, 16, cols), F32),
            pltpu.VMEM((2, 16, cols), BF16),
            pltpu.VMEM((2, 16, cols), BF16),
            pltpu.VMEM((2, 2, 16, cols), BF16),
            pltpu.VMEM((2, 2, 16, cols), BF16),
            pltpu.VMEM((16, cols), F32),
            pltpu.VMEM((4, 16, cols), BF16),
            pltpu.VMEM((4, 16, cols), BF16),
            pltpu.VMEM((2, 2, 4, 16, cols), BF16),
            pltpu.VMEM((3, wide, 256), BF16),
            pltpu.VMEM((256, depth), F32),
            pltpu.VMEM((256, depth), BF16),
            pltpu.VMEM((8, 32, depth), BF16),
            pltpu.SemaphoreType.DMA((messages,)),
            pltpu.SemaphoreType.DMA((messages,)),
            pltpu.SemaphoreType.DMA((2 + 6 * n,)),
            pltpu.SemaphoreType.DMA((1 + n,)),
        ],
        compiler_params=pltpu.CompilerParams(
            collective_id=0, has_side_effects=True, vmem_limit_bytes=50 * 1024 * 1024
        ),
        cost_estimate=pl.CostEstimate(
            flops=10 * 256 * depth * width, bytes_accessed=6 * depth * width + 6 * 256 * width,
            transcendentals=0,
        ),
        name="exchange",
    )(tokens, out_grad, token_weight.reshape(1, 256), gate_weight, up_weight, down_weight)


GRAD_ROWS = 336


def grads_kernel(r_h, ab_h, gate_grad, up_grad, down_grad, r, ab, out, isem, osem):
    step = GRAD_ROWS
    n = gate_grad.shape[0] // step

    def load(i):
        rows = pl.ds(pl.multiple_of(i * step, 16), step)
        return pltpu.make_async_copy(r_h.at[:, rows], r.at[:, rows], isem.at[i])

    def store(i, part):
        rows = pl.ds(pl.multiple_of(i * step, 16), step)
        to = (gate_grad, up_grad, down_grad)[part]
        return pltpu.make_async_copy(out.at[part, rows], to.at[rows], osem.at[3 * i + part])

    sides = pltpu.make_async_copy(ab_h, ab, isem.at[n])
    sides.start()
    for i in range(n):
        load(i).start()
    sides.wait()

    for i in range(n):
        load(i).wait()
        rows = slice(i * step, i * step + step)
        for part in range(3):
            out[part, rows, :] = jnp.dot(
                r[part, rows, :], ab[part // 2], preferred_element_type=F32
            ).astype(BF16)
            store(i, part).start()

    for i in range(n):
        for part in range(3):
            store(i, part).wait()


def grads(r, ab, width):
    depth = ab.shape[2]
    assert width % GRAD_ROWS == 0
    n = width // GRAD_ROWS
    hbm = pl.BlockSpec(memory_space=pl.ANY)
    return pl.pallas_call(
        grads_kernel,
        in_specs=[hbm, hbm],
        out_specs=(hbm, hbm, hbm),
        out_shape=(pltpu.HBM((width, depth), BF16),) * 3,
        scratch_shapes=[
            pltpu.VMEM(r.shape, BF16),
            pltpu.VMEM(ab.shape, BF16),
            pltpu.VMEM((3, width, depth), BF16),
            pltpu.SemaphoreType.DMA((n + 1,)),
            pltpu.SemaphoreType.DMA((3 * n,)),
        ],
        compiler_params=pltpu.CompilerParams(vmem_limit_bytes=24 * 1024 * 1024),
        name="grads",
    )(r, ab)


def body(tokens, out_grad, token_weight, gate_weight, up_weight, down_weight):
    width = gate_weight.shape[1]
    r, ab, input_grad = exchange(
        tokens, out_grad, token_weight, gate_weight.T, up_weight.T, down_weight
    )
    gate_grad, up_grad, down_grad = grads(r, ab, width)
    return input_grad, gate_grad.T, up_grad.T, down_grad


def solution(mesh):
    return jax.shard_map(
        body,
        mesh=mesh,
        in_specs=(
            P("col", "row"),
            P("col", "row"),
            P(),
            P("row", "col"),
            P("row", "col"),
            P("col", "row"),
        ),
        out_specs=(P("col", "row"), P("row", "col"), P("row", "col"), P("col", "row")),
        check_vma=False,
    )
```

```python
import functools

import jax
import jax.numpy as jnp
from jax import lax
from jax.experimental import pallas as pl
from jax.experimental.pallas import tpu as pltpu
from jax.sharding import PartitionSpec as P

BF16, F32 = jnp.bfloat16, jnp.float32
MESH = pl.DeviceIdType.MESH
LANE = 128
JOBS = (
    ("E", 4, "xz", "zx"),
    ("L", 4, "xz", "zx"),
    ("T", 5, "xz", "xz"),
    ("T", 3, "xz", "xz"),
    ("T", 3, "xz", "xz"),
    ("T", 2, "zx", "xz"),
    ("T", 5, "zx", "zx"),
    ("T", 3, "zx", "xz"),
)
ORDER = (
    (0, -1), (1, -1), (0, 0), (1, 0), (2, -1), (2, 0), (3, -1), (0, 1), (1, 1), (0, 2), (1, 2),
    (0, 3), (1, 3), (0, 4), (1, 4), (0, 5), (1, 5), (0, 6), (2, 1), (3, 0), (2, 2), (2, 3), (4, 0),
    (2, 4), (2, 5), (1, 6), (0, 7), (3, 1), (5, 0), (3, 5), (1, 7), (4, 1), (2, 6), (6, 0), (3, 2),
    (4, 5), (2, 7), (5, 1), (3, 6), (7, 0), (4, 2), (3, 3), (6, 1), (3, 4), (5, 5), (3, 7), (4, 6),
    (5, 2), (7, 1), (8, 0), (4, 3), (6, 5), (4, 4), (5, 6), (9, 0), (6, 2), (5, 3), (7, 5), (4, 7),
    (5, 4), (10, 0), (6, 6), (8, 1), (6, 3), (5, 7), (8, 5), (7, 2), (9, 1), (7, 6), (6, 4),
    (10, 1), (9, 5), (7, 3), (6, 7), (10, 5), (8, 2), (7, 4), (8, 3), (9, 2), (10, 2), (7, 7),
    (8, 6), (9, 3), (8, 4), (10, 3), (8, 7), (9, 6), (10, 6), (9, 4), (10, 4), (9, 7), (4, -1),
    (10, 7),
)
NT = (((1,), (1,)), ((), ()))


def places_of(width):
    out, at, pairs, taken = [], 0, 0, 0
    for kind, tiles, _, _ in JOBS:
        size = tiles * LANE
        if kind == "E":
            unit, pairs = pairs, pairs + 2 * size
        elif kind == "L":
            unit, taken = taken, taken + 2 * size
        else:
            assert taken == pairs or taken == 0
            unit = max(pairs, units_end(out))
        out.append((kind, 0, unit, size, min(size, width - unit)))
        at += 3 * size
    assert taken == pairs and at == 3 * LANE * pl.cdiv(width, LANE)
    return out


def units_end(places):
    return max((unit + size for kind, _, unit, size, _ in places if kind == "T"), default=0)


(
    PAIR, PB, PC, PD, ZA, ZB, ZUP, ZDOWN, X1, GUP, GDOWN, FUP, FDOWN, XA, CA,
) = range(15)
PER_CHUNK = 15
COLS = 9 + 8


BUFFERS = (
    ((2, 2, 4, 16), F32), ((2, 4, 16), F32),
    ((2, 16), BF16), ((2, 16), BF16), ((2, 2, 16), BF16), ((2, 2, 16), BF16),
    ((16,), F32), ((4, 16), BF16), ((4, 16), BF16), ((2, 2, 4, 16), BF16),
)


def exchange_kernel(
    width,
    tok, og, tw, wg_h, wu_h, wd_h,
    r_out, ab_out, ig_out,
    wgu, wd, ab, rt, ig, igs, igr, ssem, rsem, lsem, osem, *of_jobs,
):
    pf, pr, zs1, zr1, zs2, zr2, own, xs, xr, res = (of_jobs[i :: 10] for i in range(10))
    places = places_of(width)
    n = len(places)
    row, k = lax.axis_index("row"), lax.axis_index("col")
    x, z, c = row // 8, (row // 2) % 4, row % 2
    y, h = k // 2, k % 2
    zp, zm, zo = (z + 1) % 4, (z + 3) % 4, (z + 2) % 4
    yp, ym, yo = (y + 1) % 4, (y + 3) % 4, (y + 2) % 4

    def rdev(xx, zz, cc):
        return (xx * 8 + zz * 2 + cc, k)

    def cdev(yy, hh):
        return (row, yy * 2 + hh)

    sib, xn = rdev(x, z, 1 - c), rdev(1 - x, z, c)
    up, down = rdev(x, zp, c), rdev(x, zm, c)

    def owner(slot):
        return ((y, h), (ym, h), (yp, h), (y, 1 - h), (ym, 1 - h), (yp, 1 - h), (yo, h), (yo, 1 - h))[slot]

    sent = []

    def send(src, dst, idx, dev):
        copy = pltpu.make_async_remote_copy(
            src_ref=src, dst_ref=dst, send_sem=ssem.at[idx], recv_sem=rsem.at[idx],
            device_id=dev, device_id_type=MESH,
        )
        copy.start()
        sent.append(copy)

    def landed(ref, idx):
        pltpu.make_async_remote_copy(
            src_ref=ref, dst_ref=ref, send_sem=ssem.at[idx], recv_sem=rsem.at[idx],
            device_id=sib, device_id_type=MESH,
        ).wait_recv()

    first = [
        pltpu.make_async_copy(tok, ab.at[0, :32], lsem.at[0]),
        pltpu.make_async_copy(og, ab.at[1, :32], lsem.at[1]),
    ]
    weights = [[] for _ in places]
    for j, (kind, _, unit, size, valid) in enumerate(places):
        if kind == "L":
            continue
        for lo in (unit,) if kind == "T" else (unit, unit + size):
            for src, dst, to in (
                (wg_h, wgu, 2 * lo), (wu_h, wgu, 2 * lo + size), (wd_h, wd, lo)
            ):
                weights[j].append(pltpu.make_async_copy(
                    src.at[pl.ds(lo, valid)], dst.at[pl.ds(to, valid)],
                    lsem.at[2 + 6 * j + len(weights[j])],
                ))
                if valid < size:
                    dst[to + valid : to + size, :] = jnp.zeros((size - valid, dst.shape[1]), BF16)
    for copy in first + sum(weights, []):
        copy.start()

    barrier = pltpu.get_barrier_semaphore()
    greeted = [sib, xn, up, down]
    for slot in range(1, 8):
        greeted.append(cdev(*owner(slot)))
    for dev in greeted:
        pl.semaphore_signal(barrier, inc=1, device_id=dev, device_id_type=MESH)
    ig[...] = jnp.zeros_like(ig)
    for copy in first:
        copy.wait()
    pl.semaphore_wait(barrier, len(greeted))

    base = n * PER_CHUNK

    def both(slot):
        return ab.at[:, slot * 32 : slot * 32 + 32]

    def one(part, slot):
        return ab.at[part, slot * 32 : slot * 32 + 32]

    send(both(0), both(3), base + 2, cdev(y, 1 - h))
    send(both(0), both(1), base + 0, cdev(yp, h))
    send(both(0), both(2), base + 1, cdev(ym, h))

    def col_near():
        landed(both(1), base + 0)
        send(one(0, 1), one(0, 6), base + 5, cdev(yp, h))
        landed(both(2), base + 1)
        send(one(1, 2), one(1, 6), base + 6, cdev(ym, h))

    def col_cross():
        landed(both(3), base + 2)
        send(both(3), both(4), base + 3, cdev(yp, h))
        send(both(3), both(5), base + 4, cdev(ym, h))

    def col_next():
        landed(both(4), base + 3)
        send(one(0, 4), one(0, 7), base + 7, cdev(yp, h))
        landed(both(5), base + 4)
        send(one(1, 5), one(1, 7), base + 8, cdev(ym, h))

    outs = []

    def col_far():
        landed(one(0, 6), base + 5)
        landed(one(1, 6), base + 6)
        landed(one(0, 7), base + 7)
        landed(one(1, 7), base + 8)
        copy = pltpu.make_async_copy(ab, ab_out, osem.at[0])
        copy.start()
        outs.append(copy)

    def column_of(half):
        lanes = lax.broadcasted_iota(jnp.int32, (16, 256), 1)
        rows = lax.broadcasted_iota(jnp.int32, (16, 256), 0)
        place, among = x * 2 + z // 2, 0
        for i in range(4):
            yy, hh = owner(4 * half + i)
            among = among + jnp.where(place == i, (yy * 2 + hh) * 32, 0)
        at = rows + (among + (z % 2) * 16)
        return jnp.sum(
            jnp.where(lanes == at, jnp.broadcast_to(tw[...], (16, 256)), 0.0), axis=1, keepdims=True
        )

    columns = {"E": column_of(0), "L": column_of(1)}
    columns["T"] = jnp.where(c == 0, columns["E"], columns["L"])

    def span(j):
        _, at, _, size, _ = places[j]
        return slice(at, at + 3 * size)

    def halves(j):
        _, at, _, size, _ = places[j]
        cut = at + (3 * size // LANE // 2) * LANE
        return slice(at, cut), slice(cut, at + 3 * size)

    def multiply(j, side, wide, first, count, to):
        kind, _, unit, size, _ = places[j]
        rows = {"E": slice(0, 128), "L": slice(128, 256), "T": slice(0, 256)}[kind]

        def block(half, lo, at, width):
            value = lax.dot_general(
                ab[side, rows, :], wide[lo : lo + width, :], NT, preferred_element_type=F32
            )
            if kind == "T":
                pf[j][:, :, :, :, at : at + width] = value.reshape(2, 2, 4, 16, width)
            else:
                pf[j][half, :, :, :, at : at + width] = value.reshape(2, 4, 16, width)

        for half in range(1 if kind == "T" else 2):
            lo = first + half * count

            for at in range(0, count, 256):
                block(half, lo + at, to + at, min(256, count - at))

    def products(j):
        kind, base_at, unit, size, _ = places[j]
        for copy in weights[j]:
            copy.wait()
        multiply(j, 0, wgu, 2 * unit, 2 * size, base_at)

    def back_products(j):
        _, base_at, unit, size, _ = places[j]
        m, cols = j * PER_CHUNK, span(j)
        multiply(j, 1, wd, unit, size, base_at + 2 * size)
        if j > 0:
            send(pf[j].at[1 - c], pr[j], m + PAIR, sib)
        elif JOBS[j][2] == "zx":
            for zz, idx in ((zo, PAIR), (zp, PB), (zm, PC), (z, PD)):
                send(pf[j].at[1 - c, :, zz, :, cols], pr[j].at[:, zz, :, cols], m + idx, sib)
        else:
            for xx, idx in ((1 - x, PAIR), (x, PB)):
                send(pf[j].at[1 - c, xx, :, :, cols], pr[j].at[xx, :, :, cols], m + idx, sib)

    def chip(j, xx, zz, cols):
        return pf[j][c, xx, zz, :, cols] + pr[j][xx, zz, :, cols]

    def chip_sum(j, xx, zz, cols):
        return chip(j, xx, zz, cols) + xr[j][zz, :, cols].astype(F32)

    def zx_far(j):
        m, cols = j * PER_CHUNK, span(j)
        landed(pr[j] if j > 0 else pr[j].at[:, zo], m + PAIR)
        zs1[j][0, :, cols] = chip(j, 0, zo, cols).astype(BF16)
        send(zs1[j].at[0, :, cols], zr1[j].at[0, :, cols], m + ZA, up)
        zs1[j][1, :, cols] = chip(j, 1, zo, cols).astype(BF16)
        send(zs1[j].at[1, :, cols], zr1[j].at[1, :, cols], m + ZB, down)

    def zx_near(j):
        m, cols = j * PER_CHUNK, span(j)
        if j == 0:
            landed(pr[j].at[:, zp], m + PB)
        landed(zr1[j].at[0, :, cols], m + ZA)
        zs2[j][0, 0, :, cols] = (chip(j, 0, zp, cols) + zr1[j][0, :, cols].astype(F32)).astype(BF16)
        zs2[j][0, 1, :, cols] = chip(j, 1, zp, cols).astype(BF16)
        send(zs2[j].at[0, :, :, cols], zr2[j].at[0, :, :, cols], m + ZUP, up)
        if j == 0:
            landed(pr[j].at[:, zm], m + PC)
        landed(zr1[j].at[1, :, cols], m + ZB)
        zs2[j][1, 0, :, cols] = chip(j, 0, zm, cols).astype(BF16)
        zs2[j][1, 1, :, cols] = (chip(j, 1, zm, cols) + zr1[j][1, :, cols].astype(F32)).astype(BF16)
        send(zs2[j].at[1, :, :, cols], zr2[j].at[1, :, :, cols], m + ZDOWN, down)

    def zx_cross(j):
        m, cols = j * PER_CHUNK, span(j)
        if j == 0:
            landed(pr[j].at[:, z], m + PD)
        landed(zr2[j].at[0, :, :, cols], m + ZUP)
        landed(zr2[j].at[1, :, :, cols], m + ZDOWN)

        def ring(xx):
            return chip(j, xx, z, cols) + zr2[j][0, xx, :, cols].astype(F32) + zr2[j][1, xx, :, cols].astype(F32)

        xs[j][0, :, cols] = ring(1 - x).astype(BF16)
        send(xs[j].at[0, :, cols], xr[j].at[0, :, cols], m + X1, xn)
        own[j][:, cols] = ring(x)

    def zx_total(j):
        m, cols = j * PER_CHUNK, span(j)
        landed(xr[j].at[0, :, cols], m + X1)
        return lambda at: own[j][:, at] + xr[j][0, :, at].astype(F32)

    def xz_cross(j):
        m, cols = j * PER_CHUNK, span(j)
        landed(pr[j] if j > 0 else pr[j].at[1 - x], m + PAIR)
        xs[j][:, :, cols] = (pf[j][c, 1 - x, :, :, cols] + pr[j][1 - x, :, :, cols]).astype(BF16)
        send(xs[j].at[:, :, cols], xr[j].at[:, :, cols], m + X1, xn)

    def xz_far(j):
        m, cols = j * PER_CHUNK, span(j)
        lo, hi = halves(j)
        if j == 0:
            landed(pr[j].at[x], m + PB)
        landed(xr[j].at[:, :, cols], m + X1)
        zs1[j][0, :, lo] = chip_sum(j, x, zo, lo).astype(BF16)
        send(zs1[j].at[0, :, lo], zr1[j].at[0, :, lo], m + ZA, up)
        zs1[j][1, :, hi] = chip_sum(j, x, zo, hi).astype(BF16)
        send(zs1[j].at[1, :, hi], zr1[j].at[1, :, hi], m + ZB, down)

    def xz_near(j):
        m, cols = j * PER_CHUNK, span(j)
        lo, hi = halves(j)
        landed(zr1[j].at[0, :, lo], m + ZA)
        zs2[j][0, 0, :, lo] = (chip_sum(j, x, zp, lo) + zr1[j][0, :, lo].astype(F32)).astype(BF16)
        zs2[j][0, 0, :, hi] = chip_sum(j, x, zp, hi).astype(BF16)
        send(zs2[j].at[0, 0, :, cols], zr2[j].at[0, 0, :, cols], m + ZUP, up)
        landed(zr1[j].at[1, :, hi], m + ZB)
        zs2[j][1, 0, :, lo] = chip_sum(j, x, zm, lo).astype(BF16)
        zs2[j][1, 0, :, hi] = (chip_sum(j, x, zm, hi) + zr1[j][1, :, hi].astype(F32)).astype(BF16)
        send(zs2[j].at[1, 0, :, cols], zr2[j].at[1, 0, :, cols], m + ZDOWN, down)

    def xz_total(j):
        m, cols = j * PER_CHUNK, span(j)
        landed(zr2[j].at[0, 0, :, cols], m + ZUP)
        landed(zr2[j].at[1, 0, :, cols], m + ZDOWN)
        return lambda at: (
            chip_sum(j, x, z, at) + zr2[j][0, 0, :, at].astype(F32) + zr2[j][1, 0, :, at].astype(F32)
        )

    def here(j, xx, zz, cols):
        return res[j].at[c, xx, zz, :, cols]

    def push(j, xx, zz, cols, idx, dev):
        send(here(j, xx, zz, cols), here(j, xx, zz, cols), idx, dev)

    def push_pair(j, zz, cols, idx, dev):
        part = res[j].at[c, :, zz, :, cols]
        send(part, part, idx, dev)

    def activate(j):
        kind, base_at, _, size, _ = places[j]
        m, cols = j * PER_CHUNK, span(j)
        total = (xz_total if JOBS[j][2] == "xz" else zx_total)(j)
        column = columns[kind]

        def place(part):
            return slice(base_at + part * size, base_at + part * size + size)

        gate, linear, back = total(place(0)), total(place(1)), total(place(2))
        sig = jax.nn.sigmoid(gate)
        silu = gate * sig
        scaled = column * back
        for part, value in enumerate((
            scaled * linear * sig * (1.0 + gate * (1.0 - sig)),
            scaled * silu,
            column * (silu * linear),
        )):
            res[j][c, x, z, :, place(part)] = value.astype(BF16)
        if JOBS[j][3] == "zx":
            push(j, x, z, cols, m + GUP, up)
            push(j, x, z, cols, m + GDOWN, down)
        else:
            push(j, x, z, cols, m + XA, xn)

    def zx_gather_near(j):
        m, cols = j * PER_CHUNK, span(j)
        lo, hi = halves(j)
        landed(here(j, x, zm, cols), m + GUP)
        push(j, x, zm, lo, m + FUP, up)
        landed(here(j, x, zp, cols), m + GDOWN)
        push(j, x, zp, hi, m + FDOWN, down)

    def zx_gather_far(j):
        m = j * PER_CHUNK
        lo, hi = halves(j)
        landed(here(j, x, zo, lo), m + FUP)
        landed(here(j, x, zo, hi), m + FDOWN)
        part = res[j].at[c, x]
        send(part, part, m + XA, xn)

    def zx_gather_cross(j):
        landed(res[j].at[c, 1 - x], j * PER_CHUNK + XA)
        part = res[j].at[c]
        send(part, part, j * PER_CHUNK + CA, sib)

    def xz_gather_cross(j):
        m, cols = j * PER_CHUNK, span(j)
        landed(here(j, 1 - x, z, cols), m + XA)
        push_pair(j, z, cols, m + GUP, up)
        push_pair(j, z, cols, m + GDOWN, down)

    def xz_gather_near(j):
        m, cols = j * PER_CHUNK, span(j)
        landed(res[j].at[c, :, zm, :, cols], m + GUP)
        push(j, 0, zm, cols, m + FUP, up)
        landed(res[j].at[c, :, zp, :, cols], m + GDOWN)
        push(j, 1, zp, cols, m + FDOWN, down)

    def xz_gather_far(j):
        m, cols = j * PER_CHUNK, span(j)
        landed(here(j, 0, zo, cols), m + FUP)
        landed(here(j, 1, zo, cols), m + FDOWN)
        part = res[j].at[c]
        send(part, part, m + CA, sib)

    def finish(j):
        kind, base_at, unit, size, _ = places[j]
        landed(res[j].at[1 - c], j * PER_CHUNK + CA)
        at = slice(base_at, base_at + 2 * size)
        if kind == "T":
            piece = res[j][:, :, :, :, at].reshape(256, 2 * size)
            ig[...] += jnp.dot(
                piece, wgu[2 * unit : 2 * unit + 2 * size, :], preferred_element_type=F32
            )
        else:
            start = 128 * (kind == "L")
            lo = 2 * unit
            value = jnp.dot(
                res[j][0, :, :, :, at].reshape(128, 2 * size), wgu[lo : lo + 2 * size, :],
                preferred_element_type=F32,
            )
            lo += 2 * size
            value += jnp.dot(
                res[j][1, :, :, :, at].reshape(128, 2 * size), wgu[lo : lo + 2 * size, :],
                preferred_element_type=F32,
            )
            ig[start : start + 128, :] += value

    def transposes(j):
        kind, base_at, unit, size, _ = places[j]
        for part in range(3):
            cols = slice(base_at + part * size, base_at + part * size + size)
            if kind == "T":
                rt[part, unit : unit + size, :] = res[j][:, :, :, :, cols].reshape(256, size).T
            else:
                start = 128 * (kind == "L")
                for lo, half in ((unit, 0), (unit + size, 1)):
                    rt[part, lo : lo + size, start : start + 128] = (
                        res[j][half, :, :, :, cols].reshape(128, size).T
                    )
        if kind == "T":
            tokens, units = pl.ds(0, 256), pl.ds(unit, size)
        else:
            tokens, units = pl.ds(128 * (kind == "L"), 128), pl.ds(unit, 2 * size)
        copy = pltpu.make_async_copy(
            rt.at[:, units, tokens], r_out.at[:, units, tokens], osem.at[1 + j]
        )
        copy.start()
        outs.append(copy)

    def col_send():
        igs[...] = ig[...].astype(BF16)
        for slot in range(1, 8):
            send(
                igs.at[slot * 32 : slot * 32 + 32], igr.at[slot], base + 9 + slot,
                cdev(*owner(slot)),
            )

    reduce = {"zx": (zx_far, zx_near, zx_cross), "xz": (xz_cross, xz_far, xz_near)}
    gather = {
        "zx": (zx_gather_near, zx_gather_far, zx_gather_cross),
        "xz": (xz_gather_cross, xz_gather_near, xz_gather_far),
    }
    col = (col_near, col_cross, col_next, col_far, col_send)
    for stage, j in ORDER:
        if j < 0:
            col[stage]()
        else:
            _, _, over, back = JOBS[j]
            (
                products, back_products, *reduce[over], activate, *gather[back], finish, transposes,
            )[stage](j)

    total = ig[:32, :]
    for slot in range(1, 8):
        landed(igr.at[slot], base + 9 + slot)
        total = total + igr[slot].astype(F32)
    ig_out[...] = total

    for copy in sent:
        copy.wait_send()
    for copy in outs:
        copy.wait()


def exchange(tokens, out_grad, token_weight, gate_weight, up_weight, down_weight):
    width, depth = gate_weight.shape
    wide = pl.cdiv(width, LANE) * LANE
    n = len(JOBS)
    messages = n * PER_CHUNK + COLS
    hbm = pl.BlockSpec(memory_space=pl.ANY)
    vmem = pl.BlockSpec(memory_space=pltpu.VMEM)
    return pl.pallas_call(
        functools.partial(exchange_kernel, width),
        out_shape=(
            pltpu.VMEM((3, wide, 256), BF16),
            pltpu.VMEM((2, 256, depth), BF16),
            jax.ShapeDtypeStruct((32, depth), F32),
        ),
        in_specs=[hbm, hbm, vmem, hbm, hbm, hbm],
        out_specs=(hbm, hbm, vmem),
        scratch_shapes=[
            pltpu.VMEM((2 * wide, depth), BF16),
            pltpu.VMEM((wide, depth), BF16),
            pltpu.VMEM((2, 256, depth), BF16),
            pltpu.VMEM((3, wide, 256), BF16),
            pltpu.VMEM((256, depth), F32),
            pltpu.VMEM((256, depth), BF16),
            pltpu.VMEM((8, 32, depth), BF16),
            pltpu.SemaphoreType.DMA((messages,)),
            pltpu.SemaphoreType.DMA((messages,)),
            pltpu.SemaphoreType.DMA((2 + 6 * n,)),
            pltpu.SemaphoreType.DMA((1 + n,)),
            *(
                pltpu.VMEM((*dims, 3 * tiles * LANE), dtype)
                for _, tiles, _, _ in JOBS
                for dims, dtype in BUFFERS
            ),
        ],
        compiler_params=pltpu.CompilerParams(
            collective_id=0, has_side_effects=True, vmem_limit_bytes=50 * 1024 * 1024
        ),
        cost_estimate=pl.CostEstimate(
            flops=10 * 256 * depth * width, bytes_accessed=6 * depth * width + 6 * 256 * width,
            transcendentals=0,
        ),
        name="exchange",
    )(tokens, out_grad, token_weight.reshape(1, 256), gate_weight, up_weight, down_weight)


GRAD_ROWS = 336


def grads_kernel(r, ab, gate_grad, up_grad, down_grad, out, osem):
    step = GRAD_ROWS
    n = gate_grad.shape[0] // step

    def store(i, part):
        rows = pl.ds(pl.multiple_of(i * step, 16), step)
        to = (gate_grad, up_grad, down_grad)[part]
        return pltpu.make_async_copy(out.at[part, rows], to.at[rows], osem.at[3 * i + part])

    @pl.loop(0, n)
    def _(i):
        rows = pl.ds(pl.multiple_of(i * step, 16), step)
        for part in range(3):
            out[part, rows, :] = jnp.dot(
                r[part, rows, :], ab[part // 2], preferred_element_type=F32
            ).astype(BF16)
            store(i, part).start()

    for i in range(n):
        for part in range(3):
            store(i, part).wait()


def grads(r, ab, width):
    depth = ab.shape[2]
    assert width % GRAD_ROWS == 0
    n = width // GRAD_ROWS
    hbm = pl.BlockSpec(memory_space=pl.ANY)
    vmem = pl.BlockSpec(memory_space=pltpu.VMEM)
    return pl.pallas_call(
        grads_kernel,
        in_specs=[vmem, vmem],
        out_specs=(hbm, hbm, hbm),
        out_shape=(pltpu.HBM((width, depth), BF16),) * 3,
        scratch_shapes=[
            pltpu.VMEM((3, width, depth), BF16),
            pltpu.SemaphoreType.DMA((3 * n,)),
        ],
        compiler_params=pltpu.CompilerParams(vmem_limit_bytes=24 * 1024 * 1024),
        name="grads",
    )(r, ab)


def body(tokens, out_grad, token_weight, gate_weight, up_weight, down_weight):
    width = gate_weight.shape[1]
    r, ab, input_grad = exchange(
        tokens, out_grad, token_weight, gate_weight.T, up_weight.T, down_weight
    )
    gate_grad, up_grad, down_grad = grads(r, ab, width)
    return input_grad, gate_grad.T, up_grad.T, down_grad


def solution(mesh):
    return jax.shard_map(
        body,
        mesh=mesh,
        in_specs=(
            P("col", "row"),
            P("col", "row"),
            P(),
            P("row", "col"),
            P("row", "col"),
            P("col", "row"),
        ),
        out_specs=(P("col", "row"), P("row", "col"), P("row", "col"), P("col", "row")),
        check_vma=False,
    )
```

```python
import functools

import jax
import jax.numpy as jnp
from jax import lax
from jax.experimental import pallas as pl
from jax.experimental.pallas import tpu as pltpu
from jax.sharding import PartitionSpec as P

BF16, F32 = jnp.bfloat16, jnp.float32
MESH = pl.DeviceIdType.MESH
LANE = 128
JOBS = (
    ("E", 4, "zx", "zx"),
    ("L", 4, "xz", "zx"),
    ("T", 4, "zx", "xz"),
    ("T", 3, "zx", "xz"),
    ("T", 4, "xz", "zx"),
    ("T", 3, "zx", "xz"),
    ("T", 3, "zx", "xz"),
    ("T", 2, "xz", "zx"),
    ("T", 2, "zx", "zx"),
)
ORDER = (
    (0, -1), (1, -1), (0, 0), (1, 0), (2, -1), (2, 0), (3, -1), (0, 1), (1, 1), (3, 0), (0, 2),
    (1, 2), (0, 3), (1, 3), (2, 1), (0, 4), (2, 2), (4, 0), (1, 4), (0, 5), (2, 3), (1, 5), (0, 6),
    (3, 2), (2, 4), (1, 6), (3, 1), (3, 3), (5, 0), (2, 5), (0, 7), (2, 6), (1, 7), (4, 2), (0, 8),
    (4, 1), (1, 8), (4, 3), (2, 7), (3, 4), (6, 0), (2, 8), (3, 5), (5, 2), (3, 6), (5, 1), (5, 3),
    (7, 0), (4, 4), (3, 8), (3, 7), (4, 5), (4, 6), (6, 2), (6, 1), (6, 3), (5, 4), (8, 0), (4, 7),
    (4, 8), (5, 5), (5, 6), (7, 2), (9, 0), (7, 1), (10, 0), (7, 3), (6, 4), (5, 8), (6, 5), (5, 7),
    (8, 2), (6, 6), (8, 1), (8, 3), (7, 4), (6, 8), (9, 2), (10, 2), (7, 5), (9, 1), (9, 3), (6, 7),
    (10, 1), (8, 4), (7, 6), (7, 8), (10, 3), (8, 5), (7, 7), (9, 4), (8, 6), (8, 8), (10, 4),
    (9, 5), (10, 5), (8, 7), (9, 6), (9, 8), (10, 6), (10, 8), (9, 7), (4, -1), (10, 7),
)
NT = (((1,), (1,)), ((), ()))


def places_of(width):
    out, at, pairs, taken = [], 0, 0, 0
    for kind, tiles, _, _ in JOBS:
        size = tiles * LANE
        if kind == "E":
            unit, pairs = pairs, pairs + 2 * size
        elif kind == "L":
            unit, taken = taken, taken + 2 * size
        else:
            assert taken == pairs or taken == 0
            unit = max(pairs, units_end(out))
        out.append((kind, at, unit, size, min(size, width - unit)))
        at += 3 * size
    assert taken == pairs and at == 3 * LANE * pl.cdiv(width, LANE)
    return out


def units_end(places):
    return max((unit + size for kind, _, unit, size, _ in places if kind == "T"), default=0)


(
    PAIR, PB, PC, PD, ZA, ZB, ZUP, ZDOWN, X1,
    GUP, GDOWN, FUP, FDOWN, XA, XB, XC, XD, CA, CB, CC, CD,
) = range(21)
PER_CHUNK = 21
COLS = 9 + 8


def exchange_kernel(
    width,
    tok, og, tw, wg_h, wu_h, wd_h,
    r_out, ab_out, ig_out,
    wgu, wd, ab, pf, pr, zs1, zr1, zs2, zr2, own, xs, xr, res, rt, ig, igs, igr,
    ssem, rsem, lsem, osem,
):
    places = places_of(width)
    n = len(places)
    row, k = lax.axis_index("row"), lax.axis_index("col")
    x, z, c = row // 8, (row // 2) % 4, row % 2
    y, h = k // 2, k % 2
    zp, zm, zo = (z + 1) % 4, (z + 3) % 4, (z + 2) % 4
    yp, ym, yo = (y + 1) % 4, (y + 3) % 4, (y + 2) % 4

    def rdev(xx, zz, cc):
        return (xx * 8 + zz * 2 + cc, k)

    def cdev(yy, hh):
        return (row, yy * 2 + hh)

    sib, xn = rdev(x, z, 1 - c), rdev(1 - x, z, c)
    up, down = rdev(x, zp, c), rdev(x, zm, c)

    def owner(slot):
        return ((y, h), (ym, h), (yp, h), (y, 1 - h), (ym, 1 - h), (yp, 1 - h), (yo, h), (yo, 1 - h))[slot]

    sent = []

    def send(src, dst, idx, dev):
        copy = pltpu.make_async_remote_copy(
            src_ref=src, dst_ref=dst, send_sem=ssem.at[idx], recv_sem=rsem.at[idx],
            device_id=dev, device_id_type=MESH,
        )
        copy.start()
        sent.append(copy)

    def landed(ref, idx):
        pltpu.make_async_remote_copy(
            src_ref=ref, dst_ref=ref, send_sem=ssem.at[idx], recv_sem=rsem.at[idx],
            device_id=sib, device_id_type=MESH,
        ).wait_recv()

    first = [
        pltpu.make_async_copy(tok, ab.at[0, :32], lsem.at[0]),
        pltpu.make_async_copy(og, ab.at[1, :32], lsem.at[1]),
    ]
    weights = [[] for _ in places]
    for j, (kind, _, unit, size, valid) in enumerate(places):
        if kind == "L":
            continue
        for lo in (unit,) if kind == "T" else (unit, unit + size):
            for src, dst, to in (
                (wg_h, wgu, 2 * lo), (wu_h, wgu, 2 * lo + size), (wd_h, wd, lo)
            ):
                weights[j].append(pltpu.make_async_copy(
                    src.at[pl.ds(lo, valid)], dst.at[pl.ds(to, valid)],
                    lsem.at[2 + 6 * j + len(weights[j])],
                ))

    for copy in first:
        copy.start()
    barrier = pltpu.get_barrier_semaphore()
    greeted = [sib, xn, up, down]
    for slot in range(1, 8):
        greeted.append(cdev(*owner(slot)))
    for dev in greeted:
        pl.semaphore_signal(barrier, inc=1, device_id=dev, device_id_type=MESH)
    for copy in weights[0]:
        copy.start()
    for copy in first:
        copy.wait()
    pl.semaphore_wait(barrier, len(greeted))

    base = n * PER_CHUNK

    def both(slot):
        return ab.at[:, slot * 32 : slot * 32 + 32]

    def one(part, slot):
        return ab.at[part, slot * 32 : slot * 32 + 32]

    send(both(0), both(3), base + 2, cdev(y, 1 - h))
    send(both(0), both(1), base + 0, cdev(yp, h))
    send(both(0), both(2), base + 1, cdev(ym, h))
    for copy in sum(weights[1:], []):
        copy.start()
    kind, _, unit, size, valid = places[-1]
    assert kind == "T" and all(place[3] == place[4] for place in places[:-1])
    if valid < size:
        rows = jnp.zeros((size - valid, wd.shape[1]), BF16)
        wgu[2 * unit + valid : 2 * unit + size, :] = rows
        wgu[2 * unit + size + valid : 2 * unit + 2 * size, :] = rows
        wd[unit + valid : unit + size, :] = rows
    ig[...] = jnp.zeros_like(ig)

    def col_near():
        landed(both(1), base + 0)
        send(one(0, 1), one(0, 6), base + 5, cdev(yp, h))
        landed(both(2), base + 1)
        send(one(1, 2), one(1, 6), base + 6, cdev(ym, h))

    def col_cross():
        landed(both(3), base + 2)
        send(both(3), both(4), base + 3, cdev(yp, h))
        send(both(3), both(5), base + 4, cdev(ym, h))

    def col_next():
        landed(both(4), base + 3)
        send(one(0, 4), one(0, 7), base + 7, cdev(yp, h))
        landed(both(5), base + 4)
        send(one(1, 5), one(1, 7), base + 8, cdev(ym, h))

    outs = []

    def col_far():
        landed(one(0, 6), base + 5)
        landed(one(1, 6), base + 6)
        landed(one(0, 7), base + 7)
        landed(one(1, 7), base + 8)
        copy = pltpu.make_async_copy(ab, ab_out, osem.at[0])
        copy.start()
        outs.append(copy)

    def column_of(half):
        lanes = lax.broadcasted_iota(jnp.int32, (16, 256), 1)
        rows = lax.broadcasted_iota(jnp.int32, (16, 256), 0)
        place, among = x * 2 + z // 2, 0
        for i in range(4):
            yy, hh = owner(4 * half + i)
            among = among + jnp.where(place == i, (yy * 2 + hh) * 32, 0)
        at = rows + (among + (z % 2) * 16)
        return jnp.sum(
            jnp.where(lanes == at, jnp.broadcast_to(tw[...], (16, 256)), 0.0), axis=1, keepdims=True
        )

    columns = {"E": column_of(0), "L": column_of(1)}
    columns["T"] = jnp.where(c == 0, columns["E"], columns["L"])

    def span(j):
        _, at, _, size, _ = places[j]
        return slice(at, at + 3 * size)

    def halves(j):
        _, at, _, size, _ = places[j]
        cut = at + (3 * size // LANE // 2) * LANE
        return slice(at, cut), slice(cut, at + 3 * size)

    def multiply(j, side, wide, first, count, to):
        kind, _, unit, size, _ = places[j]
        rows = {"E": slice(0, 128), "L": slice(128, 256), "T": slice(0, 256)}[kind]

        def block(half, lo, at, width):
            value = lax.dot_general(
                ab[side, rows, :], wide[lo : lo + width, :], NT, preferred_element_type=F32
            )
            if kind == "T":
                pf[:, :, :, :, at : at + width] = value.reshape(2, 2, 4, 16, width)
            else:
                pf[half, :, :, :, at : at + width] = value.reshape(2, 4, 16, width)

        for half in range(1 if kind == "T" else 2):
            lo = first + half * count

            for at in range(0, count, 256):
                block(half, lo + at, to + at, min(256, count - at))

    def products(j):
        kind, base_at, unit, size, _ = places[j]
        for copy in weights[j]:
            copy.wait()
        multiply(j, 0, wgu, 2 * unit, 2 * size, base_at)

    def back_products(j):
        _, base_at, unit, size, _ = places[j]
        m, cols = j * PER_CHUNK, span(j)
        multiply(j, 1, wd, unit, size, base_at + 2 * size)
        if JOBS[j][2] == "zx":
            for zz, idx in ((zo, PAIR), (zp, PB), (zm, PC), (z, PD)):
                send(pf.at[1 - c, :, zz, :, cols], pr.at[:, zz, :, cols], m + idx, sib)
        else:
            for xx, idx in ((1 - x, PAIR), (x, PB)):
                send(pf.at[1 - c, xx, :, :, cols], pr.at[xx, :, :, cols], m + idx, sib)

    def chip(xx, zz, cols):
        return pf[c, xx, zz, :, cols] + pr[xx, zz, :, cols]

    def chip_sum(xx, zz, cols):
        return chip(xx, zz, cols) + xr[zz, :, cols].astype(F32)

    def zx_far(j):
        m, cols = j * PER_CHUNK, span(j)
        landed(pr.at[:, zo, :, cols], m + PAIR)
        zs1[0, :, cols] = chip(0, zo, cols).astype(BF16)
        send(zs1.at[0, :, cols], zr1.at[0, :, cols], m + ZA, up)
        zs1[1, :, cols] = chip(1, zo, cols).astype(BF16)
        send(zs1.at[1, :, cols], zr1.at[1, :, cols], m + ZB, down)

    def zx_near(j):
        m, cols = j * PER_CHUNK, span(j)
        landed(pr.at[:, zp, :, cols], m + PB)
        landed(zr1.at[0, :, cols], m + ZA)
        zs2[0, 0, :, cols] = (chip(0, zp, cols) + zr1[0, :, cols].astype(F32)).astype(BF16)
        zs2[0, 1, :, cols] = chip(1, zp, cols).astype(BF16)
        send(zs2.at[0, :, :, cols], zr2.at[0, :, :, cols], m + ZUP, up)
        landed(pr.at[:, zm, :, cols], m + PC)
        landed(zr1.at[1, :, cols], m + ZB)
        zs2[1, 0, :, cols] = chip(0, zm, cols).astype(BF16)
        zs2[1, 1, :, cols] = (chip(1, zm, cols) + zr1[1, :, cols].astype(F32)).astype(BF16)
        send(zs2.at[1, :, :, cols], zr2.at[1, :, :, cols], m + ZDOWN, down)

    def zx_cross(j):
        m, cols = j * PER_CHUNK, span(j)
        landed(pr.at[:, z, :, cols], m + PD)
        landed(zr2.at[0, :, :, cols], m + ZUP)
        landed(zr2.at[1, :, :, cols], m + ZDOWN)

        def ring(xx):
            return chip(xx, z, cols) + zr2[0, xx, :, cols].astype(F32) + zr2[1, xx, :, cols].astype(F32)

        xs[0, :, cols] = ring(1 - x).astype(BF16)
        send(xs.at[0, :, cols], xr.at[0, :, cols], m + X1, xn)
        own[:, cols] = ring(x)

    def zx_total(j):
        m, cols = j * PER_CHUNK, span(j)
        landed(xr.at[0, :, cols], m + X1)
        return lambda at: own[:, at] + xr[0, :, at].astype(F32)

    def xz_cross(j):
        m, cols = j * PER_CHUNK, span(j)
        landed(pr.at[1 - x, :, :, cols], m + PAIR)
        xs[:, :, cols] = (pf[c, 1 - x, :, :, cols] + pr[1 - x, :, :, cols]).astype(BF16)
        send(xs.at[:, :, cols], xr.at[:, :, cols], m + X1, xn)

    def xz_far(j):
        m, cols = j * PER_CHUNK, span(j)
        lo, hi = halves(j)
        landed(pr.at[x, :, :, cols], m + PB)
        landed(xr.at[:, :, cols], m + X1)
        zs1[0, :, lo] = chip_sum(x, zo, lo).astype(BF16)
        send(zs1.at[0, :, lo], zr1.at[0, :, lo], m + ZA, up)
        zs1[1, :, hi] = chip_sum(x, zo, hi).astype(BF16)
        send(zs1.at[1, :, hi], zr1.at[1, :, hi], m + ZB, down)

    def xz_near(j):
        m, cols = j * PER_CHUNK, span(j)
        lo, hi = halves(j)
        landed(zr1.at[0, :, lo], m + ZA)
        zs2[0, 0, :, lo] = (chip_sum(x, zp, lo) + zr1[0, :, lo].astype(F32)).astype(BF16)
        zs2[0, 0, :, hi] = chip_sum(x, zp, hi).astype(BF16)
        send(zs2.at[0, 0, :, cols], zr2.at[0, 0, :, cols], m + ZUP, up)
        landed(zr1.at[1, :, hi], m + ZB)
        zs2[1, 0, :, lo] = chip_sum(x, zm, lo).astype(BF16)
        zs2[1, 0, :, hi] = (chip_sum(x, zm, hi) + zr1[1, :, hi].astype(F32)).astype(BF16)
        send(zs2.at[1, 0, :, cols], zr2.at[1, 0, :, cols], m + ZDOWN, down)

    def xz_total(j):
        m, cols = j * PER_CHUNK, span(j)
        landed(zr2.at[0, 0, :, cols], m + ZUP)
        landed(zr2.at[1, 0, :, cols], m + ZDOWN)
        return lambda at: (
            chip_sum(x, z, at) + zr2[0, 0, :, at].astype(F32) + zr2[1, 0, :, at].astype(F32)
        )

    def here(xx, zz, cols):
        return res.at[c, xx, zz, :, cols]

    def push(xx, zz, cols, idx, dev):
        send(here(xx, zz, cols), here(xx, zz, cols), idx, dev)

    def push_pair(zz, cols, idx, dev):
        part = res.at[c, :, zz, :, cols]
        send(part, part, idx, dev)

    def activate(j):
        kind, base_at, _, size, _ = places[j]
        m, cols = j * PER_CHUNK, span(j)
        total = (xz_total if JOBS[j][2] == "xz" else zx_total)(j)
        column = columns[kind]

        def place(part):
            return slice(base_at + part * size, base_at + part * size + size)

        gate, linear, back = total(place(0)), total(place(1)), total(place(2))
        sig = jax.nn.sigmoid(gate)
        silu = gate * sig
        scaled = column * back
        for part, value in enumerate((
            scaled * linear * sig * (1.0 + gate * (1.0 - sig)),
            scaled * silu,
            column * (silu * linear),
        )):
            res[c, x, z, :, place(part)] = value.astype(BF16)
        push(x, z, cols, m + XA, xn)
        if JOBS[j][3] == "zx":
            push(x, z, cols, m + GUP, up)
            push(x, z, cols, m + GDOWN, down)

    def zx_gather_near(j):
        m, cols = j * PER_CHUNK, span(j)
        lo, hi = halves(j)
        landed(here(x, zm, cols), m + GUP)
        push(x, zm, lo, m + FUP, up)
        push(x, zm, cols, m + XB, xn)
        landed(here(x, zp, cols), m + GDOWN)
        push(x, zp, hi, m + FDOWN, down)
        push(x, zp, cols, m + XC, xn)

    def zx_gather_far(j):
        m, cols = j * PER_CHUNK, span(j)
        lo, hi = halves(j)
        landed(here(x, zo, lo), m + FUP)
        landed(here(x, zo, hi), m + FDOWN)
        push(x, zo, cols, m + XD, xn)
        part = res.at[c, x, :, :, cols]
        send(part, part, m + CA, sib)

    def zx_gather_cross(j):
        m, cols = j * PER_CHUNK, span(j)
        landed(here(1 - x, z, cols), m + XA)
        landed(here(1 - x, zm, cols), m + XB)
        landed(here(1 - x, zp, cols), m + XC)
        landed(here(1 - x, zo, cols), m + XD)
        part = res.at[c, 1 - x, :, :, cols]
        send(part, part, m + CB, sib)

    def zx_all(j):
        m, cols = j * PER_CHUNK, span(j)
        landed(res.at[1 - c, x, :, :, cols], m + CA)
        landed(res.at[1 - c, 1 - x, :, :, cols], m + CB)

    def xz_gather_cross(j):
        m, cols = j * PER_CHUNK, span(j)
        landed(here(1 - x, z, cols), m + XA)
        push_pair(z, cols, m + GUP, up)
        push_pair(z, cols, m + GDOWN, down)
        push_pair(z, cols, m + CA, sib)

    def xz_gather_near(j):
        m, cols = j * PER_CHUNK, span(j)
        landed(res.at[c, :, zm, :, cols], m + GUP)
        push(0, zm, cols, m + FUP, up)
        landed(res.at[c, :, zp, :, cols], m + GDOWN)
        push(1, zp, cols, m + FDOWN, down)
        push_pair(zm, cols, m + CB, sib)
        push_pair(zp, cols, m + CC, sib)

    def xz_gather_far(j):
        m, cols = j * PER_CHUNK, span(j)
        landed(here(0, zo, cols), m + FUP)
        landed(here(1, zo, cols), m + FDOWN)
        push_pair(zo, cols, m + CD, sib)

    def xz_all(j):
        m, cols = j * PER_CHUNK, span(j)
        for zz, idx in ((z, CA), (zm, CB), (zp, CC), (zo, CD)):
            landed(res.at[1 - c, :, zz, :, cols], m + idx)

    def finish(j):
        kind, base_at, unit, size, _ = places[j]
        (zx_all if JOBS[j][3] == "zx" else xz_all)(j)
        at = slice(base_at, base_at + 2 * size)
        if kind == "T":
            piece = res[:, :, :, :, at].reshape(256, 2 * size)
            ig[...] += jnp.dot(
                piece, wgu[2 * unit : 2 * unit + 2 * size, :], preferred_element_type=F32
            )
        else:
            start = 128 * (kind == "L")
            lo = 2 * unit
            value = jnp.dot(
                res[0, :, :, :, at].reshape(128, 2 * size), wgu[lo : lo + 2 * size, :],
                preferred_element_type=F32,
            )
            lo += 2 * size
            value += jnp.dot(
                res[1, :, :, :, at].reshape(128, 2 * size), wgu[lo : lo + 2 * size, :],
                preferred_element_type=F32,
            )
            ig[start : start + 128, :] += value

    def transposes(j):
        kind, base_at, unit, size, _ = places[j]
        for part in range(3):
            cols = slice(base_at + part * size, base_at + part * size + size)
            if kind == "T":
                rt[part, unit : unit + size, :] = res[:, :, :, :, cols].reshape(256, size).T
            else:
                start = 128 * (kind == "L")
                for lo, half in ((unit, 0), (unit + size, 1)):
                    rt[part, lo : lo + size, start : start + 128] = (
                        res[half, :, :, :, cols].reshape(128, size).T
                    )
        if kind == "T":
            tokens, units = pl.ds(0, 256), pl.ds(unit, size)
        else:
            tokens, units = pl.ds(128 * (kind == "L"), 128), pl.ds(unit, 2 * size)
        copy = pltpu.make_async_copy(
            rt.at[:, units, tokens], r_out.at[:, units, tokens], osem.at[1 + j]
        )
        copy.start()
        outs.append(copy)

    def col_send():
        igs[...] = ig[...].astype(BF16)
        for slot in (3, 7, 4, 5, 6, 1, 2):
            send(
                igs.at[slot * 32 : slot * 32 + 32], igr.at[slot], base + 9 + slot,
                cdev(*owner(slot)),
            )

    reduce = {"zx": (zx_far, zx_near, zx_cross), "xz": (xz_cross, xz_far, xz_near)}
    gather = {
        "zx": (zx_gather_near, zx_gather_far, zx_gather_cross),
        "xz": (xz_gather_cross, xz_gather_near, xz_gather_far),
    }
    col = (col_near, col_cross, col_next, col_far, col_send)
    for stage, j in ORDER:
        if j < 0:
            col[stage]()
        else:
            _, _, over, back = JOBS[j]
            (
                products, back_products, *reduce[over], activate, *gather[back], finish, transposes,
            )[stage](j)

    for copy in sent[:-7]:
        copy.wait_send()
    for copy in outs:
        copy.wait()
    total = ig[:32, :]
    for slot in range(1, 8):
        landed(igr.at[slot], base + 9 + slot)
        total = total + igr[slot].astype(F32)
    ig_out[...] = total

    for copy in sent[-7:]:
        copy.wait_send()


def exchange(tokens, out_grad, token_weight, gate_weight, up_weight, down_weight):
    width, depth = gate_weight.shape
    wide = pl.cdiv(width, LANE) * LANE
    cols = 3 * wide
    n = len(JOBS)
    messages = n * PER_CHUNK + COLS
    hbm = pl.BlockSpec(memory_space=pl.ANY)
    vmem = pl.BlockSpec(memory_space=pltpu.VMEM)
    return pl.pallas_call(
        functools.partial(exchange_kernel, width),
        out_shape=(
            pltpu.VMEM((3, wide, 256), BF16),
            pltpu.VMEM((2, 256, depth), BF16),
            jax.ShapeDtypeStruct((32, depth), F32),
        ),
        in_specs=[hbm, hbm, vmem, hbm, hbm, hbm],
        out_specs=(hbm, hbm, vmem),
        scratch_shapes=[
            pltpu.VMEM((2 * wide, depth), BF16),
            pltpu.VMEM((wide, depth), BF16),
            pltpu.VMEM((2, 256, depth), BF16),
            pltpu.VMEM((2, 2, 4, 16, cols), F32),
            pltpu.VMEM((2, 4, 16, cols), F32),
            pltpu.VMEM((2, 16, cols), BF16),
            pltpu.VMEM((2, 16, cols), BF16),
            pltpu.VMEM((2, 2, 16, cols), BF16),
            pltpu.VMEM((2, 2, 16, cols), BF16),
            pltpu.VMEM((16, cols), F32),
            pltpu.VMEM((4, 16, cols), BF16),
            pltpu.VMEM((4, 16, cols), BF16),
            pltpu.VMEM((2, 2, 4, 16, cols), BF16),
            pltpu.VMEM((3, wide, 256), BF16),
            pltpu.VMEM((256, depth), F32),
            pltpu.VMEM((256, depth), BF16),
            pltpu.VMEM((8, 32, depth), BF16),
            pltpu.SemaphoreType.DMA((messages,)),
            pltpu.SemaphoreType.DMA((messages,)),
            pltpu.SemaphoreType.DMA((2 + 6 * n,)),
            pltpu.SemaphoreType.DMA((1 + n,)),
        ],
        compiler_params=pltpu.CompilerParams(
            collective_id=0, has_side_effects=True, vmem_limit_bytes=50 * 1024 * 1024
        ),
        cost_estimate=pl.CostEstimate(
            flops=10 * 256 * depth * width, bytes_accessed=6 * depth * width + 6 * 256 * width,
            transcendentals=0,
        ),
        name="exchange",
    )(tokens, out_grad, token_weight.reshape(1, 256), gate_weight, up_weight, down_weight)


GRAD_ROWS = 336


def grads_kernel(r, ab, gate_grad, up_grad, down_grad, out, osem):
    step = GRAD_ROWS
    n = gate_grad.shape[0] // step

    def store(i, part):
        rows = pl.ds(pl.multiple_of(i * step, 16), step)
        to = (gate_grad, up_grad, down_grad)[part]
        return pltpu.make_async_copy(out.at[part, rows], to.at[rows], osem.at[3 * i + part])

    @pl.loop(0, n)
    def _(i):
        rows = pl.ds(pl.multiple_of(i * step, 16), step)
        for part in range(3):
            out[part, rows, :] = jnp.dot(
                r[part, rows, :], ab[part // 2], preferred_element_type=F32
            ).astype(BF16)
            store(i, part).start()

    for i in range(n):
        for part in range(3):
            store(i, part).wait()


def grads(r, ab, width):
    depth = ab.shape[2]
    assert width % GRAD_ROWS == 0
    n = width // GRAD_ROWS
    hbm = pl.BlockSpec(memory_space=pl.ANY)
    vmem = pl.BlockSpec(memory_space=pltpu.VMEM)
    return pl.pallas_call(
        grads_kernel,
        in_specs=[vmem, vmem],
        out_specs=(hbm, hbm, hbm),
        out_shape=(pltpu.HBM((width, depth), BF16),) * 3,
        scratch_shapes=[
            pltpu.VMEM((3, width, depth), BF16),
            pltpu.SemaphoreType.DMA((3 * n,)),
        ],
        compiler_params=pltpu.CompilerParams(vmem_limit_bytes=24 * 1024 * 1024),
        name="grads",
    )(r, ab)


def body(tokens, out_grad, token_weight, gate_weight, up_weight, down_weight):
    width = gate_weight.shape[1]
    r, ab, input_grad = exchange(
        tokens, out_grad, token_weight, gate_weight.T, up_weight.T, down_weight
    )
    gate_grad, up_grad, down_grad = grads(r, ab, width)
    return input_grad, gate_grad.T, up_grad.T, down_grad


def solution(mesh):
    return jax.shard_map(
        body,
        mesh=mesh,
        in_specs=(
            P("col", "row"),
            P("col", "row"),
            P(),
            P("row", "col"),
            P("row", "col"),
            P("col", "row"),
        ),
        out_specs=(P("col", "row"), P("row", "col"), P("row", "col"), P("col", "row")),
        check_vma=False,
    )
```

```python
import functools

import jax
import jax.numpy as jnp
from jax import lax
from jax.experimental import pallas as pl
from jax.experimental.pallas import tpu as pltpu
from jax.sharding import PartitionSpec as P

BF16, F32 = jnp.bfloat16, jnp.float32
MESH = pl.DeviceIdType.MESH
LANE = 128
JOBS = (
    ("E", 4, "xz", "zx"),
    ("L", 4, "xz", "xz"),
    ("T", 5, "zx", "zx"),
    ("T", 3, "xz", "xz"),
    ("T", 5, "xz", "xz"),
    ("T", 5, "zx", "zx"),
    ("T", 1, "zx", "zx"),
    ("T", 2, "zx", "xz"),
)
ORDER = (
    (0, -1), (1, -1), (0, 0), (1, 0), (2, -1), (2, 0), (3, -1), (0, 1), (1, 1), (0, 2), (1, 2),
    (0, 3), (1, 3), (0, 4), (2, 1), (3, 0), (1, 4), (2, 2), (0, 5), (1, 5), (4, 0), (2, 3), (0, 6),
    (1, 6), (3, 2), (5, 0), (3, 1), (2, 4), (2, 5), (3, 3), (2, 6), (4, 2), (0, 7), (1, 7), (6, 0),
    (4, 1), (2, 7), (3, 5), (7, 0), (4, 3), (5, 1), (3, 4), (5, 2), (3, 6), (3, 7), (4, 5), (5, 3),
    (8, 0), (4, 4), (6, 1), (6, 2), (4, 6), (9, 0), (10, 0), (4, 7), (5, 5), (6, 3), (5, 4), (7, 1),
    (7, 2), (5, 6), (5, 7), (6, 5), (7, 3), (6, 4), (8, 1), (6, 6), (8, 2), (7, 5), (6, 7), (8, 3),
    (9, 1), (10, 1), (9, 2), (10, 2), (9, 3), (10, 3), (7, 4), (7, 6), (7, 7), (8, 5), (8, 6),
    (8, 4), (8, 7), (9, 5), (9, 6), (10, 5), (10, 6), (9, 4), (9, 7), (4, -1), (10, 4), (10, 7),
)
NT = (((1,), (1,)), ((), ()))


def places_of(width):
    out, at, pairs, taken = [], 0, 0, 0
    for kind, tiles, _, _ in JOBS:
        size = tiles * LANE
        if kind == "E":
            unit, pairs = pairs, pairs + 2 * size
        elif kind == "L":
            unit, taken = taken, taken + 2 * size
        else:
            assert taken == pairs or taken == 0
            unit = max(pairs, units_end(out))
        out.append((kind, at, unit, size, min(size, width - unit)))
        at += 3 * size
    assert taken == pairs and at == 3 * LANE * pl.cdiv(width, LANE)
    return out


def units_end(places):
    return max((unit + size for kind, _, unit, size, _ in places if kind == "T"), default=0)


(
    PAIR, PB, PC, PD, ZA, ZB, ZUP, ZDOWN, X1,
    GUP, GDOWN, FUP, FDOWN, XA, XB, XC, XD, CA, CB, CC, CD,
) = range(21)
PER_CHUNK = 21
COLS = 9 + 8


def exchange_kernel(
    width,
    tok, og, tw, wg_h, wu_h, wd_h,
    r_out, ab_out, ig_out,
    wgu, wd, ab, pf, pr, zs1, zr1, zs2, zr2, own, xs, xr, res, rt, ig, igs, igr,
    ssem, rsem, lsem, osem,
):
    places = places_of(width)
    n = len(places)
    row, k = lax.axis_index("row"), lax.axis_index("col")
    x, z, c = row // 8, (row // 2) % 4, row % 2
    y, h = k // 2, k % 2
    zp, zm, zo = (z + 1) % 4, (z + 3) % 4, (z + 2) % 4
    yp, ym, yo = (y + 1) % 4, (y + 3) % 4, (y + 2) % 4

    def rdev(xx, zz, cc):
        return (xx * 8 + zz * 2 + cc, k)

    def cdev(yy, hh):
        return (row, yy * 2 + hh)

    sib, xn = rdev(x, z, 1 - c), rdev(1 - x, z, c)
    up, down = rdev(x, zp, c), rdev(x, zm, c)

    def owner(slot):
        return ((y, h), (ym, h), (yp, h), (y, 1 - h), (ym, 1 - h), (yp, 1 - h), (yo, h), (yo, 1 - h))[slot]

    sent = []

    def send(src, dst, idx, dev):
        copy = pltpu.make_async_remote_copy(
            src_ref=src, dst_ref=dst, send_sem=ssem.at[idx], recv_sem=rsem.at[idx],
            device_id=dev, device_id_type=MESH,
        )
        copy.start()
        sent.append(copy)

    def landed(ref, idx):
        pltpu.make_async_remote_copy(
            src_ref=ref, dst_ref=ref, send_sem=ssem.at[idx], recv_sem=rsem.at[idx],
            device_id=sib, device_id_type=MESH,
        ).wait_recv()

    first = [
        pltpu.make_async_copy(tok, ab.at[0, :32], lsem.at[0]),
        pltpu.make_async_copy(og, ab.at[1, :32], lsem.at[1]),
    ]
    weights = [[] for _ in places]
    for j, (kind, _, unit, size, valid) in enumerate(places):
        if kind == "L":
            continue
        for lo in (unit,) if kind == "T" else (unit, unit + size):
            for src, dst, to in (
                (wg_h, wgu, 2 * lo), (wu_h, wgu, 2 * lo + size), (wd_h, wd, lo)
            ):
                weights[j].append(pltpu.make_async_copy(
                    src.at[pl.ds(lo, valid)], dst.at[pl.ds(to, valid)],
                    lsem.at[2 + 6 * j + len(weights[j])],
                ))

    for copy in first:
        copy.start()
    barrier = pltpu.get_barrier_semaphore()
    greeted = [sib, xn, up, down]
    for slot in range(1, 8):
        greeted.append(cdev(*owner(slot)))
    for dev in greeted:
        pl.semaphore_signal(barrier, inc=1, device_id=dev, device_id_type=MESH)
    for copy in weights[0]:
        copy.start()
    for copy in first:
        copy.wait()
    pl.semaphore_wait(barrier, len(greeted))

    base = n * PER_CHUNK

    def both(slot):
        return ab.at[:, slot * 32 : slot * 32 + 32]

    def one(part, slot):
        return ab.at[part, slot * 32 : slot * 32 + 32]

    send(both(0), both(3), base + 2, cdev(y, 1 - h))
    send(both(0), both(1), base + 0, cdev(yp, h))
    send(both(0), both(2), base + 1, cdev(ym, h))
    for copy in sum(weights[1:], []):
        copy.start()
    kind, _, unit, size, valid = places[-1]
    assert kind == "T" and all(place[3] == place[4] for place in places[:-1])
    if valid < size:
        rows = jnp.zeros((size - valid, wd.shape[1]), BF16)
        wgu[2 * unit + valid : 2 * unit + size, :] = rows
        wgu[2 * unit + size + valid : 2 * unit + 2 * size, :] = rows
        wd[unit + valid : unit + size, :] = rows
    ig[...] = jnp.zeros_like(ig)

    def col_near():
        landed(both(1), base + 0)
        send(one(0, 1), one(0, 6), base + 5, cdev(yp, h))
        landed(both(2), base + 1)
        send(one(1, 2), one(1, 6), base + 6, cdev(ym, h))

    def col_cross():
        landed(both(3), base + 2)
        send(both(3), both(4), base + 3, cdev(yp, h))
        send(both(3), both(5), base + 4, cdev(ym, h))

    def col_next():
        landed(both(4), base + 3)
        send(one(0, 4), one(0, 7), base + 7, cdev(yp, h))
        landed(both(5), base + 4)
        send(one(1, 5), one(1, 7), base + 8, cdev(ym, h))

    outs = []

    def col_far():
        landed(one(0, 6), base + 5)
        landed(one(1, 6), base + 6)
        landed(one(0, 7), base + 7)
        landed(one(1, 7), base + 8)
        copy = pltpu.make_async_copy(ab, ab_out, osem.at[0])
        copy.start()
        outs.append(copy)

    def column_of(half):
        lanes = lax.broadcasted_iota(jnp.int32, (16, 256), 1)
        rows = lax.broadcasted_iota(jnp.int32, (16, 256), 0)
        place, among = x * 2 + z // 2, 0
        for i in range(4):
            yy, hh = owner(4 * half + i)
            among = among + jnp.where(place == i, (yy * 2 + hh) * 32, 0)
        at = rows + (among + (z % 2) * 16)
        return jnp.sum(
            jnp.where(lanes == at, jnp.broadcast_to(tw[...], (16, 256)), 0.0), axis=1, keepdims=True
        )

    columns = {"E": column_of(0), "L": column_of(1)}
    columns["T"] = jnp.where(c == 0, columns["E"], columns["L"])

    def span(j):
        _, at, _, size, _ = places[j]
        return slice(at, at + 3 * size)

    def halves(j):
        _, at, _, size, _ = places[j]
        cut = at + (3 * size // LANE // 2) * LANE
        return slice(at, cut), slice(cut, at + 3 * size)

    def multiply(j, side, wide, first, count, to):
        kind, _, unit, size, _ = places[j]
        rows = {"E": slice(0, 128), "L": slice(128, 256), "T": slice(0, 256)}[kind]

        def block(half, lo, at, width):
            value = lax.dot_general(
                ab[side, rows, :], wide[lo : lo + width, :], NT, preferred_element_type=F32
            )
            if kind == "T":
                pf[:, :, :, :, at : at + width] = value.reshape(2, 2, 4, 16, width)
            else:
                pf[half, :, :, :, at : at + width] = value.reshape(2, 4, 16, width)

        for half in range(1 if kind == "T" else 2):
            lo = first + half * count

            for at in range(0, count, 256):
                block(half, lo + at, to + at, min(256, count - at))

    def products(j):
        kind, base_at, unit, size, _ = places[j]
        for copy in weights[j]:
            copy.wait()
        multiply(j, 0, wgu, 2 * unit, 2 * size, base_at)

    def back_products(j):
        _, base_at, unit, size, _ = places[j]
        m, cols = j * PER_CHUNK, span(j)
        multiply(j, 1, wd, unit, size, base_at + 2 * size)
        if JOBS[j][2] == "zx":
            for zz, idx in ((zo, PAIR), (zp, PB), (zm, PC), (z, PD)):
                send(pf.at[1 - c, :, zz, :, cols], pr.at[:, zz, :, cols], m + idx, sib)
        else:
            for xx, idx in ((1 - x, PAIR), (x, PB)):
                send(pf.at[1 - c, xx, :, :, cols], pr.at[xx, :, :, cols], m + idx, sib)

    def chip(xx, zz, cols):
        return pf[c, xx, zz, :, cols] + pr[xx, zz, :, cols]

    def chip_sum(xx, zz, cols):
        return chip(xx, zz, cols) + xr[zz, :, cols].astype(F32)

    def zx_far(j):
        m, cols = j * PER_CHUNK, span(j)
        landed(pr.at[:, zo, :, cols], m + PAIR)
        zs1[0, :, cols] = chip(0, zo, cols).astype(BF16)
        send(zs1.at[0, :, cols], zr1.at[0, :, cols], m + ZA, up)
        zs1[1, :, cols] = chip(1, zo, cols).astype(BF16)
        send(zs1.at[1, :, cols], zr1.at[1, :, cols], m + ZB, down)

    def zx_near(j):
        m, cols = j * PER_CHUNK, span(j)
        landed(pr.at[:, zp, :, cols], m + PB)
        landed(zr1.at[0, :, cols], m + ZA)
        zs2[0, 0, :, cols] = (chip(0, zp, cols) + zr1[0, :, cols].astype(F32)).astype(BF16)
        zs2[0, 1, :, cols] = chip(1, zp, cols).astype(BF16)
        send(zs2.at[0, :, :, cols], zr2.at[0, :, :, cols], m + ZUP, up)
        landed(pr.at[:, zm, :, cols], m + PC)
        landed(zr1.at[1, :, cols], m + ZB)
        zs2[1, 0, :, cols] = chip(0, zm, cols).astype(BF16)
        zs2[1, 1, :, cols] = (chip(1, zm, cols) + zr1[1, :, cols].astype(F32)).astype(BF16)
        send(zs2.at[1, :, :, cols], zr2.at[1, :, :, cols], m + ZDOWN, down)

    def zx_cross(j):
        m, cols = j * PER_CHUNK, span(j)
        landed(pr.at[:, z, :, cols], m + PD)
        landed(zr2.at[0, :, :, cols], m + ZUP)
        landed(zr2.at[1, :, :, cols], m + ZDOWN)

        def ring(xx):
            return chip(xx, z, cols) + zr2[0, xx, :, cols].astype(F32) + zr2[1, xx, :, cols].astype(F32)

        xs[0, :, cols] = ring(1 - x).astype(BF16)
        send(xs.at[0, :, cols], xr.at[0, :, cols], m + X1, xn)
        own[:, cols] = ring(x)

    def zx_total(j):
        m, cols = j * PER_CHUNK, span(j)
        landed(xr.at[0, :, cols], m + X1)
        return lambda at: own[:, at] + xr[0, :, at].astype(F32)

    def xz_cross(j):
        m, cols = j * PER_CHUNK, span(j)
        landed(pr.at[1 - x, :, :, cols], m + PAIR)
        xs[:, :, cols] = (pf[c, 1 - x, :, :, cols] + pr[1 - x, :, :, cols]).astype(BF16)
        send(xs.at[:, :, cols], xr.at[:, :, cols], m + X1, xn)

    def xz_far(j):
        m, cols = j * PER_CHUNK, span(j)
        lo, hi = halves(j)
        landed(pr.at[x, :, :, cols], m + PB)
        landed(xr.at[:, :, cols], m + X1)
        zs1[0, :, lo] = chip_sum(x, zo, lo).astype(BF16)
        send(zs1.at[0, :, lo], zr1.at[0, :, lo], m + ZA, up)
        zs1[1, :, hi] = chip_sum(x, zo, hi).astype(BF16)
        send(zs1.at[1, :, hi], zr1.at[1, :, hi], m + ZB, down)

    def xz_near(j):
        m, cols = j * PER_CHUNK, span(j)
        lo, hi = halves(j)
        landed(zr1.at[0, :, lo], m + ZA)
        zs2[0, 0, :, lo] = (chip_sum(x, zp, lo) + zr1[0, :, lo].astype(F32)).astype(BF16)
        zs2[0, 0, :, hi] = chip_sum(x, zp, hi).astype(BF16)
        send(zs2.at[0, 0, :, cols], zr2.at[0, 0, :, cols], m + ZUP, up)
        landed(zr1.at[1, :, hi], m + ZB)
        zs2[1, 0, :, lo] = chip_sum(x, zm, lo).astype(BF16)
        zs2[1, 0, :, hi] = (chip_sum(x, zm, hi) + zr1[1, :, hi].astype(F32)).astype(BF16)
        send(zs2.at[1, 0, :, cols], zr2.at[1, 0, :, cols], m + ZDOWN, down)

    def xz_total(j):
        m, cols = j * PER_CHUNK, span(j)
        landed(zr2.at[0, 0, :, cols], m + ZUP)
        landed(zr2.at[1, 0, :, cols], m + ZDOWN)
        return lambda at: (
            chip_sum(x, z, at) + zr2[0, 0, :, at].astype(F32) + zr2[1, 0, :, at].astype(F32)
        )

    def here(xx, zz, cols):
        return res.at[c, xx, zz, :, cols]

    def push(xx, zz, cols, idx, dev):
        send(here(xx, zz, cols), here(xx, zz, cols), idx, dev)

    def push_pair(zz, cols, idx, dev):
        part = res.at[c, :, zz, :, cols]
        send(part, part, idx, dev)

    def activate(j):
        kind, base_at, _, size, _ = places[j]
        m, cols = j * PER_CHUNK, span(j)
        total = (xz_total if JOBS[j][2] == "xz" else zx_total)(j)
        column = columns[kind]

        def place(part):
            return slice(base_at + part * size, base_at + part * size + size)

        gate, linear, back = total(place(0)), total(place(1)), total(place(2))
        sig = jax.nn.sigmoid(gate)
        silu = gate * sig
        scaled = column * back
        for part, value in enumerate((
            scaled * linear * sig * (1.0 + gate * (1.0 - sig)),
            scaled * silu,
            column * (silu * linear),
        )):
            res[c, x, z, :, place(part)] = value.astype(BF16)
        push(x, z, cols, m + XA, xn)
        if JOBS[j][3] == "zx":
            push(x, z, cols, m + GUP, up)
            push(x, z, cols, m + GDOWN, down)

    def zx_gather_near(j):
        m, cols = j * PER_CHUNK, span(j)
        lo, hi = halves(j)
        landed(here(x, zm, cols), m + GUP)
        push(x, zm, lo, m + FUP, up)
        push(x, zm, cols, m + XB, xn)
        landed(here(x, zp, cols), m + GDOWN)
        push(x, zp, hi, m + FDOWN, down)
        push(x, zp, cols, m + XC, xn)

    def zx_gather_far(j):
        m, cols = j * PER_CHUNK, span(j)
        lo, hi = halves(j)
        landed(here(x, zo, lo), m + FUP)
        landed(here(x, zo, hi), m + FDOWN)
        push(x, zo, cols, m + XD, xn)
        part = res.at[c, x, :, :, cols]
        send(part, part, m + CA, sib)

    def zx_gather_cross(j):
        m, cols = j * PER_CHUNK, span(j)
        landed(here(1 - x, z, cols), m + XA)
        landed(here(1 - x, zm, cols), m + XB)
        landed(here(1 - x, zp, cols), m + XC)
        landed(here(1 - x, zo, cols), m + XD)
        part = res.at[c, 1 - x, :, :, cols]
        send(part, part, m + CB, sib)

    def zx_all(j):
        m, cols = j * PER_CHUNK, span(j)
        landed(res.at[1 - c, x, :, :, cols], m + CA)
        landed(res.at[1 - c, 1 - x, :, :, cols], m + CB)

    def xz_gather_cross(j):
        m, cols = j * PER_CHUNK, span(j)
        landed(here(1 - x, z, cols), m + XA)
        push_pair(z, cols, m + GUP, up)
        push_pair(z, cols, m + GDOWN, down)
        push_pair(z, cols, m + CA, sib)

    def xz_gather_near(j):
        m, cols = j * PER_CHUNK, span(j)
        landed(res.at[c, :, zm, :, cols], m + GUP)
        push(0, zm, cols, m + FUP, up)
        landed(res.at[c, :, zp, :, cols], m + GDOWN)
        push(1, zp, cols, m + FDOWN, down)
        push_pair(zm, cols, m + CB, sib)
        push_pair(zp, cols, m + CC, sib)

    def xz_gather_far(j):
        m, cols = j * PER_CHUNK, span(j)
        landed(here(0, zo, cols), m + FUP)
        landed(here(1, zo, cols), m + FDOWN)
        push_pair(zo, cols, m + CD, sib)

    def xz_all(j):
        m, cols = j * PER_CHUNK, span(j)
        for zz, idx in ((z, CA), (zm, CB), (zp, CC), (zo, CD)):
            landed(res.at[1 - c, :, zz, :, cols], m + idx)

    def finish(j):
        kind, base_at, unit, size, _ = places[j]
        (zx_all if JOBS[j][3] == "zx" else xz_all)(j)
        at = slice(base_at, base_at + 2 * size)
        if kind == "T":
            piece = res[:, :, :, :, at].reshape(256, 2 * size)
            ig[...] += jnp.dot(
                piece, wgu[2 * unit : 2 * unit + 2 * size, :], preferred_element_type=F32
            )
        else:
            start = 128 * (kind == "L")
            lo = 2 * unit
            value = jnp.dot(
                res[0, :, :, :, at].reshape(128, 2 * size), wgu[lo : lo + 2 * size, :],
                preferred_element_type=F32,
            )
            lo += 2 * size
            value += jnp.dot(
                res[1, :, :, :, at].reshape(128, 2 * size), wgu[lo : lo + 2 * size, :],
                preferred_element_type=F32,
            )
            ig[start : start + 128, :] += value

    def transposes(j):
        kind, base_at, unit, size, _ = places[j]
        for part in range(3):
            cols = slice(base_at + part * size, base_at + part * size + size)
            if kind == "T":
                rt[part, unit : unit + size, :] = res[:, :, :, :, cols].reshape(256, size).T
            else:
                start = 128 * (kind == "L")
                for lo, half in ((unit, 0), (unit + size, 1)):
                    rt[part, lo : lo + size, start : start + 128] = (
                        res[half, :, :, :, cols].reshape(128, size).T
                    )
        if kind == "T":
            tokens, units = pl.ds(0, 256), pl.ds(unit, size)
        else:
            tokens, units = pl.ds(128 * (kind == "L"), 128), pl.ds(unit, 2 * size)
        copy = pltpu.make_async_copy(
            rt.at[:, units, tokens], r_out.at[:, units, tokens], osem.at[1 + j]
        )
        copy.start()
        outs.append(copy)

    def col_send():
        igs[...] = ig[...].astype(BF16)
        for slot in (3, 7, 4, 5, 6, 1, 2):
            send(
                igs.at[slot * 32 : slot * 32 + 32], igr.at[slot], base + 9 + slot,
                cdev(*owner(slot)),
            )

    reduce = {"zx": (zx_far, zx_near, zx_cross), "xz": (xz_cross, xz_far, xz_near)}
    gather = {
        "zx": (zx_gather_near, zx_gather_far, zx_gather_cross),
        "xz": (xz_gather_cross, xz_gather_near, xz_gather_far),
    }
    col = (col_near, col_cross, col_next, col_far, col_send)
    for stage, j in ORDER:
        if j < 0:
            col[stage]()
        else:
            _, _, over, back = JOBS[j]
            (
                products, back_products, *reduce[over], activate, *gather[back], finish, transposes,
            )[stage](j)

    for copy in sent[:-7]:
        copy.wait_send()
    for copy in outs:
        copy.wait()
    total = ig[:32, :]
    for slot in range(1, 8):
        landed(igr.at[slot], base + 9 + slot)
        total = total + igr[slot].astype(F32)
    ig_out[...] = total

    for copy in sent[-7:]:
        copy.wait_send()


def exchange(tokens, out_grad, token_weight, gate_weight, up_weight, down_weight):
    width, depth = gate_weight.shape
    wide = pl.cdiv(width, LANE) * LANE
    cols = 3 * wide
    n = len(JOBS)
    messages = n * PER_CHUNK + COLS
    hbm = pl.BlockSpec(memory_space=pl.ANY)
    vmem = pl.BlockSpec(memory_space=pltpu.VMEM)
    return pl.pallas_call(
        functools.partial(exchange_kernel, width),
        out_shape=(
            pltpu.VMEM((3, wide, 256), BF16),
            pltpu.VMEM((2, 256, depth), BF16),
            pltpu.VMEM((32, depth), F32),
        ),
        in_specs=[hbm, hbm, vmem, hbm, hbm, hbm],
        out_specs=(hbm, hbm, vmem),
        scratch_shapes=[
            pltpu.VMEM((2 * wide, depth), BF16),
            pltpu.VMEM((wide, depth), BF16),
            pltpu.VMEM((2, 256, depth), BF16),
            pltpu.VMEM((2, 2, 4, 16, cols), F32),
            pltpu.VMEM((2, 4, 16, cols), F32),
            pltpu.VMEM((2, 16, cols), BF16),
            pltpu.VMEM((2, 16, cols), BF16),
            pltpu.VMEM((2, 2, 16, cols), BF16),
            pltpu.VMEM((2, 2, 16, cols), BF16),
            pltpu.VMEM((16, cols), F32),
            pltpu.VMEM((4, 16, cols), BF16),
            pltpu.VMEM((4, 16, cols), BF16),
            pltpu.VMEM((2, 2, 4, 16, cols), BF16),
            pltpu.VMEM((3, wide, 256), BF16),
            pltpu.VMEM((256, depth), F32),
            pltpu.VMEM((256, depth), BF16),
            pltpu.VMEM((8, 32, depth), BF16),
            pltpu.SemaphoreType.DMA((messages,)),
            pltpu.SemaphoreType.DMA((messages,)),
            pltpu.SemaphoreType.DMA((2 + 6 * n,)),
            pltpu.SemaphoreType.DMA((1 + n,)),
        ],
        compiler_params=pltpu.CompilerParams(
            collective_id=0, has_side_effects=True, vmem_limit_bytes=50 * 1024 * 1024
        ),
        cost_estimate=pl.CostEstimate(
            flops=10 * 256 * depth * width, bytes_accessed=6 * depth * width + 6 * 256 * width,
            transcendentals=0,
        ),
        name="exchange",
    )(tokens, out_grad, token_weight.reshape(1, 256), gate_weight, up_weight, down_weight)


GRAD_ROWS = 336


def grads_kernel(r, ab, ig, gate_grad, up_grad, down_grad, ig_out, out, osem):
    step = GRAD_ROWS
    n = gate_grad.shape[0] // step

    def store(i, part):
        rows = pl.ds(pl.multiple_of(i * step, 16), step)
        to = (gate_grad, up_grad, down_grad)[part]
        return pltpu.make_async_copy(out.at[part, rows], to.at[rows], osem.at[3 * i + part])

    whole = pltpu.make_async_copy(ig, ig_out, osem.at[3 * n])
    whole.start()

    @pl.loop(0, n)
    def _(i):
        rows = pl.ds(pl.multiple_of(i * step, 16), step)
        for part in range(3):
            out[part, rows, :] = jnp.dot(
                r[part, rows, :], ab[part // 2], preferred_element_type=F32
            ).astype(BF16)
            store(i, part).start()

    for i in range(n):
        for part in range(3):
            store(i, part).wait()
    whole.wait()


def grads(r, ab, ig, width):
    depth = ab.shape[2]
    assert width % GRAD_ROWS == 0
    n = width // GRAD_ROWS
    hbm = pl.BlockSpec(memory_space=pl.ANY)
    vmem = pl.BlockSpec(memory_space=pltpu.VMEM)
    return pl.pallas_call(
        grads_kernel,
        in_specs=[vmem, vmem, vmem],
        out_specs=(hbm,) * 4,
        out_shape=(pltpu.HBM((width, depth), BF16),) * 3 + (pltpu.HBM(ig.shape, F32),),
        scratch_shapes=[
            pltpu.VMEM((3, width, depth), BF16),
            pltpu.SemaphoreType.DMA((3 * n + 1,)),
        ],
        compiler_params=pltpu.CompilerParams(vmem_limit_bytes=24 * 1024 * 1024),
        name="grads",
    )(r, ab, ig)


def body(tokens, out_grad, token_weight, gate_weight, up_weight, down_weight):
    width = gate_weight.shape[1]
    r, ab, input_grad = exchange(
        tokens, out_grad, token_weight, gate_weight.T, up_weight.T, down_weight
    )
    gate_grad, up_grad, down_grad, input_grad = grads(r, ab, input_grad, width)
    return input_grad, gate_grad.T, up_grad.T, down_grad


def solution(mesh):
    return jax.shard_map(
        body,
        mesh=mesh,
        in_specs=(
            P("col", "row"),
            P("col", "row"),
            P(),
            P("row", "col"),
            P("row", "col"),
            P("col", "row"),
        ),
        out_specs=(P("col", "row"), P("row", "col"), P("row", "col"), P("col", "row")),
        check_vma=False,
    )
```

```python
import functools

import jax
import jax.numpy as jnp
from jax import lax
from jax.experimental import pallas as pl
from jax.experimental.pallas import tpu as pltpu
from jax.sharding import PartitionSpec as P

BF16, F32 = jnp.bfloat16, jnp.float32
MESH = pl.DeviceIdType.MESH
LANE = 128
JOBS = (
    ("E", 5, "zx", "xz"),
    ("L", 5, "zx", "xz"),
    ("T", 5, "zx", "zx"),
    ("T", 2, "xz", "xz"),
    ("T", 5, "zx", "zx"),
    ("T", 4, "xz", "xz"),
    ("T", 2, "xz", "xz"),
    ("T", 1, "xz", "xz"),
)
ORDER = (
    (0, -1), (1, -1), (0, 0), (1, 0), (2, -1), (2, 0), (3, -1), (0, 1), (1, 1), (3, 0), (0, 2),
    (2, 1), (1, 2), (0, 3), (1, 3), (0, 4), (1, 4), (2, 2), (4, 0), (0, 5), (3, 1), (2, 3), (1, 5),
    (3, 2), (5, 0), (2, 4), (2, 5), (4, 1), (3, 3), (0, 6), (6, 0), (1, 6), (0, 7), (1, 7), (4, 2),
    (3, 4), (4, 3), (2, 6), (3, 5), (2, 7), (7, 0), (5, 1), (5, 2), (4, 4), (5, 3), (4, 5), (3, 6),
    (3, 7), (8, 0), (6, 1), (6, 2), (9, 0), (5, 5), (4, 6), (4, 7), (5, 4), (6, 3), (7, 1), (7, 2),
    (10, 0), (5, 6), (5, 7), (6, 5), (6, 4), (7, 3), (8, 1), (8, 2), (6, 6), (6, 7), (9, 1), (7, 5),
    (7, 4), (9, 2), (8, 3), (10, 1), (10, 2), (7, 6), (7, 7), (9, 3), (8, 4), (10, 3), (8, 5),
    (8, 6), (8, 7), (9, 4), (9, 5), (9, 6), (9, 7), (4, -1), (10, 4), (10, 5), (10, 6), (10, 7),
)
NT = (((1,), (1,)), ((), ()))


def places_of(width):
    out, at, pairs, taken = [], 0, 0, 0
    for kind, tiles, _, _ in JOBS:
        size = tiles * LANE
        if kind == "E":
            unit, pairs = pairs, pairs + 2 * size
        elif kind == "L":
            unit, taken = taken, taken + 2 * size
        else:
            assert taken == pairs or taken == 0
            unit = max(pairs, units_end(out))
        out.append((kind, at, unit, size, min(size, width - unit)))
        at += 3 * size
    assert taken == pairs and at == 3 * LANE * pl.cdiv(width, LANE)
    return out


def units_end(places):
    return max((unit + size for kind, _, unit, size, _ in places if kind == "T"), default=0)


(
    PAIR, PB, PC, PD, ZA, ZB, ZUP, ZDOWN, X1,
    GUP, GDOWN, FUP, FDOWN, XA, XB, XC, XD, CA, CB, CC, CD,
) = range(21)
PER_CHUNK = 21
COLS = 9 + 8


def exchange_kernel(
    width,
    tok, og, tw, wg_h, wu_h, wd_h,
    r_out, ab_out, ig_out,
    wgu, wd, ab, pf, pr, zs1, zr1, zs2, zr2, own, xs, xr, res, rt, ig, igs, igr,
    ssem, rsem, lsem, osem,
):
    places = places_of(width)
    n = len(places)
    row, k = lax.axis_index("row"), lax.axis_index("col")
    x, z, c = row // 8, (row // 2) % 4, row % 2
    y, h = k // 2, k % 2
    zp, zm, zo = (z + 1) % 4, (z + 3) % 4, (z + 2) % 4
    yp, ym, yo = (y + 1) % 4, (y + 3) % 4, (y + 2) % 4

    def rdev(xx, zz, cc):
        return (xx * 8 + zz * 2 + cc, k)

    def cdev(yy, hh):
        return (row, yy * 2 + hh)

    sib, xn = rdev(x, z, 1 - c), rdev(1 - x, z, c)
    up, down = rdev(x, zp, c), rdev(x, zm, c)

    def owner(slot):
        return ((y, h), (ym, h), (yp, h), (y, 1 - h), (ym, 1 - h), (yp, 1 - h), (yo, h), (yo, 1 - h))[slot]

    sent = []

    def send(src, dst, idx, dev):
        copy = pltpu.make_async_remote_copy(
            src_ref=src, dst_ref=dst, send_sem=ssem.at[idx], recv_sem=rsem.at[idx],
            device_id=dev, device_id_type=MESH,
        )
        copy.start()
        sent.append(copy)

    def landed(ref, idx):
        pltpu.make_async_remote_copy(
            src_ref=ref, dst_ref=ref, send_sem=ssem.at[idx], recv_sem=rsem.at[idx],
            device_id=sib, device_id_type=MESH,
        ).wait_recv()

    first = [
        pltpu.make_async_copy(tok, ab.at[0, :32], lsem.at[0]),
        pltpu.make_async_copy(og, ab.at[1, :32], lsem.at[1]),
    ]
    weights = [[] for _ in places]
    for j, (kind, _, unit, size, valid) in enumerate(places):
        if kind == "L":
            continue
        for lo in (unit,) if kind == "T" else (unit, unit + size):
            for src, dst, to in (
                (wg_h, wgu, 2 * lo), (wu_h, wgu, 2 * lo + size), (wd_h, wd, lo)
            ):
                weights[j].append(pltpu.make_async_copy(
                    src.at[pl.ds(lo, valid)], dst.at[pl.ds(to, valid)],
                    lsem.at[2 + 6 * j + len(weights[j])],
                ))

    for copy in first:
        copy.start()
    barrier = pltpu.get_barrier_semaphore()
    greeted = [sib, xn, up, down]
    for slot in range(1, 8):
        greeted.append(cdev(*owner(slot)))
    for dev in greeted:
        pl.semaphore_signal(barrier, inc=1, device_id=dev, device_id_type=MESH)
    for copy in weights[0]:
        copy.start()
    for copy in first:
        copy.wait()
    pl.semaphore_wait(barrier, len(greeted))

    base = n * PER_CHUNK

    def both(slot):
        return ab.at[:, slot * 32 : slot * 32 + 32]

    def one(part, slot):
        return ab.at[part, slot * 32 : slot * 32 + 32]

    send(both(0), both(3), base + 2, cdev(y, 1 - h))
    send(both(0), both(1), base + 0, cdev(yp, h))
    send(both(0), both(2), base + 1, cdev(ym, h))
    for copy in sum(weights[1:], []):
        copy.start()
    kind, _, unit, size, valid = places[-1]
    assert kind == "T" and all(place[3] == place[4] for place in places[:-1])
    if valid < size:
        rows = jnp.zeros((size - valid, wd.shape[1]), BF16)
        wgu[2 * unit + valid : 2 * unit + size, :] = rows
        wgu[2 * unit + size + valid : 2 * unit + 2 * size, :] = rows
        wd[unit + valid : unit + size, :] = rows
    ig[...] = jnp.zeros_like(ig)

    def col_near():
        landed(both(1), base + 0)
        send(one(0, 1), one(0, 6), base + 5, cdev(yp, h))
        landed(both(2), base + 1)
        send(one(1, 2), one(1, 6), base + 6, cdev(ym, h))

    def col_cross():
        landed(both(3), base + 2)
        send(both(3), both(4), base + 3, cdev(yp, h))
        send(both(3), both(5), base + 4, cdev(ym, h))

    def col_next():
        landed(both(4), base + 3)
        send(one(0, 4), one(0, 7), base + 7, cdev(yp, h))
        landed(both(5), base + 4)
        send(one(1, 5), one(1, 7), base + 8, cdev(ym, h))

    outs = []

    def col_far():
        landed(one(0, 6), base + 5)
        landed(one(1, 6), base + 6)
        landed(one(0, 7), base + 7)
        landed(one(1, 7), base + 8)
        copy = pltpu.make_async_copy(ab, ab_out, osem.at[0])
        copy.start()
        outs.append(copy)

    def column_of(half):
        lanes = lax.broadcasted_iota(jnp.int32, (16, 256), 1)
        rows = lax.broadcasted_iota(jnp.int32, (16, 256), 0)
        place, among = x * 2 + z // 2, 0
        for i in range(4):
            yy, hh = owner(4 * half + i)
            among = among + jnp.where(place == i, (yy * 2 + hh) * 32, 0)
        at = rows + (among + (z % 2) * 16)
        return jnp.sum(
            jnp.where(lanes == at, jnp.broadcast_to(tw[...], (16, 256)), 0.0), axis=1, keepdims=True
        )

    columns = {"E": column_of(0), "L": column_of(1)}
    columns["T"] = jnp.where(c == 0, columns["E"], columns["L"])

    def span(j):
        _, at, _, size, _ = places[j]
        return slice(at, at + 3 * size)

    def halves(j):
        _, at, _, size, _ = places[j]
        cut = at + (3 * size // LANE // 2) * LANE
        return slice(at, cut), slice(cut, at + 3 * size)

    def multiply(j, side, wide, first, count, to):
        kind, _, unit, size, _ = places[j]
        rows = {"E": slice(0, 128), "L": slice(128, 256), "T": slice(0, 256)}[kind]

        def block(half, lo, at, width):
            value = lax.dot_general(
                ab[side, rows, :], wide[lo : lo + width, :], NT, preferred_element_type=F32
            )
            if kind == "T":
                pf[:, :, :, :, at : at + width] = value.reshape(2, 2, 4, 16, width)
            else:
                pf[half, :, :, :, at : at + width] = value.reshape(2, 4, 16, width)

        for half in range(1 if kind == "T" else 2):
            lo = first + half * count

            for at in range(0, count, 256):
                block(half, lo + at, to + at, min(256, count - at))

    def products(j):
        kind, base_at, unit, size, _ = places[j]
        for copy in weights[j]:
            copy.wait()
        multiply(j, 0, wgu, 2 * unit, 2 * size, base_at)

    def back_products(j):
        _, base_at, unit, size, _ = places[j]
        m, cols = j * PER_CHUNK, span(j)
        multiply(j, 1, wd, unit, size, base_at + 2 * size)
        if JOBS[j][2] == "zx":
            for zz, idx in ((zo, PAIR), (zp, PB), (zm, PC), (z, PD)):
                send(pf.at[1 - c, :, zz, :, cols], pr.at[:, zz, :, cols], m + idx, sib)
        else:
            for xx, idx in ((1 - x, PAIR), (x, PB)):
                send(pf.at[1 - c, xx, :, :, cols], pr.at[xx, :, :, cols], m + idx, sib)

    def chip(xx, zz, cols):
        return pf[c, xx, zz, :, cols] + pr[xx, zz, :, cols]

    def chip_sum(xx, zz, cols):
        return chip(xx, zz, cols) + xr[zz, :, cols].astype(F32)

    def zx_far(j):
        m, cols = j * PER_CHUNK, span(j)
        landed(pr.at[:, zo, :, cols], m + PAIR)
        zs1[0, :, cols] = chip(0, zo, cols).astype(BF16)
        send(zs1.at[0, :, cols], zr1.at[0, :, cols], m + ZA, up)
        zs1[1, :, cols] = chip(1, zo, cols).astype(BF16)
        send(zs1.at[1, :, cols], zr1.at[1, :, cols], m + ZB, down)

    def zx_near(j):
        m, cols = j * PER_CHUNK, span(j)
        landed(pr.at[:, zp, :, cols], m + PB)
        landed(zr1.at[0, :, cols], m + ZA)
        zs2[0, 0, :, cols] = (chip(0, zp, cols) + zr1[0, :, cols].astype(F32)).astype(BF16)
        zs2[0, 1, :, cols] = chip(1, zp, cols).astype(BF16)
        send(zs2.at[0, :, :, cols], zr2.at[0, :, :, cols], m + ZUP, up)
        landed(pr.at[:, zm, :, cols], m + PC)
        landed(zr1.at[1, :, cols], m + ZB)
        zs2[1, 0, :, cols] = chip(0, zm, cols).astype(BF16)
        zs2[1, 1, :, cols] = (chip(1, zm, cols) + zr1[1, :, cols].astype(F32)).astype(BF16)
        send(zs2.at[1, :, :, cols], zr2.at[1, :, :, cols], m + ZDOWN, down)

    def zx_cross(j):
        m, cols = j * PER_CHUNK, span(j)
        landed(pr.at[:, z, :, cols], m + PD)
        landed(zr2.at[0, :, :, cols], m + ZUP)
        landed(zr2.at[1, :, :, cols], m + ZDOWN)

        def ring(xx):
            return chip(xx, z, cols) + zr2[0, xx, :, cols].astype(F32) + zr2[1, xx, :, cols].astype(F32)

        xs[0, :, cols] = ring(1 - x).astype(BF16)
        send(xs.at[0, :, cols], xr.at[0, :, cols], m + X1, xn)
        own[:, cols] = ring(x)

    def zx_total(j):
        m, cols = j * PER_CHUNK, span(j)
        landed(xr.at[0, :, cols], m + X1)
        return lambda at: own[:, at] + xr[0, :, at].astype(F32)

    def xz_cross(j):
        m, cols = j * PER_CHUNK, span(j)
        landed(pr.at[1 - x, :, :, cols], m + PAIR)
        xs[:, :, cols] = (pf[c, 1 - x, :, :, cols] + pr[1 - x, :, :, cols]).astype(BF16)
        send(xs.at[:, :, cols], xr.at[:, :, cols], m + X1, xn)

    def xz_far(j):
        m, cols = j * PER_CHUNK, span(j)
        lo, hi = halves(j)
        landed(pr.at[x, :, :, cols], m + PB)
        landed(xr.at[:, :, cols], m + X1)
        zs1[0, :, lo] = chip_sum(x, zo, lo).astype(BF16)
        send(zs1.at[0, :, lo], zr1.at[0, :, lo], m + ZA, up)
        zs1[1, :, hi] = chip_sum(x, zo, hi).astype(BF16)
        send(zs1.at[1, :, hi], zr1.at[1, :, hi], m + ZB, down)

    def xz_near(j):
        m, cols = j * PER_CHUNK, span(j)
        lo, hi = halves(j)
        landed(zr1.at[0, :, lo], m + ZA)
        zs2[0, 0, :, lo] = (chip_sum(x, zp, lo) + zr1[0, :, lo].astype(F32)).astype(BF16)
        zs2[0, 0, :, hi] = chip_sum(x, zp, hi).astype(BF16)
        send(zs2.at[0, 0, :, cols], zr2.at[0, 0, :, cols], m + ZUP, up)
        landed(zr1.at[1, :, hi], m + ZB)
        zs2[1, 0, :, lo] = chip_sum(x, zm, lo).astype(BF16)
        zs2[1, 0, :, hi] = (chip_sum(x, zm, hi) + zr1[1, :, hi].astype(F32)).astype(BF16)
        send(zs2.at[1, 0, :, cols], zr2.at[1, 0, :, cols], m + ZDOWN, down)

    def xz_total(j):
        m, cols = j * PER_CHUNK, span(j)
        landed(zr2.at[0, 0, :, cols], m + ZUP)
        landed(zr2.at[1, 0, :, cols], m + ZDOWN)
        return lambda at: (
            chip_sum(x, z, at) + zr2[0, 0, :, at].astype(F32) + zr2[1, 0, :, at].astype(F32)
        )

    def here(xx, zz, cols):
        return res.at[c, xx, zz, :, cols]

    def push(xx, zz, cols, idx, dev):
        send(here(xx, zz, cols), here(xx, zz, cols), idx, dev)

    def push_pair(zz, cols, idx, dev):
        part = res.at[c, :, zz, :, cols]
        send(part, part, idx, dev)

    def activate(j):
        kind, base_at, _, size, _ = places[j]
        m, cols = j * PER_CHUNK, span(j)
        total = (xz_total if JOBS[j][2] == "xz" else zx_total)(j)
        column = columns[kind]

        def place(part):
            return slice(base_at + part * size, base_at + part * size + size)

        gate, linear, back = total(place(0)), total(place(1)), total(place(2))
        sig = jax.nn.sigmoid(gate)
        silu = gate * sig
        scaled = column * back
        for part, value in enumerate((
            scaled * linear * sig * (1.0 + gate * (1.0 - sig)),
            scaled * silu,
            column * (silu * linear),
        )):
            res[c, x, z, :, place(part)] = value.astype(BF16)
        push(x, z, cols, m + XA, xn)
        if JOBS[j][3] == "zx":
            push(x, z, cols, m + GUP, up)
            push(x, z, cols, m + GDOWN, down)

    def zx_gather_near(j):
        m, cols = j * PER_CHUNK, span(j)
        lo, hi = halves(j)
        landed(here(x, zm, cols), m + GUP)
        push(x, zm, lo, m + FUP, up)
        push(x, zm, cols, m + XB, xn)
        landed(here(x, zp, cols), m + GDOWN)
        push(x, zp, hi, m + FDOWN, down)
        push(x, zp, cols, m + XC, xn)

    def zx_gather_far(j):
        m, cols = j * PER_CHUNK, span(j)
        lo, hi = halves(j)
        landed(here(x, zo, lo), m + FUP)
        landed(here(x, zo, hi), m + FDOWN)
        push(x, zo, cols, m + XD, xn)
        part = res.at[c, x, :, :, cols]
        send(part, part, m + CA, sib)

    def zx_gather_cross(j):
        m, cols = j * PER_CHUNK, span(j)
        landed(here(1 - x, z, cols), m + XA)
        landed(here(1 - x, zm, cols), m + XB)
        landed(here(1 - x, zp, cols), m + XC)
        landed(here(1 - x, zo, cols), m + XD)
        part = res.at[c, 1 - x, :, :, cols]
        send(part, part, m + CB, sib)

    def zx_all(j):
        m, cols = j * PER_CHUNK, span(j)
        landed(res.at[1 - c, x, :, :, cols], m + CA)
        landed(res.at[1 - c, 1 - x, :, :, cols], m + CB)

    def xz_gather_cross(j):
        m, cols = j * PER_CHUNK, span(j)
        landed(here(1 - x, z, cols), m + XA)
        push_pair(z, cols, m + GUP, up)
        push_pair(z, cols, m + GDOWN, down)
        push_pair(z, cols, m + CA, sib)

    def xz_gather_near(j):
        m, cols = j * PER_CHUNK, span(j)
        landed(res.at[c, :, zm, :, cols], m + GUP)
        push(0, zm, cols, m + FUP, up)
        landed(res.at[c, :, zp, :, cols], m + GDOWN)
        push(1, zp, cols, m + FDOWN, down)
        push_pair(zm, cols, m + CB, sib)
        push_pair(zp, cols, m + CC, sib)

    def xz_gather_far(j):
        m, cols = j * PER_CHUNK, span(j)
        landed(here(0, zo, cols), m + FUP)
        landed(here(1, zo, cols), m + FDOWN)
        push_pair(zo, cols, m + CD, sib)

    def xz_all(j):
        m, cols = j * PER_CHUNK, span(j)
        for zz, idx in ((z, CA), (zm, CB), (zp, CC), (zo, CD)):
            landed(res.at[1 - c, :, zz, :, cols], m + idx)

    def finish(j):
        kind, base_at, unit, size, _ = places[j]
        (zx_all if JOBS[j][3] == "zx" else xz_all)(j)
        at = slice(base_at, base_at + 2 * size)
        if kind == "T":
            piece = res[:, :, :, :, at].reshape(256, 2 * size)
            ig[...] += jnp.dot(
                piece, wgu[2 * unit : 2 * unit + 2 * size, :], preferred_element_type=F32
            )
        else:
            start = 128 * (kind == "L")
            lo = 2 * unit
            value = jnp.dot(
                res[0, :, :, :, at].reshape(128, 2 * size), wgu[lo : lo + 2 * size, :],
                preferred_element_type=F32,
            )
            lo += 2 * size
            value += jnp.dot(
                res[1, :, :, :, at].reshape(128, 2 * size), wgu[lo : lo + 2 * size, :],
                preferred_element_type=F32,
            )
            ig[start : start + 128, :] += value

    def transposes(j):
        kind, base_at, unit, size, _ = places[j]
        for part in range(3):
            cols = slice(base_at + part * size, base_at + part * size + size)
            if kind == "T":
                rt[part, unit : unit + size, :] = res[:, :, :, :, cols].reshape(256, size).T
            else:
                start = 128 * (kind == "L")
                for lo, half in ((unit, 0), (unit + size, 1)):
                    rt[part, lo : lo + size, start : start + 128] = (
                        res[half, :, :, :, cols].reshape(128, size).T
                    )
        if kind == "T":
            tokens, units = pl.ds(0, 256), pl.ds(unit, size)
        else:
            tokens, units = pl.ds(128 * (kind == "L"), 128), pl.ds(unit, 2 * size)
        copy = pltpu.make_async_copy(
            rt.at[:, units, tokens], r_out.at[:, units, tokens], osem.at[1 + j]
        )
        copy.start()
        outs.append(copy)

    def col_send():
        igs[...] = ig[...].astype(BF16)
        for slot in (3, 7, 4, 5, 6, 1, 2):
            send(
                igs.at[slot * 32 : slot * 32 + 32], igr.at[slot], base + 9 + slot,
                cdev(*owner(slot)),
            )

    reduce = {"zx": (zx_far, zx_near, zx_cross), "xz": (xz_cross, xz_far, xz_near)}
    gather = {
        "zx": (zx_gather_near, zx_gather_far, zx_gather_cross),
        "xz": (xz_gather_cross, xz_gather_near, xz_gather_far),
    }
    col = (col_near, col_cross, col_next, col_far, col_send)
    for stage, j in ORDER:
        if j < 0:
            col[stage]()
        else:
            _, _, over, back = JOBS[j]
            (
                products, back_products, *reduce[over], activate, *gather[back], finish, transposes,
            )[stage](j)

    for copy in sent[:-7]:
        copy.wait_send()
    for copy in outs:
        copy.wait()
    total = ig[:32, :]
    for slot in range(1, 8):
        landed(igr.at[slot], base + 9 + slot)
        total = total + igr[slot].astype(F32)
    ig_out[...] = total

    for copy in sent[-7:]:
        copy.wait_send()


def exchange(tokens, out_grad, token_weight, gate_weight, up_weight, down_weight):
    width, depth = gate_weight.shape
    wide = pl.cdiv(width, LANE) * LANE
    cols = 3 * wide
    n = len(JOBS)
    messages = n * PER_CHUNK + COLS
    hbm = pl.BlockSpec(memory_space=pl.ANY)
    vmem = pl.BlockSpec(memory_space=pltpu.VMEM)
    return pl.pallas_call(
        functools.partial(exchange_kernel, width),
        out_shape=(
            pltpu.VMEM((3, wide, 256), BF16),
            pltpu.VMEM((2, 256, depth), BF16),
            pltpu.VMEM((32, depth), F32),
        ),
        in_specs=[hbm, hbm, vmem, hbm, hbm, hbm],
        out_specs=(hbm, hbm, vmem),
        scratch_shapes=[
            pltpu.VMEM((2 * wide, depth), BF16),
            pltpu.VMEM((wide, depth), BF16),
            pltpu.VMEM((2, 256, depth), BF16),
            pltpu.VMEM((2, 2, 4, 16, cols), F32),
            pltpu.VMEM((2, 4, 16, cols), F32),
            pltpu.VMEM((2, 16, cols), BF16),
            pltpu.VMEM((2, 16, cols), BF16),
            pltpu.VMEM((2, 2, 16, cols), BF16),
            pltpu.VMEM((2, 2, 16, cols), BF16),
            pltpu.VMEM((16, cols), F32),
            pltpu.VMEM((4, 16, cols), BF16),
            pltpu.VMEM((4, 16, cols), BF16),
            pltpu.VMEM((2, 2, 4, 16, cols), BF16),
            pltpu.VMEM((3, wide, 256), BF16),
            pltpu.VMEM((256, depth), F32),
            pltpu.VMEM((256, depth), BF16),
            pltpu.VMEM((8, 32, depth), BF16),
            pltpu.SemaphoreType.DMA((messages,)),
            pltpu.SemaphoreType.DMA((messages,)),
            pltpu.SemaphoreType.DMA((2 + 6 * n,)),
            pltpu.SemaphoreType.DMA((1 + n,)),
        ],
        compiler_params=pltpu.CompilerParams(
            collective_id=0, has_side_effects=True, vmem_limit_bytes=50 * 1024 * 1024
        ),
        cost_estimate=pl.CostEstimate(
            flops=10 * 256 * depth * width, bytes_accessed=6 * depth * width + 6 * 256 * width,
            transcendentals=0,
        ),
        name="exchange",
    )(tokens, out_grad, token_weight.reshape(1, 256), gate_weight, up_weight, down_weight)


GRAD_ROWS = 336


def grads_kernel(r, ab, ig, gate_grad, up_grad, down_grad, ig_out, out, osem):
    step = GRAD_ROWS
    n = gate_grad.shape[0] // step

    def store(i, part):
        rows = pl.ds(pl.multiple_of(i * step, 16), step)
        to = (gate_grad, up_grad, down_grad)[part]
        return pltpu.make_async_copy(out.at[part, rows], to.at[rows], osem.at[3 * i + part])

    whole = pltpu.make_async_copy(ig, ig_out, osem.at[3 * n])
    whole.start()

    @pl.loop(0, n)
    def _(i):
        rows = pl.ds(pl.multiple_of(i * step, 16), step)
        for part in range(3):
            out[part, rows, :] = jnp.dot(
                r[part, rows, :], ab[part // 2], preferred_element_type=F32
            ).astype(BF16)
            store(i, part).start()

    for i in range(n):
        for part in range(3):
            store(i, part).wait()
    whole.wait()


def grads(r, ab, ig, width):
    depth = ab.shape[2]
    assert width % GRAD_ROWS == 0
    n = width // GRAD_ROWS
    hbm = pl.BlockSpec(memory_space=pl.ANY)
    vmem = pl.BlockSpec(memory_space=pltpu.VMEM)
    return pl.pallas_call(
        grads_kernel,
        in_specs=[vmem, vmem, vmem],
        out_specs=(hbm,) * 4,
        out_shape=(pltpu.HBM((width, depth), BF16),) * 3 + (pltpu.HBM(ig.shape, F32),),
        scratch_shapes=[
            pltpu.VMEM((3, width, depth), BF16),
            pltpu.SemaphoreType.DMA((3 * n + 1,)),
        ],
        compiler_params=pltpu.CompilerParams(vmem_limit_bytes=24 * 1024 * 1024),
        name="grads",
    )(r, ab, ig)


def body(tokens, out_grad, token_weight, gate_weight, up_weight, down_weight):
    width = gate_weight.shape[1]
    r, ab, input_grad = exchange(
        tokens, out_grad, token_weight, gate_weight.T, up_weight.T, down_weight
    )
    gate_grad, up_grad, down_grad, input_grad = grads(r, ab, input_grad, width)
    return input_grad, gate_grad.T, up_grad.T, down_grad


def solution(mesh):
    return jax.shard_map(
        body,
        mesh=mesh,
        in_specs=(
            P("col", "row"),
            P("col", "row"),
            P(),
            P("row", "col"),
            P("row", "col"),
            P("col", "row"),
        ),
        out_specs=(P("col", "row"), P("row", "col"), P("row", "col"), P("col", "row")),
        check_vma=False,
    )
```
